32 devices in a mesh: dp: 2 (over x), seq: 16 (over z, y, core).
Axes of the slice: x: 2, y: 2, z: 4, core: 2. Of those that a mesh axis runs over, the one named last changes fastest.
Arguments:
- signal: bfloat16 [2, 32768, 256], P('dp', 'seq'), may hold values from -6 to 6
- gating: bfloat16 [2, 32768, 256], P('dp', 'seq'), may hold values from -6 to 6
- upstream: bfloat16 [2, 32768, 256], P('dp', 'seq'), may hold values from -1.5 to 1.5
- left_factor: bfloat16 [64, 512, 512], P('seq'), may hold values from -0.25 to 0.25
- right_factor: bfloat16 [512, 64, 64], P('seq'), may hold values from -0.75 to 0.75
Outputs:
- output: bfloat16 [2, 32768, 256], P('dp', 'seq')
- grad_gating: bfloat16 [2, 32768, 256], P('dp', 'seq')
- grad_signal: bfloat16 [2, 32768, 256], P('dp', 'seq')
- grad_left: bfloat16 [64, 512, 512], P('seq')
- grad_right: bfloat16 [512, 64, 64], P('seq')
The draws below stay inside these ranges and needn't reach their ends.
All inputs are finite; a program needn't handle non-finite values.
Results may differ from the reference program's by a relative error of at most 0.0075.
Values may be sent and summed in bfloat16 or wider, within the bound.
No kernel may reach another device: no remote copies, remote signals or barrier semaphores. Data moves between devices by JAX's collectives and lax.ppermute only.
A program may use at most 64 MiB of HBM per device.

```python
import jax
import jax.numpy as jnp
from jax import lax

D = 256
B2 = 512
B1 = 64
LEN = 32768
SEQS = 2


def shard_levels(stream_key, dims, split, least, largest):
    level = 1.0
    for dim, blocks in split:
        heights = jax.random.uniform(jax.random.fold_in(jax.random.fold_in(stream_key, 6), dim), (blocks,), jnp.float32, least / len(split), largest / len(split))
        level = level * jnp.repeat(jnp.exp(heights), dims[dim] // blocks).reshape((-1,) + (1,) * (len(dims) - 1 - dim))
    return level


def normal_values(rng, extent, spread, bound, shards=(), dtype=jnp.bfloat16):
    array = spread * jax.random.normal(rng, extent, jnp.float32)
    if shards:
        array = array * shard_levels(rng, extent, shards, -0.22, 0.18)
    return jnp.clip(array, -bound, bound).astype(dtype)


def setup_inputs(seed: int = 0) -> dict:
    key_list = jax.random.split(jax.random.key(seed), 6)
    return {
        "signal": normal_values(key_list[0], (SEQS, LEN, D), 1.0, 6.0, ((0, 2), (1, 16))),
        "gating": normal_values(key_list[1], (SEQS, LEN, D), 1.0, 6.0, ((0, 2), (1, 16))),
        "upstream": normal_values(key_list[2], (SEQS, LEN, D), 0.25, 1.5, ((0, 2), (1, 16))),
        "left_factor": normal_values(key_list[3], (B1, B2, B2), B2 ** -0.5, 0.25, ((0, 16),)),
        "right_factor": normal_values(key_list[4], (B2, B1, B1), B1 ** -0.5, 0.75, ((0, 16),)),
    }


def rounded(value):
    return lax.optimization_barrier(value.astype(jnp.bfloat16)).astype(jnp.float32)


def reference(signal, gating, upstream, left_factor, right_factor):
    left_full = left_factor.astype(jnp.float32)
    right_full = right_factor.astype(jnp.float32)
    outputs = []
    grad_gates = []
    grad_signals = []
    left_total = jnp.zeros(left_factor.shape, jnp.float32)
    right_total = jnp.zeros(right_factor.shape, jnp.float32)
    for index in range(SEQS):
        values = signal[index].reshape(B1, B2, D).astype(jnp.float32)
        gate_rows = gating[index].reshape(B1, B2, D).astype(jnp.float32)
        upstream_rows = upstream[index].reshape(B1, B2, D).astype(jnp.float32)
        mixed_rows = rounded(jnp.einsum("ikj,ijd->ikd", left_full, values))
        second = rounded(jnp.einsum("kmi,ikd->mkd", right_full, mixed_rows))
        outputs.append((gate_rows * second).astype(jnp.bfloat16).reshape(LEN, D))
        grad_gates.append((upstream_rows * second).astype(jnp.bfloat16).reshape(LEN, D))
        grad_rows = rounded(upstream_rows * gate_rows)
        right_total = right_total + rounded(jnp.einsum("mkd,ikd->kmi", grad_rows, mixed_rows))
        grad_back = rounded(jnp.einsum("kmi,mkd->ikd", right_full, grad_rows))
        left_total = left_total + rounded(jnp.einsum("ikd,ijd->ikj", grad_back, values))
        grad_signals.append(jnp.einsum("ikj,ikd->ijd", left_full, grad_back).astype(jnp.bfloat16).reshape(LEN, D))
    return (jnp.stack(outputs), jnp.stack(grad_gates), jnp.stack(grad_signals),
            left_total.astype(jnp.bfloat16), right_total.astype(jnp.bfloat16))
```

```python
import jax
import jax.numpy as jnp
from jax import lax
from jax.sharding import PartitionSpec as P

BF16 = jnp.bfloat16
F32 = jnp.float32


def exchange(blocks):
    return lax.all_to_all(blocks, "seq", split_axis=0, concat_axis=0, tiled=True)


def swap_sequences(array):
    return lax.ppermute(array, "dp", [(0, 1), (1, 0)])


def shards(signal, gating, upstream, left_factor, right_factor):
    seq = lax.axis_size("seq")
    rows, block_len = left_factor.shape[:2]
    cols, block_count = right_factor.shape[:2]
    channels = signal.shape[2]
    values = signal.reshape(rows, block_len, channels)
    gate = gating.reshape(rows, block_len, channels)
    cotangent = upstream.reshape(rows, block_len, channels)

    def to_send(by_row):
        return by_row.reshape(rows, seq, cols, channels).transpose(1, 0, 2, 3)

    def from_received(blocks):
        return blocks.transpose(1, 0, 2, 3).reshape(rows, block_len, channels)

    def by_column(blocks):
        return blocks.reshape(block_count, cols, channels)

    grad_rows = (cotangent.astype(F32) * gate.astype(F32)).astype(BF16)
    grad_column = by_column(exchange(to_send(grad_rows)))
    other_values = swap_sequences(values)
    mixed_rows = jnp.einsum(
        "ikj,ijd->ikd", left_factor, values, preferred_element_type=F32
    ).astype(BF16)
    mixed_column = by_column(exchange(to_send(mixed_rows)))
    grad_second = jnp.einsum(
        "kmi,mkd->ikd", right_factor, grad_column, preferred_element_type=F32
    ).astype(BF16)
    grad_back = from_received(exchange(grad_second.reshape(seq, rows, cols, channels)))
    second = jnp.einsum(
        "kmi,ikd->mkd", right_factor, mixed_column, preferred_element_type=F32
    ).astype(BF16)
    second_rows = from_received(exchange(second.reshape(seq, rows, cols, channels)))
    right_part = jnp.einsum(
        "mkd,ikd->kmi", grad_column, mixed_column, preferred_element_type=F32
    ).astype(BF16)
    other_right = swap_sequences(right_part)
    other_grad_back = swap_sequences(grad_back)
    grad_signal = jnp.einsum(
        "ikj,ikd->ijd", left_factor, grad_back, preferred_element_type=F32
    ).astype(BF16)

    def left_term(grad, vals):
        return jnp.einsum("ikd,ijd->ikj", grad, vals, preferred_element_type=F32).astype(BF16)

    grad_left = left_term(grad_back, values).astype(F32) + left_term(
        other_grad_back, other_values
    ).astype(F32)
    grad_right = right_part.astype(F32) + other_right.astype(F32)
    wide = second_rows.astype(F32)
    output = (gate.astype(F32) * wide).astype(BF16)
    grad_gate = (cotangent.astype(F32) * wide).astype(BF16)
    return (
        output.reshape(signal.shape),
        grad_gate.reshape(signal.shape),
        grad_signal.reshape(signal.shape),
        grad_left.astype(BF16),
        grad_right.astype(BF16),
    )


def solution(mesh):
    by_position = P("dp", "seq", None)
    by_block = P("seq", None, None)
    return jax.shard_map(
        shards,
        mesh=mesh,
        in_specs=(by_position,) * 3 + (by_block,) * 2,
        out_specs=(by_position,) * 3 + (by_block,) * 2,
        check_vma=False,
    )
```

```python
import functools

import jax
import jax.numpy as jnp
from jax import lax
from jax.experimental import pallas as pl
from jax.experimental.pallas import tpu as pltpu
from jax.sharding import PartitionSpec as P

BF16 = jnp.bfloat16
F32 = jnp.float32
VMEM_LIMIT = 48 * 1024 * 1024


def partner_order(seq):
    return sorted(range(seq), key=lambda s: (-(s // (seq // 2)), s % (seq // 2), s))


def swap_sequences(array):
    return lax.ppermute(array, "dp", [(0, 1), (1, 0)])


def exchange(blocks):
    seq = len(blocks)
    received = list(blocks)
    for s in partner_order(seq):
        if s:
            received[s] = lax.ppermute(blocks[s], "seq", [(i, i ^ s) for i in range(seq)])
    return received


def call(kernel, me, inputs, out_shapes, scratch=(), flops=0):
    whole = pl.BlockSpec(memory_space=pltpu.VMEM)
    moved = sum(x.size * x.dtype.itemsize for x in (*inputs, *out_shapes))
    return pl.pallas_call(
        kernel,
        out_shape=out_shapes,
        in_specs=[pl.BlockSpec(memory_space=pltpu.SMEM)] + [whole] * len(inputs),
        out_specs=[whole] * len(out_shapes),
        scratch_shapes=scratch,
        compiler_params=pltpu.CompilerParams(vmem_limit_bytes=VMEM_LIMIT),
        cost_estimate=pl.CostEstimate(flops=flops, bytes_accessed=moved, transcendentals=0),
    )(me, *inputs)


def dot(a, b, contract):
    return lax.dot_general(a, b, (contract, ((), ())), preferred_element_type=F32)


def product_kernel(seq, me_ref, gate_ref, cotangent_ref, *out_refs):
    me = me_ref[0]
    for s in range(seq):
        c = me ^ s
        wide = gate_ref[:, c].astype(F32) * cotangent_ref[:, c].astype(F32)
        out_refs[s][...] = wide.astype(BF16)


def mix_kernel(seq, me_ref, left_ref, values_ref, *refs):
    out_refs, hold = refs[:seq], refs[seq]
    rows, _, cols, channels = hold.shape
    me = me_ref[0]
    for i in range(rows):
        mixed = dot(left_ref[i], values_ref[i], ((1,), (0,)))
        hold[i] = mixed.astype(BF16).reshape(seq, cols, channels)
    for s in range(seq):
        out_refs[s][...] = hold[:, me ^ s]


def load_columns(seq, me, in_refs, wide):
    rows, cols, channels = in_refs[0].shape
    size = rows * cols
    for s in range(seq):
        block = in_refs[s][...].reshape(size, channels).astype(F32)
        start = pl.multiple_of((me ^ s) * size, size)
        for h in range(channels // 128):
            wide[h, pl.ds(start, size), :] = block[:, h * 128 : (h + 1) * 128]


def column(wide, k, count, cols):
    halves = [wide[h, pl.ds(k, count, stride=cols), :] for h in range(wide.shape[0])]
    return jnp.concatenate(halves, axis=1).astype(BF16)


def store_column(wide, k, count, cols, value):
    for h in range(wide.shape[0]):
        wide[h, pl.ds(k, count, stride=cols), :] = value[:, h * 128 : (h + 1) * 128]


def send_columns(seq, me, wide, out_refs):
    rows, cols, channels = out_refs[0].shape
    size = rows * cols
    for s in range(seq):
        start = pl.multiple_of((me ^ s) * size, size)
        halves = [wide[h, pl.ds(start, size), :] for h in range(wide.shape[0])]
        block = jnp.concatenate(halves, axis=1).astype(BF16)
        out_refs[s][...] = block.reshape(rows, cols, channels)


def column_backward_kernel(seq, me_ref, right_ref, *refs):
    in_refs, out_refs = refs[:seq], refs[seq : 2 * seq]
    by_column_ref, wide, wide_out = refs[2 * seq :]
    cols, count, _ = right_ref.shape
    me = me_ref[0]
    load_columns(seq, me, in_refs, wide)
    for k in range(cols):
        grad = column(wide, k, count, cols)
        by_column_ref[k] = grad
        store_column(wide_out, k, count, cols, dot(right_ref[k], grad, ((0,), (0,))))
    send_columns(seq, me, wide_out, out_refs)


def column_forward_kernel(seq, me_ref, right_ref, grad_ref, *refs):
    in_refs, out_refs = refs[:seq], refs[seq : 2 * seq]
    right_part_ref, wide, wide_out = refs[2 * seq :]
    cols, count, _ = right_ref.shape
    me = me_ref[0]
    load_columns(seq, me, in_refs, wide)
    for k in range(cols):
        mixed = column(wide, k, count, cols)
        store_column(wide_out, k, count, cols, dot(right_ref[k], mixed, ((1,), (0,))))
        right_part_ref[k] = dot(grad_ref[k], mixed, ((1,), (1,))).astype(BF16)
    send_columns(seq, me, wide_out, out_refs)


def gather_kernel(seq, me_ref, *refs):
    in_refs, out_ref = refs[:seq], refs[seq]
    me = me_ref[0]
    for s in range(seq):
        out_ref[:, me ^ s] = in_refs[s][...]


def row_backward_kernel(me_ref, left_ref, values_ref, grad_ref, signal_ref, term_ref):
    for i in range(left_ref.shape[0]):
        grad = grad_ref[i]
        signal_ref[i] = dot(left_ref[i], grad, ((0,), (0,))).astype(BF16)
        term_ref[i] = dot(grad, values_ref[i], ((1,), (1,))).astype(BF16)


def left_sum_kernel(me_ref, term_ref, values_ref, grad_ref, out_ref):
    for i in range(term_ref.shape[0]):
        other = dot(grad_ref[i], values_ref[i], ((1,), (1,))).astype(BF16)
        out_ref[i] = (term_ref[i].astype(F32) + other.astype(F32)).astype(BF16)


def output_kernel(seq, me_ref, gate_ref, cotangent_ref, *refs):
    in_refs, (out_ref, grad_ref) = refs[:seq], refs[seq:]
    me = me_ref[0]
    for s in range(seq):
        c = me ^ s
        second = in_refs[s][...].astype(F32)
        out_ref[:, c] = (gate_ref[:, c].astype(F32) * second).astype(BF16)
        grad_ref[:, c] = (cotangent_ref[:, c].astype(F32) * second).astype(BF16)


def direct_shards(signal, gating, upstream, left_factor, right_factor):
    seq = lax.axis_size("seq")
    rows, block_len = left_factor.shape[:2]
    cols, count = right_factor.shape[:2]
    channels = signal.shape[2]
    me = lax.axis_index("seq").astype(jnp.int32).reshape(1)
    values = signal.reshape(rows, block_len, channels)
    gate = gating.reshape(rows, seq, cols, channels)
    cotangent = upstream.reshape(rows, seq, cols, channels)

    block = jax.ShapeDtypeStruct((rows, cols, channels), BF16)
    blocks = [block] * seq
    whole = jax.ShapeDtypeStruct((rows, seq, cols, channels), BF16)
    by_row = jax.ShapeDtypeStruct((rows, block_len, channels), BF16)
    left = jax.ShapeDtypeStruct(left_factor.shape, BF16)
    right = jax.ShapeDtypeStruct(right_factor.shape, BF16)
    by_column = jax.ShapeDtypeStruct((cols, count, channels), BF16)
    wide = pltpu.VMEM((channels // 128, count * cols, 128), F32)
    row_flops = 2 * rows * block_len * block_len * channels
    column_flops = 2 * cols * count * count * channels

    grad_rows = call(
        functools.partial(product_kernel, seq), me, [gate, cotangent], blocks
    )
    grad_blocks = exchange(grad_rows)
    other_values = swap_sequences(values)
    mixed_rows = call(
        functools.partial(mix_kernel, seq),
        me,
        [left_factor, values],
        blocks,
        [pltpu.VMEM(whole.shape, BF16)],
        row_flops,
    )
    mixed_blocks = exchange(mixed_rows)
    *grad_second, grad_column = call(
        functools.partial(column_backward_kernel, seq),
        me,
        [right_factor, *grad_blocks],
        blocks + [by_column],
        [wide, wide],
        column_flops,
    )
    back_blocks = exchange(grad_second)
    *second, right_part = call(
        functools.partial(column_forward_kernel, seq),
        me,
        [right_factor, grad_column, *mixed_blocks],
        blocks + [right],
        [wide, wide],
        2 * column_flops,
    )
    second_blocks = exchange(second)
    other_right = swap_sequences(right_part)
    (gathered,) = call(functools.partial(gather_kernel, seq), me, back_blocks, [whole])
    grad_back = gathered.reshape(rows, block_len, channels)
    other_grad_back = swap_sequences(grad_back)
    grad_signal, left_term = call(
        row_backward_kernel,
        me,
        [left_factor, values, grad_back],
        [by_row, left],
        flops=2 * row_flops,
    )
    (grad_left,) = call(
        left_sum_kernel,
        me,
        [left_term, other_values, other_grad_back],
        [left],
        flops=row_flops,
    )
    grad_right = (right_part.astype(F32) + other_right.astype(F32)).astype(BF16)
    output, grad_gate = call(
        functools.partial(output_kernel, seq),
        me,
        [gate, cotangent, *second_blocks],
        [whole, whole],
    )
    return (
        output.reshape(signal.shape),
        grad_gate.reshape(signal.shape),
        grad_signal.reshape(signal.shape),
        grad_left,
        grad_right,
    )


def plain_shards(signal, gating, upstream, left_factor, right_factor):
    seq = lax.axis_size("seq")
    rows, block_len = left_factor.shape[:2]
    cols, block_count = right_factor.shape[:2]
    channels = signal.shape[2]
    values = signal.reshape(rows, block_len, channels)
    gate = gating.reshape(rows, block_len, channels)
    cotangent = upstream.reshape(rows, block_len, channels)

    def einsum(spec, a, b):
        return jnp.einsum(spec, a, b, preferred_element_type=F32).astype(BF16)

    def all_to_all(blocks):
        return lax.all_to_all(blocks, "seq", split_axis=0, concat_axis=0, tiled=True)

    def to_columns(by_row):
        blocks = by_row.reshape(rows, seq, cols, channels).transpose(1, 0, 2, 3)
        return all_to_all(blocks).reshape(block_count, cols, channels)

    def to_rows(by_column):
        blocks = all_to_all(by_column.reshape(seq, rows, cols, channels))
        return blocks.transpose(1, 0, 2, 3).reshape(rows, block_len, channels)

    grad_rows = (cotangent.astype(F32) * gate.astype(F32)).astype(BF16)
    grad_column = to_columns(grad_rows)
    other_values = swap_sequences(values)
    mixed_column = to_columns(einsum("ikj,ijd->ikd", left_factor, values))
    grad_back = to_rows(einsum("kmi,mkd->ikd", right_factor, grad_column))
    second_rows = to_rows(einsum("kmi,ikd->mkd", right_factor, mixed_column))
    right_part = einsum("mkd,ikd->kmi", grad_column, mixed_column)
    other_right = swap_sequences(right_part)
    other_grad_back = swap_sequences(grad_back)
    grad_signal = einsum("ikj,ikd->ijd", left_factor, grad_back)
    left_term = einsum("ikd,ijd->ikj", grad_back, values)
    other_left = einsum("ikd,ijd->ikj", other_grad_back, other_values)
    grad_left = (left_term.astype(F32) + other_left.astype(F32)).astype(BF16)
    grad_right = (right_part.astype(F32) + other_right.astype(F32)).astype(BF16)
    wide = second_rows.astype(F32)
    output = (gate.astype(F32) * wide).astype(BF16)
    grad_gate = (cotangent.astype(F32) * wide).astype(BF16)
    return (
        output.reshape(signal.shape),
        grad_gate.reshape(signal.shape),
        grad_signal.reshape(signal.shape),
        grad_left,
        grad_right,
    )


def shards(signal, gating, upstream, left_factor, right_factor):
    seq = lax.axis_size("seq")
    cols = right_factor.shape[0]
    direct = seq <= 16 and seq & (seq - 1) == 0 and cols % 32 == 0
    run = direct_shards if direct else plain_shards
    return run(signal, gating, upstream, left_factor, right_factor)


def solution(mesh):
    by_position = P("dp", "seq", None)
    by_block = P("seq", None, None)
    return jax.shard_map(
        shards,
        mesh=mesh,
        in_specs=(by_position,) * 3 + (by_block,) * 2,
        out_specs=(by_position,) * 3 + (by_block,) * 2,
        check_vma=False,
    )
```

```python
import jax
import jax.numpy as jnp
from jax import lax
from jax.experimental import pallas as pl
from jax.experimental.pallas import tpu as pltpu
from jax.sharding import PartitionSpec as P

BF16 = jnp.bfloat16
F32 = jnp.float32
VMEM_LIMIT = 48 * 1024 * 1024


def swap_sequences(array):
    return lax.ppermute(array, "dp", [(0, 1), (1, 0)])


def exchange(blocks):
    return lax.all_to_all(blocks, "seq", split_axis=0, concat_axis=0, tiled=True)


def call(kernel, inputs, out_shapes, scratch=(), flops=0):
    whole = pl.BlockSpec(memory_space=pltpu.VMEM)
    moved = sum(x.size * x.dtype.itemsize for x in (*inputs, *out_shapes))
    return pl.pallas_call(
        kernel,
        out_shape=out_shapes,
        in_specs=[whole] * len(inputs),
        out_specs=[whole] * len(out_shapes),
        scratch_shapes=scratch,
        compiler_params=pltpu.CompilerParams(vmem_limit_bytes=VMEM_LIMIT),
        cost_estimate=pl.CostEstimate(flops=flops, bytes_accessed=moved, transcendentals=0),
    )(*inputs)


def dot(a, b, contract):
    return lax.dot_general(a, b, (contract, ((), ())), preferred_element_type=F32)


def product_kernel(gate_ref, cotangent_ref, out_ref):
    for i in range(gate_ref.shape[0]):
        wide = gate_ref[i].astype(F32) * cotangent_ref[i].astype(F32)
        out_ref[:, i] = wide.astype(BF16)


def mix_kernel(left_ref, values_ref, out_ref):
    seq, rows, cols, channels = out_ref.shape
    for i in range(rows):
        mixed = dot(left_ref[i], values_ref[i], ((1,), (0,)))
        out_ref[:, i] = mixed.astype(BF16).reshape(seq, cols, channels)


def load_columns(in_ref, wide):
    for p in range(in_ref.shape[0]):
        rows, cols, channels = in_ref.shape[1:]
        size = rows * cols
        block = in_ref[p].reshape(size, channels).astype(F32)
        for h in range(channels // 128):
            wide[h, p * size : (p + 1) * size, :] = block[:, h * 128 : (h + 1) * 128]


def column(wide, k, count, cols):
    halves = [wide[h, pl.ds(k, count, stride=cols), :] for h in range(wide.shape[0])]
    return jnp.concatenate(halves, axis=1).astype(BF16)


def store_column(wide, k, count, cols, value):
    for h in range(wide.shape[0]):
        wide[h, pl.ds(k, count, stride=cols), :] = value[:, h * 128 : (h + 1) * 128]


def store_blocks(wide, out_ref):
    seq, rows, cols, channels = out_ref.shape
    size = rows * cols
    for p in range(seq):
        halves = [wide[h, p * size : (p + 1) * size, :] for h in range(wide.shape[0])]
        block = jnp.concatenate(halves, axis=1).astype(BF16)
        out_ref[p] = block.reshape(rows, cols, channels)


def column_backward_kernel(right_ref, in_ref, out_ref, by_column_ref, wide, wide_out):
    cols, count, _ = right_ref.shape
    load_columns(in_ref, wide)
    for k in range(cols):
        grad = column(wide, k, count, cols)
        by_column_ref[k] = grad
        store_column(wide_out, k, count, cols, dot(right_ref[k], grad, ((0,), (0,))))
    store_blocks(wide_out, out_ref)


def column_forward_kernel(right_ref, grad_ref, in_ref, out_ref, part_ref, wide, wide_out):
    cols, count, _ = right_ref.shape
    load_columns(in_ref, wide)
    for k in range(cols):
        mixed = column(wide, k, count, cols)
        store_column(wide_out, k, count, cols, dot(right_ref[k], mixed, ((1,), (0,))))
        part_ref[k] = dot(grad_ref[k], mixed, ((1,), (1,))).astype(BF16)
    store_blocks(wide_out, out_ref)


def gather_kernel(in_ref, out_ref):
    for i in range(out_ref.shape[0]):
        out_ref[i] = in_ref[:, i]


def row_backward_kernel(left_ref, values_ref, grad_ref, signal_ref, term_ref):
    for i in range(left_ref.shape[0]):
        grad = grad_ref[i]
        signal_ref[i] = dot(left_ref[i], grad, ((0,), (0,))).astype(BF16)
        term_ref[i] = dot(grad, values_ref[i], ((1,), (1,))).astype(BF16)


def left_sum_kernel(term_ref, values_ref, grad_ref, out_ref):
    for i in range(term_ref.shape[0]):
        other = dot(grad_ref[i], values_ref[i], ((1,), (1,))).astype(BF16)
        out_ref[i] = (term_ref[i].astype(F32) + other.astype(F32)).astype(BF16)


def output_kernel(gate_ref, cotangent_ref, in_ref, out_ref, grad_ref):
    for i in range(gate_ref.shape[0]):
        second = in_ref[:, i].astype(F32)
        out_ref[i] = (gate_ref[i].astype(F32) * second).astype(BF16)
        grad_ref[i] = (cotangent_ref[i].astype(F32) * second).astype(BF16)


def direct_shards(signal, gating, upstream, left_factor, right_factor):
    seq = lax.axis_size("seq")
    rows, block_len = left_factor.shape[:2]
    cols, count = right_factor.shape[:2]
    channels = signal.shape[2]
    values = signal.reshape(rows, block_len, channels)
    gate = gating.reshape(rows, seq, cols, channels)
    cotangent = upstream.reshape(rows, seq, cols, channels)

    blocks = jax.ShapeDtypeStruct((seq, rows, cols, channels), BF16)
    whole = jax.ShapeDtypeStruct((rows, seq, cols, channels), BF16)
    by_row = jax.ShapeDtypeStruct((rows, block_len, channels), BF16)
    left = jax.ShapeDtypeStruct(left_factor.shape, BF16)
    right = jax.ShapeDtypeStruct(right_factor.shape, BF16)
    by_column = jax.ShapeDtypeStruct((cols, count, channels), BF16)
    wide = pltpu.VMEM((channels // 128, count * cols, 128), F32)
    row_flops = 2 * rows * block_len * block_len * channels
    column_flops = 2 * cols * count * count * channels

    (grad_rows,) = call(product_kernel, [gate, cotangent], [blocks])
    grad_blocks = exchange(grad_rows)
    other_values = swap_sequences(values)
    (mixed_rows,) = call(mix_kernel, [left_factor, values], [blocks], flops=row_flops)
    mixed_blocks = exchange(mixed_rows)
    grad_second, grad_column = call(
        column_backward_kernel,
        [right_factor, grad_blocks],
        [blocks, by_column],
        [wide, wide],
        column_flops,
    )
    back_blocks = exchange(grad_second)
    second, right_part = call(
        column_forward_kernel,
        [right_factor, grad_column, mixed_blocks],
        [blocks, right],
        [wide, wide],
        2 * column_flops,
    )
    second_blocks = exchange(second)
    other_right = swap_sequences(right_part)
    (gathered,) = call(gather_kernel, [back_blocks], [whole])
    grad_back = gathered.reshape(rows, block_len, channels)
    other_grad_back = swap_sequences(grad_back)
    grad_signal, left_term = call(
        row_backward_kernel, [left_factor, values, grad_back], [by_row, left], flops=2 * row_flops
    )
    (grad_left,) = call(
        left_sum_kernel, [left_term, other_values, other_grad_back], [left], flops=row_flops
    )
    grad_right = (right_part.astype(F32) + other_right.astype(F32)).astype(BF16)
    output, grad_gate = call(output_kernel, [gate, cotangent, second_blocks], [whole, whole])
    return (
        output.reshape(signal.shape),
        grad_gate.reshape(signal.shape),
        grad_signal.reshape(signal.shape),
        grad_left,
        grad_right,
    )


def plain_shards(signal, gating, upstream, left_factor, right_factor):
    seq = lax.axis_size("seq")
    rows, block_len = left_factor.shape[:2]
    cols, block_count = right_factor.shape[:2]
    channels = signal.shape[2]
    values = signal.reshape(rows, block_len, channels)
    gate = gating.reshape(rows, block_len, channels)
    cotangent = upstream.reshape(rows, block_len, channels)

    def einsum(spec, a, b):
        return jnp.einsum(spec, a, b, preferred_element_type=F32).astype(BF16)

    def all_to_all(blocks):
        return lax.all_to_all(blocks, "seq", split_axis=0, concat_axis=0, tiled=True)

    def to_columns(by_row):
        blocks = by_row.reshape(rows, seq, cols, channels).transpose(1, 0, 2, 3)
        return all_to_all(blocks).reshape(block_count, cols, channels)

    def to_rows(by_column):
        blocks = all_to_all(by_column.reshape(seq, rows, cols, channels))
        return blocks.transpose(1, 0, 2, 3).reshape(rows, block_len, channels)

    grad_rows = (cotangent.astype(F32) * gate.astype(F32)).astype(BF16)
    grad_column = to_columns(grad_rows)
    other_values = swap_sequences(values)
    mixed_column = to_columns(einsum("ikj,ijd->ikd", left_factor, values))
    grad_back = to_rows(einsum("kmi,mkd->ikd", right_factor, grad_column))
    second_rows = to_rows(einsum("kmi,ikd->mkd", right_factor, mixed_column))
    right_part = einsum("mkd,ikd->kmi", grad_column, mixed_column)
    other_right = swap_sequences(right_part)
    other_grad_back = swap_sequences(grad_back)
    grad_signal = einsum("ikj,ikd->ijd", left_factor, grad_back)
    left_term = einsum("ikd,ijd->ikj", grad_back, values)
    other_left = einsum("ikd,ijd->ikj", other_grad_back, other_values)
    grad_left = (left_term.astype(F32) + other_left.astype(F32)).astype(BF16)
    grad_right = (right_part.astype(F32) + other_right.astype(F32)).astype(BF16)
    wide = second_rows.astype(F32)
    output = (gate.astype(F32) * wide).astype(BF16)
    grad_gate = (cotangent.astype(F32) * wide).astype(BF16)
    return (
        output.reshape(signal.shape),
        grad_gate.reshape(signal.shape),
        grad_signal.reshape(signal.shape),
        grad_left,
        grad_right,
    )


def shards(signal, gating, upstream, left_factor, right_factor):
    seq = lax.axis_size("seq")
    cols = right_factor.shape[0]
    direct = seq <= 16 and seq & (seq - 1) == 0 and cols % 32 == 0
    run = direct_shards if direct else plain_shards
    return run(signal, gating, upstream, left_factor, right_factor)


def solution(mesh):
    by_position = P("dp", "seq", None)
    by_block = P("seq", None, None)
    return jax.shard_map(
        shards,
        mesh=mesh,
        in_specs=(by_position,) * 3 + (by_block,) * 2,
        out_specs=(by_position,) * 3 + (by_block,) * 2,
        check_vma=False,
    )
```

```python
import functools

import jax
import jax.numpy as jnp
from jax import lax
from jax.experimental import pallas as pl
from jax.experimental.pallas import tpu as pltpu
from jax.sharding import PartitionSpec as P

BF16 = jnp.bfloat16
F32 = jnp.float32
VMEM_LIMIT = 48 * 1024 * 1024


def partner_order(seq):
    half = seq // 2
    near = sorted(range(1, half), key=lambda s: (s % max(half // 2, 1), s))
    order = []
    for n in range(half):
        order += [half + n] + near[n : n + 1]
    return order


def sorted_partners(seq):
    listed = [0] * seq
    names = sorted(range(seq - 1), key=lambda n: str(n) if n else "")
    for name, s in zip(names, partner_order(seq)):
        listed[name + 1] = s
    return listed


def swap_sequences(array):
    return lax.ppermute(array, "dp", [(0, 1), (1, 0)])


def exchange(blocks):
    seq = len(blocks)
    received = list(blocks)
    for s in partner_order(seq):
        received[s] = lax.ppermute(blocks[s], "seq", [(i, i ^ s) for i in range(seq)])
    return received


def after(array, earlier):
    return lax.optimization_barrier((array, earlier))[0]


def call(kernel, me, inputs, out_shapes, scratch=(), flops=0, unread=None):
    whole = pl.BlockSpec(memory_space=pltpu.VMEM)
    moved = sum(x.size * x.dtype.itemsize for x in (*inputs, *out_shapes))
    return pl.pallas_call(
        kernel,
        out_shape=out_shapes,
        in_specs=[pl.BlockSpec(memory_space=pltpu.SMEM)] + [
            pl.BlockSpec(memory_space=pl.ANY) if n == unread else whole for n in range(len(inputs))
        ],
        out_specs=[whole] * len(out_shapes),
        scratch_shapes=scratch,
        compiler_params=pltpu.CompilerParams(vmem_limit_bytes=VMEM_LIMIT),
        cost_estimate=pl.CostEstimate(flops=flops, bytes_accessed=moved, transcendentals=0),
    )(me, *inputs)


def dot(a, b, contract):
    return lax.dot_general(a, b, (contract, ((), ())), preferred_element_type=F32)


def send_kernel(seq, me_ref, gate_ref, cotangent_ref, left_ref, values_ref, *refs):
    out_refs, hold = refs[:seq], refs[seq]
    rows, _, cols, channels = hold.shape
    me = me_ref[0]
    for i in range(rows):
        mixed = dot(left_ref[i], values_ref[i], ((1,), (0,)))
        hold[i] = mixed.astype(BF16).reshape(seq, cols, channels)
    for s in range(seq):
        c = me ^ s
        wide = gate_ref[:, c].astype(F32) * cotangent_ref[:, c].astype(F32)
        out_refs[s][0] = wide.astype(BF16)
        out_refs[s][1] = hold[:, c]


def load_columns(seq, me, in_refs, which, wide):
    rows, cols, channels = in_refs[0].shape[1:]
    size = rows * cols
    for s, in_ref in zip(sorted_partners(seq), in_refs):
        block = in_ref[which].reshape(size, channels).astype(F32)
        start = pl.multiple_of((me ^ s) * size, size)
        for h in range(channels // 128):
            wide[h, pl.ds(start, size), :] = block[:, h * 128 : (h + 1) * 128]


def column(wide, k, count, cols):
    halves = [wide[h, pl.ds(k, count, stride=cols), :] for h in range(wide.shape[0])]
    return jnp.concatenate(halves, axis=1).astype(BF16)


def store_column(wide, k, count, cols, value):
    for h in range(wide.shape[0]):
        wide[h, pl.ds(k, count, stride=cols), :] = value[:, h * 128 : (h + 1) * 128]


def send_columns(seq, me, wide, out_refs):
    rows, cols, channels = out_refs[0].shape
    size = rows * cols
    for s in range(seq):
        start = pl.multiple_of((me ^ s) * size, size)
        halves = [wide[h, pl.ds(start, size), :] for h in range(wide.shape[0])]
        block = jnp.concatenate(halves, axis=1).astype(BF16)
        out_refs[s][...] = block.reshape(rows, cols, channels)


def column_backward_kernel(seq, me_ref, right_ref, *refs):
    in_refs, out_refs = refs[:seq], refs[seq : 2 * seq]
    by_column_ref, wide, wide_out = refs[2 * seq :]
    cols, count, _ = right_ref.shape
    me = me_ref[0]
    load_columns(seq, me, in_refs, 0, wide)
    for k in range(cols):
        grad = column(wide, k, count, cols)
        by_column_ref[k] = grad
        store_column(wide_out, k, count, cols, dot(right_ref[k], grad, ((0,), (0,))))
    send_columns(seq, me, wide_out, out_refs)


def column_forward_kernel(seq, me_ref, right_ref, grad_ref, after_ref, *refs):
    in_refs, out_refs = refs[:seq], refs[seq : 2 * seq]
    right_part_ref, wide, wide_out = refs[2 * seq :]
    cols, count, _ = right_ref.shape
    me = me_ref[0]
    load_columns(seq, me, in_refs, 1, wide)
    for k in range(cols):
        mixed = column(wide, k, count, cols)
        store_column(wide_out, k, count, cols, dot(right_ref[k], mixed, ((1,), (0,))))
        right_part_ref[k] = dot(grad_ref[k], mixed, ((1,), (1,))).astype(BF16)
    send_columns(seq, me, wide_out, out_refs)


def gather_kernel(seq, me_ref, *refs):
    in_refs, out_ref = refs[:seq], refs[seq]
    me = me_ref[0]
    for s, in_ref in zip([0] + partner_order(seq), in_refs):
        out_ref[:, me ^ s] = in_ref[...]


def row_backward_kernel(me_ref, left_ref, values_ref, grad_ref, signal_ref, term_ref):
    for i in range(left_ref.shape[0]):
        grad = grad_ref[i]
        signal_ref[i] = dot(left_ref[i], grad, ((0,), (0,))).astype(BF16)
        term_ref[i] = dot(grad, values_ref[i], ((1,), (1,))).astype(BF16)


def factor_sum_kernel(
    me_ref, term_ref, values_ref, grad_ref, right_ref, other_ref, left_out_ref, right_out_ref
):
    for i in range(term_ref.shape[0]):
        other = dot(grad_ref[i], values_ref[i], ((1,), (1,))).astype(BF16)
        left_out_ref[i] = (term_ref[i].astype(F32) + other.astype(F32)).astype(BF16)
    right_out_ref[...] = (right_ref[...].astype(F32) + other_ref[...].astype(F32)).astype(BF16)


def output_kernel(seq, me_ref, gate_ref, cotangent_ref, *refs):
    in_refs, (out_ref, grad_ref) = refs[:seq], refs[seq:]
    me = me_ref[0]
    for s, in_ref in zip([0] + partner_order(seq), in_refs):
        c = me ^ s
        second = in_ref[...].astype(F32)
        out_ref[:, c] = (gate_ref[:, c].astype(F32) * second).astype(BF16)
        grad_ref[:, c] = (cotangent_ref[:, c].astype(F32) * second).astype(BF16)


def direct_shards(signal, gating, upstream, left_factor, right_factor):
    seq = lax.axis_size("seq")
    rows, block_len = left_factor.shape[:2]
    cols, count = right_factor.shape[:2]
    channels = signal.shape[2]
    me = lax.axis_index("seq").astype(jnp.int32).reshape(1)
    values = signal.reshape(rows, block_len, channels)
    gate = gating.reshape(rows, seq, cols, channels)
    cotangent = upstream.reshape(rows, seq, cols, channels)

    block = jax.ShapeDtypeStruct((rows, cols, channels), BF16)
    blocks = [block] * seq
    whole = jax.ShapeDtypeStruct((rows, seq, cols, channels), BF16)
    by_row = jax.ShapeDtypeStruct((rows, block_len, channels), BF16)
    left = jax.ShapeDtypeStruct(left_factor.shape, BF16)
    right = jax.ShapeDtypeStruct(right_factor.shape, BF16)
    by_column = jax.ShapeDtypeStruct((cols, count, channels), BF16)
    wide = pltpu.VMEM((channels // 128, count * cols, 128), F32)
    row_flops = 2 * rows * block_len * block_len * channels
    column_flops = 2 * cols * count * count * channels

    pair = jax.ShapeDtypeStruct((2, rows, cols, channels), BF16)
    sent = call(
        functools.partial(send_kernel, seq),
        me,
        [gate, cotangent, left_factor, values],
        [pair] * seq,
        [pltpu.VMEM(whole.shape, BF16)],
        row_flops,
    )
    received = exchange(sent)
    columns = [received[s] for s in sorted_partners(seq)]
    other_values = swap_sequences(values)
    *grad_second, grad_column = call(
        functools.partial(column_backward_kernel, seq),
        me,
        [right_factor, *columns],
        blocks + [by_column],
        [wide, wide],
        column_flops,
    )
    *second, right_part = call(
        functools.partial(column_forward_kernel, seq),
        me,
        [right_factor, grad_column, other_values, *columns],
        blocks + [right],
        [wide, wide],
        2 * column_flops,
        unread=2,
    )
    order = partner_order(seq)
    for s in order[seq // 2 :]:
        grad_second[s] = after(grad_second[s], right_part)
    back_blocks = exchange(grad_second)
    back_blocks = [back_blocks[s] for s in [0] + order]
    second_blocks = exchange(second)
    second_blocks = [second_blocks[s] for s in [0] + order]
    other_right = swap_sequences(right_part)
    (gathered,) = call(functools.partial(gather_kernel, seq), me, back_blocks, [whole])
    grad_back = gathered.reshape(rows, block_len, channels)
    other_grad_back = swap_sequences(grad_back)
    grad_signal, left_term = call(
        row_backward_kernel,
        me,
        [left_factor, values, grad_back],
        [by_row, left],
        flops=2 * row_flops,
    )
    grad_left, grad_right = call(
        factor_sum_kernel,
        me,
        [left_term, other_values, other_grad_back, right_part, other_right],
        [left, right],
        flops=row_flops,
    )
    output, grad_gate = call(
        functools.partial(output_kernel, seq),
        me,
        [gate, cotangent, *second_blocks],
        [whole, whole],
    )
    return (
        output.reshape(signal.shape),
        grad_gate.reshape(signal.shape),
        grad_signal.reshape(signal.shape),
        grad_left,
        grad_right,
    )


def plain_shards(signal, gating, upstream, left_factor, right_factor):
    seq = lax.axis_size("seq")
    rows, block_len = left_factor.shape[:2]
    cols, block_count = right_factor.shape[:2]
    channels = signal.shape[2]
    values = signal.reshape(rows, block_len, channels)
    gate = gating.reshape(rows, block_len, channels)
    cotangent = upstream.reshape(rows, block_len, channels)

    def einsum(spec, a, b):
        return jnp.einsum(spec, a, b, preferred_element_type=F32).astype(BF16)

    def all_to_all(blocks):
        return lax.all_to_all(blocks, "seq", split_axis=0, concat_axis=0, tiled=True)

    def to_columns(by_row):
        blocks = by_row.reshape(rows, seq, cols, channels).transpose(1, 0, 2, 3)
        return all_to_all(blocks).reshape(block_count, cols, channels)

    def to_rows(by_column):
        blocks = all_to_all(by_column.reshape(seq, rows, cols, channels))
        return blocks.transpose(1, 0, 2, 3).reshape(rows, block_len, channels)

    grad_rows = (cotangent.astype(F32) * gate.astype(F32)).astype(BF16)
    grad_column = to_columns(grad_rows)
    other_values = swap_sequences(values)
    mixed_column = to_columns(einsum("ikj,ijd->ikd", left_factor, values))
    grad_back = to_rows(einsum("kmi,mkd->ikd", right_factor, grad_column))
    second_rows = to_rows(einsum("kmi,ikd->mkd", right_factor, mixed_column))
    right_part = einsum("mkd,ikd->kmi", grad_column, mixed_column)
    other_right = swap_sequences(right_part)
    other_grad_back = swap_sequences(grad_back)
    grad_signal = einsum("ikj,ikd->ijd", left_factor, grad_back)
    left_term = einsum("ikd,ijd->ikj", grad_back, values)
    other_left = einsum("ikd,ijd->ikj", other_grad_back, other_values)
    grad_left = (left_term.astype(F32) + other_left.astype(F32)).astype(BF16)
    grad_right = (right_part.astype(F32) + other_right.astype(F32)).astype(BF16)
    wide = second_rows.astype(F32)
    output = (gate.astype(F32) * wide).astype(BF16)
    grad_gate = (cotangent.astype(F32) * wide).astype(BF16)
    return (
        output.reshape(signal.shape),
        grad_gate.reshape(signal.shape),
        grad_signal.reshape(signal.shape),
        grad_left,
        grad_right,
    )


def shards(signal, gating, upstream, left_factor, right_factor):
    seq = lax.axis_size("seq")
    cols = right_factor.shape[0]
    direct = seq <= 16 and seq & (seq - 1) == 0 and cols % 32 == 0
    run = direct_shards if direct else plain_shards
    return run(signal, gating, upstream, left_factor, right_factor)


def solution(mesh):
    by_position = P("dp", "seq", None)
    by_block = P("seq", None, None)
    return jax.shard_map(
        shards,
        mesh=mesh,
        in_specs=(by_position,) * 3 + (by_block,) * 2,
        out_specs=(by_position,) * 3 + (by_block,) * 2,
        check_vma=False,
    )
```

```python
import functools

import jax
import jax.numpy as jnp
from jax import lax
from jax.experimental import pallas as pl
from jax.experimental.pallas import tpu as pltpu
from jax.sharding import PartitionSpec as P

BF16 = jnp.bfloat16
F32 = jnp.float32
MIB = 1024 * 1024


def swap_sequences(array):
    return lax.ppermute(array, "dp", [(0, 1), (1, 0)])


def after(array, earlier):
    return lax.optimization_barrier((array, earlier))[0]


def exchange(near, far):
    half = len(far)
    seq = 2 * half
    groups = [list(range(half)), list(range(half, seq))]
    near = lax.all_to_all(
        near, "seq", split_axis=0, concat_axis=0, axis_index_groups=groups, tiled=True
    )
    far = [
        lax.ppermute(block, "seq", [(i, i ^ (half + t)) for i in range(seq)])
        for t, block in enumerate(far)
    ]
    return near, far


def call(kernel, me, inputs, out_shapes, scratch=(), flops=0, unblocked=(), vmem=40):
    whole = pl.BlockSpec(memory_space=pltpu.VMEM)
    moved = sum(x.size * x.dtype.itemsize for x in (*inputs, *out_shapes))
    in_specs = [
        pl.BlockSpec(memory_space=pl.ANY) if n in unblocked else whole for n in range(len(inputs))
    ]
    return pl.pallas_call(
        kernel,
        out_shape=out_shapes,
        in_specs=[pl.BlockSpec(memory_space=pltpu.SMEM)] + in_specs,
        out_specs=[whole] * len(out_shapes),
        scratch_shapes=scratch,
        compiler_params=pltpu.CompilerParams(vmem_limit_bytes=vmem * MIB),
        cost_estimate=pl.CostEstimate(flops=flops, bytes_accessed=moved, transcendentals=0),
    )(me, *inputs)


def dot(a, b, contract):
    return lax.dot_general(a, b, (contract, ((), ())), preferred_element_type=F32)


def block_views(half, me, near_ref, far_refs):
    base = me // half * half
    near = [(base + p, near_ref.at[p]) for p in range(half)]
    return near + [(me ^ (half + t), far_refs[t]) for t in range(half)]


def send_kernel(half, me_ref, gate_hbm, cotangent_hbm, left_hbm, values_hbm, *refs):
    near_ref, far_refs = refs[0], refs[1 : half + 1]
    gate, cotangent, left, values, hold, sems = refs[half + 1 :]
    rows, seq, cols, channels = hold.shape
    me = me_ref[0]
    loads = []
    for i in range(rows):
        for n, (source, target) in enumerate(((left_hbm, left), (values_hbm, values))):
            loads.append(pltpu.make_async_copy(source.at[i], target.at[i], sems.at[n, i]))
    loads.append(pltpu.make_async_copy(gate_hbm, gate, sems.at[2, 0]))
    loads.append(pltpu.make_async_copy(cotangent_hbm, cotangent, sems.at[2, 1]))
    for load in loads:
        load.start()
    for i in range(rows):
        loads[2 * i].wait()
        loads[2 * i + 1].wait()
        mixed = dot(left[i], values[i], ((1,), (0,)))
        hold[i] = mixed.astype(BF16).reshape(seq, cols, channels)
    loads[-2].wait()
    loads[-1].wait()
    for c, ref in block_views(half, me, near_ref, far_refs):
        wide = gate[:, c].astype(F32) * cotangent[:, c].astype(F32)
        ref[0] = wide.astype(BF16)
        ref[1] = hold[:, c]


def load_columns(half, me, near_ref, far_refs, which, wide):
    rows, cols, channels = far_refs[0].shape[1:]
    size = rows * cols
    for c, ref in block_views(half, me, near_ref, far_refs):
        block = ref[which].reshape(size, channels).astype(F32)
        start = pl.multiple_of(c * size, size)
        for h in range(channels // 128):
            wide[h, pl.ds(start, size), :] = block[:, h * 128 : (h + 1) * 128]


def column(wide, k, count, cols):
    halves = [wide[h, pl.ds(k, count, stride=cols), :] for h in range(wide.shape[0])]
    return jnp.concatenate(halves, axis=1).astype(BF16)


def store_column(wide, k, count, cols, value):
    for h in range(wide.shape[0]):
        wide[h, pl.ds(k, count, stride=cols), :] = value[:, h * 128 : (h + 1) * 128]


def send_columns(half, me, wide, near_ref, far_refs):
    rows, cols, channels = far_refs[0].shape
    size = rows * cols
    for c, ref in block_views(half, me, near_ref, far_refs):
        start = pl.multiple_of(c * size, size)
        halves = [wide[h, pl.ds(start, size), :] for h in range(wide.shape[0])]
        block = jnp.concatenate(halves, axis=1).astype(BF16)
        ref[...] = block.reshape(rows, cols, channels)


def column_backward_kernel(half, me_ref, right_ref, near_ref, *refs):
    far_refs, near_out, far_out = refs[:half], refs[half], refs[half + 1 : 2 * half + 1]
    by_column_ref, wide, wide_out = refs[2 * half + 1 :]
    cols, count, _ = right_ref.shape
    me = me_ref[0]
    load_columns(half, me, near_ref, far_refs, 0, wide)
    for k in range(cols):
        grad = column(wide, k, count, cols)
        by_column_ref[k] = grad
        store_column(wide_out, k, count, cols, dot(right_ref[k], grad, ((0,), (0,))))
    send_columns(half, me, wide_out, near_out, far_out)


def column_forward_kernel(half, me_ref, right_ref, grad_ref, after_ref, near_ref, *refs):
    far_refs, near_out, far_out = refs[:half], refs[half], refs[half + 1 : 2 * half + 1]
    right_part_ref, wide, wide_out = refs[2 * half + 1 :]
    cols, count, _ = right_ref.shape
    me = me_ref[0]
    load_columns(half, me, near_ref, far_refs, 1, wide)
    for k in range(cols):
        mixed = column(wide, k, count, cols)
        store_column(wide_out, k, count, cols, dot(right_ref[k], mixed, ((1,), (0,))))
        right_part_ref[k] = dot(grad_ref[k], mixed, ((1,), (1,))).astype(BF16)
    send_columns(half, me, wide_out, near_out, far_out)


def gather_kernel(half, me_ref, near_ref, *refs):
    for c, ref in block_views(half, me_ref[0], near_ref, refs[:half]):
        refs[half][:, c] = ref[...]


def row_backward_kernel(me_ref, left_ref, values_ref, grad_ref, signal_ref, term_ref):
    for i in range(left_ref.shape[0]):
        grad = grad_ref[i]
        signal_ref[i] = dot(left_ref[i], grad, ((0,), (0,))).astype(BF16)
        term_ref[i] = dot(grad, values_ref[i], ((1,), (1,))).astype(BF16)


def factor_sum_kernel(
    me_ref, term_ref, values_ref, grad_ref, right_ref, other_ref, left_out_ref, right_out_ref
):
    for i in range(term_ref.shape[0]):
        other = dot(grad_ref[i], values_ref[i], ((1,), (1,))).astype(BF16)
        left_out_ref[i] = (term_ref[i].astype(F32) + other.astype(F32)).astype(BF16)
    right_out_ref[...] = (right_ref[...].astype(F32) + other_ref[...].astype(F32)).astype(BF16)


def output_kernel(half, me_ref, gate_ref, cotangent_ref, near_ref, *refs):
    far_refs, (out_ref, grad_ref) = refs[:half], refs[half:]
    for c, ref in block_views(half, me_ref[0], near_ref, far_refs):
        second = ref[...].astype(F32)
        out_ref[:, c] = (gate_ref[:, c].astype(F32) * second).astype(BF16)
        grad_ref[:, c] = (cotangent_ref[:, c].astype(F32) * second).astype(BF16)


def direct_shards(signal, gating, upstream, left_factor, right_factor):
    seq = lax.axis_size("seq")
    half = seq // 2
    rows, block_len = left_factor.shape[:2]
    cols, count = right_factor.shape[:2]
    channels = signal.shape[2]
    me = lax.axis_index("seq").astype(jnp.int32).reshape(1)
    values = signal.reshape(rows, block_len, channels)
    gate = gating.reshape(rows, seq, cols, channels)
    cotangent = upstream.reshape(rows, seq, cols, channels)

    def shape(*dims):
        return jax.ShapeDtypeStruct(dims, BF16)

    def with_half(kernel):
        return functools.partial(kernel, half)

    block = (rows, cols, channels)
    pairs = [shape(half, 2, *block)] + [shape(2, *block)] * half
    blocks = [shape(half, *block)] + [shape(*block)] * half
    whole = shape(rows, seq, cols, channels)
    by_row = shape(rows, block_len, channels)
    left = shape(*left_factor.shape)
    right = shape(*right_factor.shape)
    wide = pltpu.VMEM((channels // 128, count * cols, 128), F32)
    row_flops = 2 * rows * block_len * block_len * channels
    column_flops = 2 * cols * count * count * channels

    near, *far = call(
        with_half(send_kernel),
        me,
        [gate, cotangent, left_factor, values],
        pairs,
        [pltpu.VMEM(x.shape, BF16) for x in (gate, cotangent, left_factor, values, whole)]
        + [pltpu.SemaphoreType.DMA((3, max(rows, 2)))],
        row_flops,
        unblocked=range(4),
        vmem=60,
    )
    other_values = swap_sequences(after(values, near))
    near, far = exchange(near, far)
    *second_in, grad_column = call(
        with_half(column_backward_kernel),
        me,
        [right_factor, near, *far],
        blocks + [shape(cols, count, channels)],
        [wide, wide],
        column_flops,
    )
    back_near, *back_far = second_in
    second_near, *second_far, right_part = call(
        with_half(column_forward_kernel),
        me,
        [right_factor, grad_column, other_values, near, *far],
        blocks + [right],
        [wide, wide],
        2 * column_flops,
        unblocked=[2],
    )
    other_right = swap_sequences(right_part)
    back_far[half // 2 :] = [after(x, right_part) for x in back_far[half // 2 :]]
    back_near, back_far = exchange(back_near, back_far)
    (gathered,) = call(with_half(gather_kernel), me, [back_near, *back_far], [whole])
    grad_back = gathered.reshape(rows, block_len, channels)
    other_grad_back = swap_sequences(grad_back)
    grad_signal, left_term = call(
        row_backward_kernel,
        me,
        [left_factor, values, grad_back],
        [by_row, left],
        flops=2 * row_flops,
    )
    second_far[half // 2 :] = [after(x, left_term) for x in second_far[half // 2 :]]
    second_near, second_far = exchange(second_near, second_far)
    grad_left, grad_right = call(
        factor_sum_kernel,
        me,
        [left_term, other_values, other_grad_back, right_part, other_right],
        [left, right],
        flops=row_flops,
    )
    output, grad_gate = call(
        with_half(output_kernel), me, [gate, cotangent, second_near, *second_far], [whole, whole]
    )
    return (
        output.reshape(signal.shape),
        grad_gate.reshape(signal.shape),
        grad_signal.reshape(signal.shape),
        grad_left,
        grad_right,
    )


def plain_shards(signal, gating, upstream, left_factor, right_factor):
    seq = lax.axis_size("seq")
    rows, block_len = left_factor.shape[:2]
    cols, block_count = right_factor.shape[:2]
    channels = signal.shape[2]
    values = signal.reshape(rows, block_len, channels)
    gate = gating.reshape(rows, block_len, channels)
    cotangent = upstream.reshape(rows, block_len, channels)

    def einsum(spec, a, b):
        return jnp.einsum(spec, a, b, preferred_element_type=F32).astype(BF16)

    def all_to_all(blocks):
        return lax.all_to_all(blocks, "seq", split_axis=0, concat_axis=0, tiled=True)

    def to_columns(by_row):
        blocks = by_row.reshape(rows, seq, cols, channels).transpose(1, 0, 2, 3)
        return all_to_all(blocks).reshape(block_count, cols, channels)

    def to_rows(by_column):
        blocks = all_to_all(by_column.reshape(seq, rows, cols, channels))
        return blocks.transpose(1, 0, 2, 3).reshape(rows, block_len, channels)

    grad_rows = (cotangent.astype(F32) * gate.astype(F32)).astype(BF16)
    grad_column = to_columns(grad_rows)
    other_values = swap_sequences(values)
    mixed_column = to_columns(einsum("ikj,ijd->ikd", left_factor, values))
    grad_back = to_rows(einsum("kmi,mkd->ikd", right_factor, grad_column))
    second_rows = to_rows(einsum("kmi,ikd->mkd", right_factor, mixed_column))
    right_part = einsum("mkd,ikd->kmi", grad_column, mixed_column)
    other_right = swap_sequences(right_part)
    other_grad_back = swap_sequences(grad_back)
    grad_signal = einsum("ikj,ikd->ijd", left_factor, grad_back)
    left_term = einsum("ikd,ijd->ikj", grad_back, values)
    other_left = einsum("ikd,ijd->ikj", other_grad_back, other_values)
    grad_left = (left_term.astype(F32) + other_left.astype(F32)).astype(BF16)
    grad_right = (right_part.astype(F32) + other_right.astype(F32)).astype(BF16)
    wide = second_rows.astype(F32)
    output = (gate.astype(F32) * wide).astype(BF16)
    grad_gate = (cotangent.astype(F32) * wide).astype(BF16)
    return (
        output.reshape(signal.shape),
        grad_gate.reshape(signal.shape),
        grad_signal.reshape(signal.shape),
        grad_left,
        grad_right,
    )


def shards(signal, gating, upstream, left_factor, right_factor):
    seq = lax.axis_size("seq")
    cols = right_factor.shape[0]
    direct = seq <= 16 and seq & (seq - 1) == 0 and cols % 32 == 0
    run = direct_shards if direct else plain_shards
    return run(signal, gating, upstream, left_factor, right_factor)


def solution(mesh):
    by_position = P("dp", "seq", None)
    by_block = P("seq", None, None)
    return jax.shard_map(
        shards,
        mesh=mesh,
        in_specs=(by_position,) * 3 + (by_block,) * 2,
        out_specs=(by_position,) * 3 + (by_block,) * 2,
        check_vma=False,
    )
```

```python
import functools
import math

import jax
import jax.numpy as jnp
from jax import lax
from jax.experimental import pallas as pl
from jax.experimental.pallas import tpu as pltpu
from jax.sharding import PartitionSpec as P

BF16 = jnp.bfloat16
F32 = jnp.float32
MIB = 1024 * 1024


def swap_sequences(array):
    return lax.ppermute(array, "dp", [(0, 1), (1, 0)])


def after(array, earlier):
    return lax.optimization_barrier((array, earlier))[0]


def far_first(count):
    return sorted(range(1, count), key=lambda t: -(t // (count // 2)))


def step(messages, stride):
    seq = lax.axis_size("seq")
    received = list(messages)
    for t in far_first(len(messages)):
        pairs = [(i, i ^ (t * stride)) for i in range(seq)]
        received[t] = lax.ppermute(messages[t], "seq", pairs)
    return received


def call(kernel, me, inputs, out_shapes, scratch=(), flops=0, unblocked=(), vmem=32):
    whole = pl.BlockSpec(memory_space=pltpu.VMEM)
    moved = sum(x.size * x.dtype.itemsize for x in (*inputs, *out_shapes))
    in_specs = [
        pl.BlockSpec(memory_space=pl.ANY) if n in unblocked else whole for n in range(len(inputs))
    ]
    return pl.pallas_call(
        kernel,
        out_shape=out_shapes,
        in_specs=[pl.BlockSpec(memory_space=pltpu.SMEM)] + in_specs,
        out_specs=[whole] * len(out_shapes),
        scratch_shapes=scratch,
        compiler_params=pltpu.CompilerParams(vmem_limit_bytes=vmem * MIB),
        name=getattr(kernel, "func", kernel).__name__,
        cost_estimate=pl.CostEstimate(flops=flops, bytes_accessed=moved, transcendentals=0),
    )(me, *inputs)


def dot(a, b, contract):
    return lax.dot_general(a, b, (contract, ((), ())), preferred_element_type=F32)


def by_outer(outer, inner, me, refs):
    return [(me ^ (t * inner + r), refs[t].at[r]) for t in range(outer) for r in range(inner)]


def by_inner(outer, inner, me, refs):
    return [(me ^ (t * inner + r), refs[r].at[t]) for t in range(outer) for r in range(inner)]


def product_kernel(outer, inner, me_ref, gate_hbm, cotangent_hbm, *refs):
    out_refs, (gate, cotangent, sems) = refs[:outer], refs[outer:]
    rows = gate.shape[0]
    loads = [
        [
            pltpu.make_async_copy(source.at[i], target.at[i], sems.at[n, i])
            for n, (source, target) in enumerate(((gate_hbm, gate), (cotangent_hbm, cotangent)))
        ]
        for i in range(rows)
    ]
    for pair in loads:
        for load in pair:
            load.start()
    blocks = by_outer(outer, inner, me_ref[0], out_refs)
    for i in range(rows):
        for load in loads[i]:
            load.wait()
        for c, ref in blocks:
            ref[i] = (gate[i, c].astype(F32) * cotangent[i, c].astype(F32)).astype(BF16)


def mix_kernel(outer, inner, me_ref, left_ref, values_ref, *refs):
    out_refs, hold = refs[:outer], refs[outer]
    rows, seq, cols, channels = hold.shape
    for i in range(rows):
        mixed = dot(left_ref[i], values_ref[i], ((1,), (0,)))
        hold[i] = mixed.astype(BF16).reshape(seq, cols, channels)
    for c, ref in by_outer(outer, inner, me_ref[0], out_refs):
        ref[...] = hold[:, c]


def turn_kernel(count, me_ref, *refs):
    in_refs, out_refs = refs[:count], refs[count:]
    for t, in_ref in enumerate(in_refs):
        for r, out_ref in enumerate(out_refs):
            out_ref[t] = in_ref[r]


def load_columns(blocks, wide):
    rows, cols, channels = blocks[0][1].shape
    size = rows * cols
    for c, ref in blocks:
        block = ref[...].reshape(size, channels).astype(F32)
        start = pl.multiple_of(c * size, size)
        for h in range(channels // 128):
            wide[h, pl.ds(start, size), :] = block[:, h * 128 : (h + 1) * 128]


def column(wide, k, count, cols):
    halves = [wide[h, pl.ds(k, count, stride=cols), :] for h in range(wide.shape[0])]
    return jnp.concatenate(halves, axis=1).astype(BF16)


def store_column(wide, k, count, cols, value):
    for h in range(wide.shape[0]):
        wide[h, pl.ds(k, count, stride=cols), :] = value[:, h * 128 : (h + 1) * 128]


def send_columns(wide, blocks):
    rows, cols, channels = blocks[0][1].shape
    size = rows * cols
    for c, ref in blocks:
        start = pl.multiple_of(c * size, size)
        halves = [wide[h, pl.ds(start, size), :] for h in range(wide.shape[0])]
        block = jnp.concatenate(halves, axis=1).astype(BF16)
        ref[...] = block.reshape(rows, cols, channels)


def column_backward_kernel(outer, inner, me_ref, right_ref, *refs):
    in_refs, out_refs = refs[:inner], refs[inner : 2 * inner]
    by_column_ref, wide, wide_out = refs[2 * inner :]
    cols, count, _ = right_ref.shape
    me = me_ref[0]
    load_columns(by_inner(outer, inner, me, in_refs), wide)
    for k in range(cols):
        grad = column(wide, k, count, cols)
        by_column_ref[k] = grad
        store_column(wide_out, k, count, cols, dot(right_ref[k], grad, ((0,), (0,))))
    send_columns(wide_out, by_inner(outer, inner, me, out_refs))


def column_forward_kernel(outer, inner, me_ref, right_ref, grad_ref, after_ref, *refs):
    in_refs, out_refs = refs[:inner], refs[inner : 2 * inner]
    right_part_ref, wide, wide_out = refs[2 * inner :]
    cols, count, _ = right_ref.shape
    me = me_ref[0]
    load_columns(by_inner(outer, inner, me, in_refs), wide)
    for k in range(cols):
        mixed = column(wide, k, count, cols)
        store_column(wide_out, k, count, cols, dot(right_ref[k], mixed, ((1,), (0,))))
        right_part_ref[k] = dot(grad_ref[k], mixed, ((1,), (1,))).astype(BF16)
    send_columns(wide_out, by_inner(outer, inner, me, out_refs))


def gather_kernel(outer, inner, me_ref, *refs):
    for c, ref in by_outer(outer, inner, me_ref[0], refs[:outer]):
        refs[outer][:, c] = ref[...]


def row_backward_kernel(me_ref, left_ref, values_ref, grad_ref, signal_ref, term_ref):
    for i in range(left_ref.shape[0]):
        grad = grad_ref[i]
        signal_ref[i] = dot(left_ref[i], grad, ((0,), (0,))).astype(BF16)
        term_ref[i] = dot(grad, values_ref[i], ((1,), (1,))).astype(BF16)


def factor_sum_kernel(
    me_ref, term_ref, values_ref, grad_ref, right_ref, other_ref, left_out_ref, right_out_ref
):
    for i in range(term_ref.shape[0]):
        other = dot(grad_ref[i], values_ref[i], ((1,), (1,))).astype(BF16)
        left_out_ref[i] = (term_ref[i].astype(F32) + other.astype(F32)).astype(BF16)
    right_out_ref[...] = (right_ref[...].astype(F32) + other_ref[...].astype(F32)).astype(BF16)


def output_kernel(outer, inner, me_ref, gate_ref, cotangent_ref, *refs):
    out_ref, grad_ref = refs[outer:]
    for c, ref in by_outer(outer, inner, me_ref[0], refs[:outer]):
        second = ref[...].astype(F32)
        out_ref[:, c] = (gate_ref[:, c].astype(F32) * second).astype(BF16)
        grad_ref[:, c] = (cotangent_ref[:, c].astype(F32) * second).astype(BF16)


def direct_shards(signal, gating, upstream, left_factor, right_factor):
    seq = lax.axis_size("seq")
    side = math.isqrt(seq)
    rows, block_len = left_factor.shape[:2]
    cols, count = right_factor.shape[:2]
    channels = signal.shape[2]
    me = lax.axis_index("seq").astype(jnp.int32).reshape(1)
    values = signal.reshape(rows, block_len, channels)
    gate = gating.reshape(rows, seq, cols, channels)
    cotangent = upstream.reshape(rows, seq, cols, channels)

    def shape(*dims):
        return jax.ShapeDtypeStruct(dims, BF16)

    def grouped(kernel):
        return functools.partial(kernel, side, side)

    messages = [shape(side, rows, cols, channels)] * side
    whole = shape(rows, seq, cols, channels)
    by_row = shape(rows, block_len, channels)
    left = shape(*left_factor.shape)
    right = shape(*right_factor.shape)
    wide = pltpu.VMEM((channels // 128, count * cols, 128), F32)
    row_flops = 2 * rows * block_len * block_len * channels
    column_flops = 2 * cols * count * count * channels

    def turn(received):
        return call(functools.partial(turn_kernel, side), me, received, messages)

    grad_rows = call(
        grouped(product_kernel),
        me,
        [gate, cotangent],
        messages,
        [pltpu.VMEM(whole.shape, BF16)] * 2 + [pltpu.SemaphoreType.DMA((2, rows))],
        unblocked=range(2),
        vmem=60,
    )
    mixed_rows = call(
        grouped(mix_kernel),
        me,
        [left_factor, values],
        messages,
        [pltpu.VMEM(whole.shape, BF16)],
        row_flops,
    )
    grad_received = step(grad_rows, side)
    grad_received[0] = after(grad_received[0], mixed_rows[0])
    mixed_received = step(mixed_rows, side)
    grad_columns = step(turn(grad_received), 1)
    other_values = swap_sequences(after(values, grad_rows[0]))
    *grad_second, grad_column = call(
        grouped(column_backward_kernel),
        me,
        [right_factor, *grad_columns],
        messages + [shape(cols, count, channels)],
        [wide, wide],
        column_flops,
    )
    mixed_columns = step(turn(mixed_received), 1)
    back_received = step(grad_second, 1)
    back_received[0] = after(back_received[0], mixed_received[-1])
    back_turned = list(turn(back_received))
    *second, right_part = call(
        grouped(column_forward_kernel),
        me,
        [right_factor, grad_column, other_values, *mixed_columns],
        messages + [right],
        [wide, wide],
        2 * column_flops,
        unblocked=[2],
    )
    back_turned[1] = after(back_turned[1], right_part)
    back_blocks = step(back_turned, side)
    other_right = swap_sequences(right_part)
    second_turned = list(turn(step(second, 1)))
    back_blocks[0] = after(back_blocks[0], second_turned[0])
    (gathered,) = call(grouped(gather_kernel), me, back_blocks, [whole])
    grad_back = gathered.reshape(rows, block_len, channels)
    other_grad_back = swap_sequences(grad_back)
    grad_signal, left_term = call(
        row_backward_kernel,
        me,
        [left_factor, values, grad_back],
        [by_row, left],
        flops=2 * row_flops,
    )
    second_turned[1] = after(second_turned[1], left_term)
    second_blocks = step(second_turned, side)
    grad_left, grad_right = call(
        factor_sum_kernel,
        me,
        [left_term, other_values, other_grad_back, right_part, other_right],
        [left, right],
        flops=row_flops,
    )
    output, grad_gate = call(
        grouped(output_kernel), me, [gate, cotangent, *second_blocks], [whole, whole]
    )
    return (
        output.reshape(signal.shape),
        grad_gate.reshape(signal.shape),
        grad_signal.reshape(signal.shape),
        grad_left,
        grad_right,
    )


def plain_shards(signal, gating, upstream, left_factor, right_factor):
    seq = lax.axis_size("seq")
    rows, block_len = left_factor.shape[:2]
    cols, block_count = right_factor.shape[:2]
    channels = signal.shape[2]
    values = signal.reshape(rows, block_len, channels)
    gate = gating.reshape(rows, block_len, channels)
    cotangent = upstream.reshape(rows, block_len, channels)

    def einsum(spec, a, b):
        return jnp.einsum(spec, a, b, preferred_element_type=F32).astype(BF16)

    def all_to_all(blocks):
        return lax.all_to_all(blocks, "seq", split_axis=0, concat_axis=0, tiled=True)

    def to_columns(by_row):
        blocks = by_row.reshape(rows, seq, cols, channels).transpose(1, 0, 2, 3)
        return all_to_all(blocks).reshape(block_count, cols, channels)

    def to_rows(by_column):
        blocks = all_to_all(by_column.reshape(seq, rows, cols, channels))
        return blocks.transpose(1, 0, 2, 3).reshape(rows, block_len, channels)

    grad_rows = (cotangent.astype(F32) * gate.astype(F32)).astype(BF16)
    grad_column = to_columns(grad_rows)
    other_values = swap_sequences(values)
    mixed_column = to_columns(einsum("ikj,ijd->ikd", left_factor, values))
    grad_back = to_rows(einsum("kmi,mkd->ikd", right_factor, grad_column))
    second_rows = to_rows(einsum("kmi,ikd->mkd", right_factor, mixed_column))
    right_part = einsum("mkd,ikd->kmi", grad_column, mixed_column)
    other_right = swap_sequences(right_part)
    other_grad_back = swap_sequences(grad_back)
    grad_signal = einsum("ikj,ikd->ijd", left_factor, grad_back)
    left_term = einsum("ikd,ijd->ikj", grad_back, values)
    other_left = einsum("ikd,ijd->ikj", other_grad_back, other_values)
    grad_left = (left_term.astype(F32) + other_left.astype(F32)).astype(BF16)
    grad_right = (right_part.astype(F32) + other_right.astype(F32)).astype(BF16)
    wide = second_rows.astype(F32)
    output = (gate.astype(F32) * wide).astype(BF16)
    grad_gate = (cotangent.astype(F32) * wide).astype(BF16)
    return (
        output.reshape(signal.shape),
        grad_gate.reshape(signal.shape),
        grad_signal.reshape(signal.shape),
        grad_left,
        grad_right,
    )


def shards(signal, gating, upstream, left_factor, right_factor):
    seq = lax.axis_size("seq")
    cols = right_factor.shape[0]
    direct = seq in (4, 16) and cols % 32 == 0
    run = direct_shards if direct else plain_shards
    return run(signal, gating, upstream, left_factor, right_factor)


def solution(mesh):
    by_position = P("dp", "seq", None)
    by_block = P("seq", None, None)
    return jax.shard_map(
        shards,
        mesh=mesh,
        in_specs=(by_position,) * 3 + (by_block,) * 2,
        out_specs=(by_position,) * 3 + (by_block,) * 2,
        check_vma=False,
    )
```

```python
import functools

import jax
import jax.numpy as jnp
from jax import lax
from jax.experimental import pallas as pl
from jax.experimental.pallas import tpu as pltpu
from jax.sharding import PartitionSpec as P

BF16 = jnp.bfloat16
F32 = jnp.float32
MIB = 1024 * 1024


def swap_sequences(array):
    return lax.ppermute(array, "dp", [(0, 1), (1, 0)])


def after(array, earlier):
    return lax.optimization_barrier((array, earlier))[0]


def far_first(count):
    half = count // 2
    far = [t for pair in zip(range(half, half + half // 2), range(half + half // 2, count)) for t in pair]
    return far + list(range(half - 1, 0, -1))


def permute(array, offset):
    seq = lax.axis_size("seq")
    return lax.ppermute(array, "seq", [(i, i ^ offset) for i in range(seq)])


def exchange(messages):
    return [messages[0]] + [permute(message, 2 * t) for t, message in list(enumerate(messages))[1:]]


def listed(messages):
    return [messages[t] for t in [0] + far_first(len(messages))]


def call(kernel, me, inputs, out_shapes, scratch=(), flops=0, unblocked=(), vmem=32):
    whole = pl.BlockSpec(memory_space=pltpu.VMEM)
    moved = sum(x.size * x.dtype.itemsize for x in (*inputs, *out_shapes))
    in_specs = [
        pl.BlockSpec(memory_space=pl.ANY) if n in unblocked else whole for n in range(len(inputs))
    ]
    return pl.pallas_call(
        kernel,
        out_shape=out_shapes,
        in_specs=[pl.BlockSpec(memory_space=pltpu.SMEM)] + in_specs,
        out_specs=[whole] * len(out_shapes),
        scratch_shapes=scratch,
        compiler_params=pltpu.CompilerParams(vmem_limit_bytes=vmem * MIB),
        name=getattr(kernel, "func", kernel).__name__,
        cost_estimate=pl.CostEstimate(flops=flops, bytes_accessed=moved, transcendentals=0),
    )(me, *inputs)


def dot(a, b, contract):
    return lax.dot_general(a, b, (contract, ((), ())), preferred_element_type=F32)


def block_views(me, refs):
    return [(me ^ (2 * t + e), ref.at[t]) for e, ref in enumerate(refs) for t in range(ref.shape[0])]


def received_views(me, refs):
    order = [0] + far_first(len(refs))
    return [(me ^ (2 * t + e), ref.at[e]) for t, ref in zip(order, refs) for e in range(2)]


def send_kernel(me_ref, gate_hbm, cotangent_hbm, left_hbm, values_hbm, *refs):
    out_refs = refs[:2]
    gate, cotangent, left, values, hold, sems = refs[2:]
    rows, seq, cols, channels = hold.shape
    me = me_ref[0]
    loads = []
    for i in range(rows):
        for n, (source, target) in enumerate(((left_hbm, left), (values_hbm, values))):
            loads.append(pltpu.make_async_copy(source.at[i], target.at[i], sems.at[n, i]))
    loads.append(pltpu.make_async_copy(gate_hbm, gate, sems.at[2, 0]))
    loads.append(pltpu.make_async_copy(cotangent_hbm, cotangent, sems.at[2, 1]))
    for load in loads:
        load.start()
    for i in range(rows):
        loads[2 * i].wait()
        loads[2 * i + 1].wait()
        mixed = dot(left[i], values[i], ((1,), (0,)))
        hold[i] = mixed.astype(BF16).reshape(seq, cols, channels)
    loads[-2].wait()
    loads[-1].wait()
    for c, ref in block_views(me, out_refs):
        wide = gate[:, c].astype(F32) * cotangent[:, c].astype(F32)
        ref[0] = wide.astype(BF16)
        ref[1] = hold[:, c]


def pack_kernel(me_ref, own_ref, other_ref, *out_refs):
    for t, out_ref in enumerate(out_refs):
        out_ref[0] = own_ref[t]
        out_ref[1] = other_ref[t]


def load_columns(blocks, wide):
    rows, cols, channels = blocks[0][1].shape
    size = rows * cols
    for c, ref in blocks:
        block = ref[...].reshape(size, channels).astype(F32)
        start = pl.multiple_of(c * size, size)
        for h in range(channels // 128):
            wide[h, pl.ds(start, size), :] = block[:, h * 128 : (h + 1) * 128]


def column(wide, k, count, cols):
    halves = [wide[h, pl.ds(k, count, stride=cols), :] for h in range(wide.shape[0])]
    return jnp.concatenate(halves, axis=1).astype(BF16)


def store_column(wide, k, count, cols, value):
    for h in range(wide.shape[0]):
        wide[h, pl.ds(k, count, stride=cols), :] = value[:, h * 128 : (h + 1) * 128]


def send_columns(wide, blocks):
    rows, cols, channels = blocks[0][1].shape
    size = rows * cols
    for c, ref in blocks:
        start = pl.multiple_of(c * size, size)
        halves = [wide[h, pl.ds(start, size), :] for h in range(wide.shape[0])]
        block = jnp.concatenate(halves, axis=1).astype(BF16)
        ref[...] = block.reshape(rows, cols, channels)


def column_backward_kernel(chips, me_ref, right_ref, *refs):
    in_refs, out_refs = refs[:chips], refs[chips : chips + 2]
    by_column_ref, wide, wide_out = refs[chips + 2 :]
    cols, count, _ = right_ref.shape
    me = me_ref[0]
    load_columns([(c, ref.at[0]) for c, ref in received_views(me, in_refs)], wide)
    for k in range(cols):
        grad = column(wide, k, count, cols)
        by_column_ref[k] = grad
        store_column(wide_out, k, count, cols, dot(right_ref[k], grad, ((0,), (0,))))
    send_columns(wide_out, block_views(me, out_refs))


def column_forward_kernel(chips, me_ref, right_ref, grad_ref, after_ref, *refs):
    in_refs, out_refs = refs[:chips], refs[chips : chips + 2]
    right_part_ref, wide, wide_out = refs[chips + 2 :]
    cols, count, _ = right_ref.shape
    me = me_ref[0]
    load_columns([(c, ref.at[1]) for c, ref in received_views(me, in_refs)], wide)
    for k in range(cols):
        mixed = column(wide, k, count, cols)
        store_column(wide_out, k, count, cols, dot(right_ref[k], mixed, ((1,), (0,))))
        right_part_ref[k] = dot(grad_ref[k], mixed, ((1,), (1,))).astype(BF16)
    send_columns(wide_out, block_views(me, out_refs))


def gather_kernel(chips, me_ref, *refs):
    for c, ref in received_views(me_ref[0], refs[:chips]):
        refs[chips][:, c] = ref[...]


def row_backward_kernel(me_ref, left_ref, values_ref, grad_ref, signal_ref, term_ref):
    for i in range(left_ref.shape[0]):
        grad = grad_ref[i]
        signal_ref[i] = dot(left_ref[i], grad, ((0,), (0,))).astype(BF16)
        term_ref[i] = dot(grad, values_ref[i], ((1,), (1,))).astype(BF16)


def factor_sum_kernel(
    me_ref, term_ref, values_ref, grad_ref, right_ref, other_ref, left_out_ref, right_out_ref
):
    for i in range(term_ref.shape[0]):
        other = dot(grad_ref[i], values_ref[i], ((1,), (1,))).astype(BF16)
        left_out_ref[i] = (term_ref[i].astype(F32) + other.astype(F32)).astype(BF16)
    right_out_ref[...] = (right_ref[...].astype(F32) + other_ref[...].astype(F32)).astype(BF16)


def output_kernel(chips, me_ref, gate_ref, cotangent_ref, *refs):
    out_ref, grad_ref = refs[chips:]
    for c, ref in received_views(me_ref[0], refs[:chips]):
        second = ref[...].astype(F32)
        out_ref[:, c] = (gate_ref[:, c].astype(F32) * second).astype(BF16)
        grad_ref[:, c] = (cotangent_ref[:, c].astype(F32) * second).astype(BF16)


def direct_shards(signal, gating, upstream, left_factor, right_factor):
    seq = lax.axis_size("seq")
    chips = seq // 2
    rows, block_len = left_factor.shape[:2]
    cols, count = right_factor.shape[:2]
    channels = signal.shape[2]
    me = lax.axis_index("seq").astype(jnp.int32).reshape(1)
    values = signal.reshape(rows, block_len, channels)
    gate = gating.reshape(rows, seq, cols, channels)
    cotangent = upstream.reshape(rows, seq, cols, channels)

    def shape(*dims):
        return jax.ShapeDtypeStruct(dims, BF16)

    def on_chips(kernel):
        return functools.partial(kernel, chips)

    block = (rows, cols, channels)
    whole = shape(rows, seq, cols, channels)
    by_row = shape(rows, block_len, channels)
    left = shape(*left_factor.shape)
    right = shape(*right_factor.shape)
    wide = pltpu.VMEM((channels // 128, count * cols, 128), F32)
    row_flops = 2 * rows * block_len * block_len * channels
    column_flops = 2 * cols * count * count * channels

    def pack(own, other):
        message = shape(2, *own.shape[1:])
        return list(call(pack_kernel, me, [own, permute(other, 1)], [message] * chips))

    own, other = call(
        send_kernel,
        me,
        [gate, cotangent, left_factor, values],
        [shape(chips, 2, *block)] * 2,
        [pltpu.VMEM(x.shape, BF16) for x in (gate, cotangent, left_factor, values, whole)]
        + [pltpu.SemaphoreType.DMA((3, max(rows, 2)))],
        row_flops,
        unblocked=range(4),
        vmem=60,
    )
    messages = pack(own, other)
    other_values = swap_sequences(after(values, messages[0]))
    columns = listed(exchange(messages))
    own, other, grad_column = call(
        on_chips(column_backward_kernel),
        me,
        [right_factor, *columns],
        [shape(chips, *block)] * 2 + [shape(cols, count, channels)],
        [wide, wide],
        column_flops,
    )
    messages = pack(own, other)
    own, other, right_part = call(
        on_chips(column_forward_kernel),
        me,
        [right_factor, grad_column, other_values, *columns],
        [shape(chips, *block)] * 2 + [right],
        [wide, wide],
        2 * column_flops,
        unblocked=[2],
    )
    second_messages = pack(own, other)
    for t in range(1, chips // 2):
        messages[t] = after(messages[t], second_messages[0])
    back = listed(exchange(messages))
    other_right = swap_sequences(right_part)
    back[0] = after(back[0], other_right)
    (gathered,) = call(on_chips(gather_kernel), me, back, [whole])
    grad_back = gathered.reshape(rows, block_len, channels)
    other_grad_back = swap_sequences(grad_back)
    grad_signal, left_term = call(
        row_backward_kernel,
        me,
        [left_factor, values, grad_back],
        [by_row, left],
        flops=2 * row_flops,
    )
    for t in range(1, chips // 2):
        second_messages[t] = after(second_messages[t], left_term)
    second = listed(exchange(second_messages))
    grad_left, grad_right = call(
        factor_sum_kernel,
        me,
        [left_term, other_values, other_grad_back, right_part, other_right],
        [left, right],
        flops=row_flops,
    )
    output, grad_gate = call(
        on_chips(output_kernel), me, [gate, cotangent, *second], [whole, whole]
    )
    return (
        output.reshape(signal.shape),
        grad_gate.reshape(signal.shape),
        grad_signal.reshape(signal.shape),
        grad_left,
        grad_right,
    )


def plain_shards(signal, gating, upstream, left_factor, right_factor):
    seq = lax.axis_size("seq")
    rows, block_len = left_factor.shape[:2]
    cols, block_count = right_factor.shape[:2]
    channels = signal.shape[2]
    values = signal.reshape(rows, block_len, channels)
    gate = gating.reshape(rows, block_len, channels)
    cotangent = upstream.reshape(rows, block_len, channels)

    def einsum(spec, a, b):
        return jnp.einsum(spec, a, b, preferred_element_type=F32).astype(BF16)

    def all_to_all(blocks):
        return lax.all_to_all(blocks, "seq", split_axis=0, concat_axis=0, tiled=True)

    def to_columns(by_row):
        blocks = by_row.reshape(rows, seq, cols, channels).transpose(1, 0, 2, 3)
        return all_to_all(blocks).reshape(block_count, cols, channels)

    def to_rows(by_column):
        blocks = all_to_all(by_column.reshape(seq, rows, cols, channels))
        return blocks.transpose(1, 0, 2, 3).reshape(rows, block_len, channels)

    grad_rows = (cotangent.astype(F32) * gate.astype(F32)).astype(BF16)
    grad_column = to_columns(grad_rows)
    other_values = swap_sequences(values)
    mixed_column = to_columns(einsum("ikj,ijd->ikd", left_factor, values))
    grad_back = to_rows(einsum("kmi,mkd->ikd", right_factor, grad_column))
    second_rows = to_rows(einsum("kmi,ikd->mkd", right_factor, mixed_column))
    right_part = einsum("mkd,ikd->kmi", grad_column, mixed_column)
    other_right = swap_sequences(right_part)
    other_grad_back = swap_sequences(grad_back)
    grad_signal = einsum("ikj,ikd->ijd", left_factor, grad_back)
    left_term = einsum("ikd,ijd->ikj", grad_back, values)
    other_left = einsum("ikd,ijd->ikj", other_grad_back, other_values)
    grad_left = (left_term.astype(F32) + other_left.astype(F32)).astype(BF16)
    grad_right = (right_part.astype(F32) + other_right.astype(F32)).astype(BF16)
    wide = second_rows.astype(F32)
    output = (gate.astype(F32) * wide).astype(BF16)
    grad_gate = (cotangent.astype(F32) * wide).astype(BF16)
    return (
        output.reshape(signal.shape),
        grad_gate.reshape(signal.shape),
        grad_signal.reshape(signal.shape),
        grad_left,
        grad_right,
    )


def shards(signal, gating, upstream, left_factor, right_factor):
    seq = lax.axis_size("seq")
    cols = right_factor.shape[0]
    direct = seq in (8, 16) and cols % 32 == 0
    run = direct_shards if direct else plain_shards
    return run(signal, gating, upstream, left_factor, right_factor)


def solution(mesh):
    by_position = P("dp", "seq", None)
    by_block = P("seq", None, None)
    return jax.shard_map(
        shards,
        mesh=mesh,
        in_specs=(by_position,) * 3 + (by_block,) * 2,
        out_specs=(by_position,) * 3 + (by_block,) * 2,
        check_vma=False,
    )
```

```python
import functools

import jax
import jax.numpy as jnp
from jax import lax
from jax.experimental import pallas as pl
from jax.experimental.pallas import tpu as pltpu
from jax.sharding import PartitionSpec as P

BF16 = jnp.bfloat16
F32 = jnp.float32
MIB = 1024 * 1024


def swap_sequences(array):
    return lax.ppermute(array, "dp", [(0, 1), (1, 0)])


def after(array, earlier):
    return lax.optimization_barrier((array, earlier))[0]


def partner_order(chips):
    half = chips // 2
    far = list(range(half, chips, 2)) + list(range(half + 1, chips, 2))
    return far[:-1] + list(range(1, half)) + far[-1:]


def permute(array, offset):
    seq = lax.axis_size("seq")
    return lax.ppermute(array, "seq", [(i, i ^ offset) for i in range(seq)])


def exchange(messages, sent=0, received=None):
    result = [permute(message, 2 * t) if t else message for t, message in enumerate(messages)]
    if received is not None:
        result[sent] = received
    return result


def listed(messages):
    return [messages[t] for t in [0] + partner_order(len(messages))]


def call(kernel, me, inputs, out_shapes, scratch=(), flops=0, unblocked=(), vmem=32):
    whole = pl.BlockSpec(memory_space=pltpu.VMEM)
    moved = sum(x.size * x.dtype.itemsize for x in (*inputs, *out_shapes))
    in_specs = [
        pl.BlockSpec(memory_space=pl.ANY) if n in unblocked else whole for n in range(len(inputs))
    ]
    return pl.pallas_call(
        kernel,
        out_shape=out_shapes,
        in_specs=[pl.BlockSpec(memory_space=pltpu.SMEM)] + in_specs,
        out_specs=[whole] * len(out_shapes),
        scratch_shapes=scratch,
        compiler_params=pltpu.CompilerParams(vmem_limit_bytes=vmem * MIB),
        name=getattr(kernel, "func", kernel).__name__,
        cost_estimate=pl.CostEstimate(flops=flops, bytes_accessed=moved, transcendentals=0),
    )(me, *inputs)


def dot(a, b, contract):
    return lax.dot_general(a, b, (contract, ((), ())), preferred_element_type=F32)


def block_views(me, refs):
    return [(me ^ (2 * t + e), ref.at[t]) for e, ref in enumerate(refs) for t in range(ref.shape[0])]


def received_views(me, refs):
    order = [0] + partner_order(len(refs))
    return [(me ^ (2 * t + e), ref.at[e]) for t, ref in zip(order, refs) for e in range(2)]


def product_kernel(me_ref, gate_hbm, cotangent_hbm, *refs):
    out_refs, (gate, cotangent, sems) = refs[:2], refs[2:]
    rows = gate.shape[0]
    loads = [
        [
            pltpu.make_async_copy(source.at[i], target.at[i], sems.at[n, i])
            for n, (source, target) in enumerate(((gate_hbm, gate), (cotangent_hbm, cotangent)))
        ]
        for i in range(rows)
    ]
    for pair in loads:
        for load in pair:
            load.start()
    blocks = block_views(me_ref[0], out_refs)
    for i in range(rows):
        for load in loads[i]:
            load.wait()
        for c, ref in blocks:
            ref[i] = (gate[i, c].astype(F32) * cotangent[i, c].astype(F32)).astype(BF16)


def mix_kernel(me_ref, left_ref, values_ref, *refs):
    out_refs, hold = refs[:2], refs[2]
    rows, seq, cols, channels = hold.shape
    for i in range(rows):
        mixed = dot(left_ref[i], values_ref[i], ((1,), (0,)))
        hold[i] = mixed.astype(BF16).reshape(seq, cols, channels)
    for c, ref in block_views(me_ref[0], out_refs):
        ref[...] = hold[:, c]


def pack_kernel(me_ref, own_ref, other_ref, *out_refs):
    for t, out_ref in enumerate(out_refs):
        out_ref[0] = own_ref[t]
        out_ref[1] = other_ref[t]


def load_columns(blocks, wide):
    rows, cols, channels = blocks[0][1].shape
    size = rows * cols
    for c, ref in blocks:
        block = ref[...].reshape(size, channels).astype(F32)
        start = pl.multiple_of(c * size, size)
        for h in range(channels // 128):
            wide[h, pl.ds(start, size), :] = block[:, h * 128 : (h + 1) * 128]


def column(wide, k, count, cols):
    halves = [wide[h, pl.ds(k, count, stride=cols), :] for h in range(wide.shape[0])]
    return jnp.concatenate(halves, axis=1).astype(BF16)


def store_column(wide, k, count, cols, value):
    for h in range(wide.shape[0]):
        wide[h, pl.ds(k, count, stride=cols), :] = value[:, h * 128 : (h + 1) * 128]


def send_columns(wide, blocks):
    rows, cols, channels = blocks[0][1].shape
    size = rows * cols
    for c, ref in blocks:
        start = pl.multiple_of(c * size, size)
        halves = [wide[h, pl.ds(start, size), :] for h in range(wide.shape[0])]
        block = jnp.concatenate(halves, axis=1).astype(BF16)
        ref[...] = block.reshape(rows, cols, channels)


def column_backward_kernel(chips, me_ref, right_ref, *refs):
    in_refs, out_refs = refs[:chips], refs[chips : chips + 2]
    by_column_ref, wide, wide_out = refs[chips + 2 :]
    cols, count, _ = right_ref.shape
    me = me_ref[0]
    load_columns(received_views(me, in_refs), wide)
    for k in range(cols):
        grad = column(wide, k, count, cols)
        by_column_ref[k] = grad
        store_column(wide_out, k, count, cols, dot(right_ref[k], grad, ((0,), (0,))))
    send_columns(wide_out, block_views(me, out_refs))


def column_forward_kernel(chips, me_ref, right_ref, grad_ref, after_ref, *refs):
    in_refs, out_refs = refs[:chips], refs[chips : chips + 2]
    right_part_ref, wide, wide_out = refs[chips + 2 :]
    cols, count, _ = right_ref.shape
    me = me_ref[0]
    load_columns(received_views(me, in_refs), wide)
    for k in range(cols):
        mixed = column(wide, k, count, cols)
        store_column(wide_out, k, count, cols, dot(right_ref[k], mixed, ((1,), (0,))))
        right_part_ref[k] = dot(grad_ref[k], mixed, ((1,), (1,))).astype(BF16)
    send_columns(wide_out, block_views(me, out_refs))


def gather_kernel(me_ref, *refs):
    out_ref = refs[-1]
    for t, ref in enumerate(refs[:-1]):
        for e in range(2):
            out_ref[2 * t + e] = ref[e]


def load_rows(me, parts, hold):
    half = parts[0].shape[0]
    order = [0] + partner_order(half)
    for n, t in enumerate(order):
        for e in range(2):
            j = 2 * n + e
            hold[:, me ^ (2 * t + e)] = parts[j // half][j % half]


def row_of(hold, i):
    seq, cols, channels = hold.shape[1:]
    return hold[i].reshape(seq * cols, channels)


def row_backward_kernel(
    me_ref, left_ref, values_ref, first_ref, second_ref, signal_ref, term_ref, hold
):
    load_rows(me_ref[0], (first_ref, second_ref), hold)
    for i in range(left_ref.shape[0]):
        grad = row_of(hold, i)
        signal_ref[i] = dot(left_ref[i], grad, ((0,), (0,))).astype(BF16)
        term_ref[i] = dot(grad, values_ref[i], ((1,), (1,))).astype(BF16)


def factor_sum_kernel(
    me_ref,
    term_ref,
    values_ref,
    first_ref,
    second_ref,
    right_ref,
    other_ref,
    left_out_ref,
    right_out_ref,
    hold,
):
    right_out_ref[...] = (right_ref[...].astype(F32) + other_ref[...].astype(F32)).astype(BF16)
    load_rows(me_ref[0], (first_ref, second_ref), hold)
    for i in range(term_ref.shape[0]):
        other = dot(row_of(hold, i), values_ref[i], ((1,), (1,))).astype(BF16)
        left_out_ref[i] = (term_ref[i].astype(F32) + other.astype(F32)).astype(BF16)


def output_kernel(chips, me_ref, gate_ref, cotangent_ref, *refs):
    out_ref, grad_ref = refs[chips:]
    for c, ref in received_views(me_ref[0], refs[:chips]):
        second = ref[...].astype(F32)
        out_ref[:, c] = (gate_ref[:, c].astype(F32) * second).astype(BF16)
        grad_ref[:, c] = (cotangent_ref[:, c].astype(F32) * second).astype(BF16)


def direct_shards(signal, gating, upstream, left_factor, right_factor):
    seq = lax.axis_size("seq")
    chips = seq // 2
    rows, block_len = left_factor.shape[:2]
    cols, count = right_factor.shape[:2]
    channels = signal.shape[2]
    me = lax.axis_index("seq").astype(jnp.int32).reshape(1)
    values = signal.reshape(rows, block_len, channels)
    gate = gating.reshape(rows, seq, cols, channels)
    cotangent = upstream.reshape(rows, seq, cols, channels)

    def shape(*dims):
        return jax.ShapeDtypeStruct(dims, BF16)

    def on_chips(kernel):
        return functools.partial(kernel, chips)

    block = (rows, cols, channels)
    whole = shape(rows, seq, cols, channels)
    by_row = shape(rows, block_len, channels)
    left = shape(*left_factor.shape)
    right = shape(*right_factor.shape)
    wide = pltpu.VMEM((channels // 128, count * cols, 128), F32)
    row_flops = 2 * rows * block_len * block_len * channels
    column_flops = 2 * cols * count * count * channels

    def pack(own, other):
        message = shape(2, *own.shape[1:])
        return list(call(pack_kernel, me, [own, permute(other, 1)], [message] * chips))

    def pin(messages, t, earlier):
        messages[t] = after(messages[t], earlier)

    last, early = chips - 1, chips // 2
    halves = [shape(chips, *block)] * 2
    hold = pltpu.VMEM(whole.shape, BF16)

    grad_rows = call(
        product_kernel,
        me,
        [gate, cotangent],
        halves,
        [hold, hold, pltpu.SemaphoreType.DMA((2, rows))],
        unblocked=range(2),
        vmem=60,
    )
    out_grad = pack(*grad_rows)
    other_values = swap_sequences(after(values, out_grad[0]))
    mixed_rows = call(
        mix_kernel, me, [left_factor, after(values, out_grad[0])], halves, [hold], row_flops
    )
    out_mixed = pack(*mixed_rows)
    pin(out_grad, last, out_mixed[0])
    grad_columns = exchange(out_grad)
    first_mixed = permute(out_mixed[early], 2 * early)
    pin(grad_columns, 0, first_mixed)
    *grad_second, grad_column = call(
        on_chips(column_backward_kernel),
        me,
        [right_factor, *listed(grad_columns)],
        halves + [shape(cols, count, channels)],
        [wide, wide],
        column_flops,
    )
    back = pack(*grad_second)
    pin(out_mixed, last, back[0])
    mixed_columns = exchange(out_mixed, early, first_mixed)
    first_back = permute(back[early], 2 * early)
    pin(mixed_columns, 0, first_back)
    *second, right_part = call(
        on_chips(column_forward_kernel),
        me,
        [right_factor, grad_column, other_values, *listed(mixed_columns)],
        halves + [right],
        [wide, wide],
        2 * column_flops,
        unblocked=[2],
    )
    second = pack(*second)
    pin(back, last, second[0])
    other_right = swap_sequences(right_part)
    back = exchange(back, early, first_back)
    first_second = permute(second[early], 2 * early)
    pin(back, last, (first_second, other_right))
    back = listed(back)
    half_rows = shape(seq // 2, *block)
    (first_half,) = call(gather_kernel, me, back[:early], [half_rows])
    (second_half,) = call(gather_kernel, me, back[early:], [half_rows])
    other_first = swap_sequences(first_half)
    other_second = swap_sequences(second_half)
    grad_signal, left_term = call(
        row_backward_kernel,
        me,
        [left_factor, values, first_half, second_half],
        [by_row, left],
        [hold],
        2 * row_flops,
    )
    pin(second, last, left_term)
    second = listed(exchange(second, early, first_second))
    grad_left, grad_right = call(
        factor_sum_kernel,
        me,
        [left_term, other_values, other_first, other_second, right_part, other_right],
        [left, right],
        [hold],
        row_flops,
    )
    output, grad_gate = call(
        on_chips(output_kernel), me, [gate, cotangent, *second], [whole, whole]
    )
    return (
        output.reshape(signal.shape),
        grad_gate.reshape(signal.shape),
        grad_signal.reshape(signal.shape),
        grad_left,
        grad_right,
    )


def plain_shards(signal, gating, upstream, left_factor, right_factor):
    seq = lax.axis_size("seq")
    rows, block_len = left_factor.shape[:2]
    cols, block_count = right_factor.shape[:2]
    channels = signal.shape[2]
    values = signal.reshape(rows, block_len, channels)
    gate = gating.reshape(rows, block_len, channels)
    cotangent = upstream.reshape(rows, block_len, channels)

    def einsum(spec, a, b):
        return jnp.einsum(spec, a, b, preferred_element_type=F32).astype(BF16)

    def all_to_all(blocks):
        return lax.all_to_all(blocks, "seq", split_axis=0, concat_axis=0, tiled=True)

    def to_columns(by_row):
        blocks = by_row.reshape(rows, seq, cols, channels).transpose(1, 0, 2, 3)
        return all_to_all(blocks).reshape(block_count, cols, channels)

    def to_rows(by_column):
        blocks = all_to_all(by_column.reshape(seq, rows, cols, channels))
        return blocks.transpose(1, 0, 2, 3).reshape(rows, block_len, channels)

    grad_rows = (cotangent.astype(F32) * gate.astype(F32)).astype(BF16)
    grad_column = to_columns(grad_rows)
    other_values = swap_sequences(values)
    mixed_column = to_columns(einsum("ikj,ijd->ikd", left_factor, values))
    grad_back = to_rows(einsum("kmi,mkd->ikd", right_factor, grad_column))
    second_rows = to_rows(einsum("kmi,ikd->mkd", right_factor, mixed_column))
    right_part = einsum("mkd,ikd->kmi", grad_column, mixed_column)
    other_right = swap_sequences(right_part)
    other_grad_back = swap_sequences(grad_back)
    grad_signal = einsum("ikj,ikd->ijd", left_factor, grad_back)
    left_term = einsum("ikd,ijd->ikj", grad_back, values)
    other_left = einsum("ikd,ijd->ikj", other_grad_back, other_values)
    grad_left = (left_term.astype(F32) + other_left.astype(F32)).astype(BF16)
    grad_right = (right_part.astype(F32) + other_right.astype(F32)).astype(BF16)
    wide = second_rows.astype(F32)
    output = (gate.astype(F32) * wide).astype(BF16)
    grad_gate = (cotangent.astype(F32) * wide).astype(BF16)
    return (
        output.reshape(signal.shape),
        grad_gate.reshape(signal.shape),
        grad_signal.reshape(signal.shape),
        grad_left,
        grad_right,
    )


def shards(signal, gating, upstream, left_factor, right_factor):
    seq = lax.axis_size("seq")
    cols = right_factor.shape[0]
    direct = seq in (8, 16) and cols % 32 == 0
    run = direct_shards if direct else plain_shards
    return run(signal, gating, upstream, left_factor, right_factor)


def solution(mesh):
    by_position = P("dp", "seq", None)
    by_block = P("seq", None, None)
    return jax.shard_map(
        shards,
        mesh=mesh,
        in_specs=(by_position,) * 3 + (by_block,) * 2,
        out_specs=(by_position,) * 3 + (by_block,) * 2,
        check_vma=False,
    )
```

```python
import jax
import jax.numpy as jnp
from jax import lax
from jax.experimental import pallas as pl
from jax.experimental.pallas import tpu as pltpu
from jax.sharding import PartitionSpec as P

BF16 = jnp.bfloat16
F32 = jnp.float32
MIB = 1024 * 1024


def swap_sequences(array):
    return lax.ppermute(array, "dp", [(0, 1), (1, 0)])


def exchange(blocks):
    return lax.all_to_all(blocks, "seq", split_axis=0, concat_axis=0, tiled=True)


def after(array, earlier):
    return lax.optimization_barrier((array, earlier))[0]


def call(kernel, inputs, out_shapes, scratch=(), flops=0, unblocked=(), vmem=48):
    whole = pl.BlockSpec(memory_space=pltpu.VMEM)
    moved = sum(x.size * x.dtype.itemsize for x in (*inputs, *out_shapes))
    return pl.pallas_call(
        kernel,
        out_shape=out_shapes,
        in_specs=[
            pl.BlockSpec(memory_space=pl.ANY) if n in unblocked else whole
            for n in range(len(inputs))
        ],
        out_specs=[whole] * len(out_shapes),
        scratch_shapes=scratch,
        compiler_params=pltpu.CompilerParams(vmem_limit_bytes=vmem * MIB),
        name=kernel.__name__,
        cost_estimate=pl.CostEstimate(flops=flops, bytes_accessed=moved, transcendentals=0),
    )(*inputs)


def dot(a, b, contract):
    return lax.dot_general(a, b, (contract, ((), ())), preferred_element_type=F32)


def send_kernel(gate_hbm, cotangent_hbm, left_hbm, values_hbm, out_ref, gate, cotangent, left, values, sems):
    seq, _, rows, cols, channels = out_ref.shape
    pairs = [(gate_hbm, gate), (cotangent_hbm, cotangent), (left_hbm, left), (values_hbm, values)]
    loads = [
        [
            pltpu.make_async_copy(source.at[i], target.at[i], sems.at[n, i])
            for n, (source, target) in enumerate(pairs)
        ]
        for i in range(rows)
    ]
    for row in loads:
        for load in row:
            load.start()
    for i in range(rows):
        for load in loads[i]:
            load.wait()
        mixed = dot(left[i], values[i], ((1,), (0,)))
        out_ref[:, 1, i] = mixed.astype(BF16).reshape(seq, cols, channels)
        wide = gate[i].astype(F32) * cotangent[i].astype(F32)
        out_ref[:, 0, i] = wide.astype(BF16)


def load_columns(in_ref, which, wide):
    for p in range(in_ref.shape[0]):
        rows, cols, channels = in_ref.shape[2:]
        size = rows * cols
        block = in_ref[p, which].reshape(size, channels).astype(F32)
        for h in range(channels // 128):
            wide[h, p * size : (p + 1) * size, :] = block[:, h * 128 : (h + 1) * 128]


def column(wide, k, count, cols):
    halves = [wide[h, pl.ds(k, count, stride=cols), :] for h in range(wide.shape[0])]
    return jnp.concatenate(halves, axis=1).astype(BF16)


def store_column(wide, k, count, cols, value):
    for h in range(wide.shape[0]):
        wide[h, pl.ds(k, count, stride=cols), :] = value[:, h * 128 : (h + 1) * 128]


def store_blocks(wide, out_ref):
    seq, rows, cols, channels = out_ref.shape
    size = rows * cols
    for p in range(seq):
        halves = [wide[h, p * size : (p + 1) * size, :] for h in range(wide.shape[0])]
        block = jnp.concatenate(halves, axis=1).astype(BF16)
        out_ref[p] = block.reshape(rows, cols, channels)


def column_backward_kernel(right_ref, after_ref, in_ref, out_ref, by_column_ref, wide, wide_out):
    cols, count, _ = right_ref.shape
    load_columns(in_ref, 0, wide)
    for k in range(cols):
        grad = column(wide, k, count, cols)
        by_column_ref[k] = grad
        store_column(wide_out, k, count, cols, dot(right_ref[k], grad, ((0,), (0,))))
    store_blocks(wide_out, out_ref)


def column_forward_kernel(right_ref, grad_ref, in_ref, out_ref, part_ref, wide, wide_out):
    cols, count, _ = right_ref.shape
    load_columns(in_ref, 1, wide)
    for k in range(cols):
        mixed = column(wide, k, count, cols)
        store_column(wide_out, k, count, cols, dot(right_ref[k], mixed, ((1,), (0,))))
        part_ref[k] = dot(grad_ref[k], mixed, ((1,), (1,))).astype(BF16)
    store_blocks(wide_out, out_ref)


def gather_kernel(in_ref, out_ref):
    for i in range(out_ref.shape[0]):
        out_ref[i] = in_ref[:, i]


def row_backward_kernel(left_ref, values_ref, grad_ref, signal_ref, term_ref):
    for i in range(left_ref.shape[0]):
        grad = grad_ref[i]
        signal_ref[i] = dot(left_ref[i], grad, ((0,), (0,))).astype(BF16)
        term_ref[i] = dot(grad, values_ref[i], ((1,), (1,))).astype(BF16)


def factor_sum_kernel(
    term_ref, values_ref, grad_ref, right_ref, other_ref, left_out_ref, right_out_ref
):
    for i in range(term_ref.shape[0]):
        other = dot(grad_ref[i], values_ref[i], ((1,), (1,))).astype(BF16)
        left_out_ref[i] = (term_ref[i].astype(F32) + other.astype(F32)).astype(BF16)
    right_out_ref[...] = (right_ref[...].astype(F32) + other_ref[...].astype(F32)).astype(BF16)


def output_kernel(gate_ref, cotangent_ref, in_ref, out_ref, grad_ref):
    for i in range(gate_ref.shape[0]):
        second = in_ref[:, i].astype(F32)
        out_ref[i] = (gate_ref[i].astype(F32) * second).astype(BF16)
        grad_ref[i] = (cotangent_ref[i].astype(F32) * second).astype(BF16)


def direct_shards(signal, gating, upstream, left_factor, right_factor):
    seq = lax.axis_size("seq")
    rows, block_len = left_factor.shape[:2]
    cols, count = right_factor.shape[:2]
    channels = signal.shape[2]
    values = signal.reshape(rows, block_len, channels)
    gate = gating.reshape(rows, seq, cols, channels)
    cotangent = upstream.reshape(rows, seq, cols, channels)

    blocks = jax.ShapeDtypeStruct((seq, rows, cols, channels), BF16)
    whole = jax.ShapeDtypeStruct((rows, seq, cols, channels), BF16)
    by_row = jax.ShapeDtypeStruct((rows, block_len, channels), BF16)
    left = jax.ShapeDtypeStruct(left_factor.shape, BF16)
    right = jax.ShapeDtypeStruct(right_factor.shape, BF16)
    by_column = jax.ShapeDtypeStruct((cols, count, channels), BF16)
    wide = pltpu.VMEM((channels // 128, count * cols, 128), F32)
    row_flops = 2 * rows * block_len * block_len * channels
    column_flops = 2 * cols * count * count * channels

    pairs = jax.ShapeDtypeStruct((seq, 2, rows, cols, channels), BF16)
    loaded = (gate, cotangent, left_factor, values)
    (sent,) = call(
        send_kernel,
        loaded,
        [pairs],
        [pltpu.VMEM(x.shape, BF16) for x in loaded] + [pltpu.SemaphoreType.DMA((4, rows))],
        row_flops,
        unblocked=range(4),
        vmem=60,
    )
    received = exchange(sent)
    other_values = swap_sequences(after(values, sent))
    grad_second, grad_column = call(
        column_backward_kernel,
        [right_factor, other_values, received],
        [blocks, by_column],
        [wide, wide],
        column_flops,
        unblocked=[1],
    )
    back_blocks = exchange(grad_second)
    second, right_part = call(
        column_forward_kernel,
        [right_factor, grad_column, received],
        [blocks, right],
        [wide, wide],
        2 * column_flops,
    )
    other_right = swap_sequences(right_part)
    second_blocks = exchange(after(second, other_right))
    (gathered,) = call(gather_kernel, [back_blocks], [whole])
    grad_back = gathered.reshape(rows, block_len, channels)
    other_grad_back = swap_sequences(grad_back)
    grad_signal, left_term = call(
        row_backward_kernel, [left_factor, values, grad_back], [by_row, left], flops=2 * row_flops
    )
    grad_left, grad_right = call(
        factor_sum_kernel,
        [left_term, other_values, other_grad_back, right_part, other_right],
        [left, right],
        flops=row_flops,
    )
    output, grad_gate = call(
        output_kernel, [after(gate, left_term), cotangent, second_blocks], [whole, whole]
    )
    return (
        output.reshape(signal.shape),
        grad_gate.reshape(signal.shape),
        grad_signal.reshape(signal.shape),
        grad_left,
        grad_right,
    )


def plain_shards(signal, gating, upstream, left_factor, right_factor):
    seq = lax.axis_size("seq")
    rows, block_len = left_factor.shape[:2]
    cols, block_count = right_factor.shape[:2]
    channels = signal.shape[2]
    values = signal.reshape(rows, block_len, channels)
    gate = gating.reshape(rows, block_len, channels)
    cotangent = upstream.reshape(rows, block_len, channels)

    def einsum(spec, a, b):
        return jnp.einsum(spec, a, b, preferred_element_type=F32).astype(BF16)

    def all_to_all(blocks):
        return lax.all_to_all(blocks, "seq", split_axis=0, concat_axis=0, tiled=True)

    def to_columns(by_row):
        blocks = by_row.reshape(rows, seq, cols, channels).transpose(1, 0, 2, 3)
        return all_to_all(blocks).reshape(block_count, cols, channels)

    def to_rows(by_column):
        blocks = all_to_all(by_column.reshape(seq, rows, cols, channels))
        return blocks.transpose(1, 0, 2, 3).reshape(rows, block_len, channels)

    grad_rows = (cotangent.astype(F32) * gate.astype(F32)).astype(BF16)
    grad_column = to_columns(grad_rows)
    other_values = swap_sequences(values)
    mixed_column = to_columns(einsum("ikj,ijd->ikd", left_factor, values))
    grad_back = to_rows(einsum("kmi,mkd->ikd", right_factor, grad_column))
    second_rows = to_rows(einsum("kmi,ikd->mkd", right_factor, mixed_column))
    right_part = einsum("mkd,ikd->kmi", grad_column, mixed_column)
    other_right = swap_sequences(right_part)
    other_grad_back = swap_sequences(grad_back)
    grad_signal = einsum("ikj,ikd->ijd", left_factor, grad_back)
    left_term = einsum("ikd,ijd->ikj", grad_back, values)
    other_left = einsum("ikd,ijd->ikj", other_grad_back, other_values)
    grad_left = (left_term.astype(F32) + other_left.astype(F32)).astype(BF16)
    grad_right = (right_part.astype(F32) + other_right.astype(F32)).astype(BF16)
    wide = second_rows.astype(F32)
    output = (gate.astype(F32) * wide).astype(BF16)
    grad_gate = (cotangent.astype(F32) * wide).astype(BF16)
    return (
        output.reshape(signal.shape),
        grad_gate.reshape(signal.shape),
        grad_signal.reshape(signal.shape),
        grad_left,
        grad_right,
    )


def shards(signal, gating, upstream, left_factor, right_factor):
    seq = lax.axis_size("seq")
    cols = right_factor.shape[0]
    direct = seq <= 16 and seq & (seq - 1) == 0 and cols % 32 == 0
    run = direct_shards if direct else plain_shards
    return run(signal, gating, upstream, left_factor, right_factor)


def solution(mesh):
    by_position = P("dp", "seq", None)
    by_block = P("seq", None, None)
    return jax.shard_map(
        shards,
        mesh=mesh,
        in_specs=(by_position,) * 3 + (by_block,) * 2,
        out_specs=(by_position,) * 3 + (by_block,) * 2,
        check_vma=False,
    )
```

```python
import functools

import jax
import jax.numpy as jnp
from jax import lax
from jax.experimental import pallas as pl
from jax.experimental.pallas import tpu as pltpu
from jax.sharding import PartitionSpec as P

BF16 = jnp.bfloat16
F32 = jnp.float32
MIB = 1024 * 1024


def swap_sequences(array):
    return lax.ppermute(array, "dp", [(0, 1), (1, 0)])


def after(array, earlier):
    return lax.optimization_barrier((array, earlier))[0]


def orders(chips):
    half = chips // 2
    near = list(range(1, half))
    far = list(range(half, chips, 2)) + list(range(half + 1, chips, 2))
    in_turns = [t for pair in zip(near, far) for t in pair]
    return [0] + in_turns + far[half - 1 :], [0] + far[:-1] + near + far[-1:]


def permute(array, offset):
    seq = lax.axis_size("seq")
    return lax.ppermute(array, "seq", [(i, i ^ offset) for i in range(seq)])


def exchange(messages, sent=0, received=None):
    result = [permute(message, 2 * t) if t else message for t, message in enumerate(messages)]
    if received is not None:
        result[sent] = received
    return result


def listed(messages, order):
    return [messages[t] for t in order]


def call(kernel, me, inputs, out_shapes, scratch=(), flops=0, unblocked=(), vmem=32):
    whole = pl.BlockSpec(memory_space=pltpu.VMEM)
    moved = sum(x.size * x.dtype.itemsize for x in (*inputs, *out_shapes))
    in_specs = [
        pl.BlockSpec(memory_space=pl.ANY) if n in unblocked else whole for n in range(len(inputs))
    ]
    return pl.pallas_call(
        kernel,
        out_shape=out_shapes,
        in_specs=[pl.BlockSpec(memory_space=pltpu.SMEM)] + in_specs,
        out_specs=[whole] * len(out_shapes),
        scratch_shapes=scratch,
        compiler_params=pltpu.CompilerParams(vmem_limit_bytes=vmem * MIB),
        name=getattr(kernel, "func", kernel).__name__,
        cost_estimate=pl.CostEstimate(flops=flops, bytes_accessed=moved, transcendentals=0),
    )(me, *inputs)


def dot(a, b, contract):
    return lax.dot_general(a, b, (contract, ((), ())), preferred_element_type=F32)


def block_views(me, refs):
    return [(me ^ (2 * t + e), ref.at[t]) for e, ref in enumerate(refs) for t in range(ref.shape[0])]


def received_views(me, refs, order):
    return [(me ^ (2 * t + e), ref.at[e]) for t, ref in zip(order, refs) for e in range(2)]


def send_kernel(me_ref, gate_hbm, cotangent_hbm, left_hbm, values_hbm, *refs):
    out_refs = refs[:2]
    gate, cotangent, left, values, hold, sems = refs[2:]
    rows, seq, cols, channels = hold.shape
    me = me_ref[0]
    loads = []
    for i in range(rows):
        for n, (source, target) in enumerate(((left_hbm, left), (values_hbm, values))):
            loads.append(pltpu.make_async_copy(source.at[i], target.at[i], sems.at[n, i]))
    loads.append(pltpu.make_async_copy(gate_hbm, gate, sems.at[2, 0]))
    loads.append(pltpu.make_async_copy(cotangent_hbm, cotangent, sems.at[2, 1]))
    for load in loads:
        load.start()
    for i in range(rows):
        loads[2 * i].wait()
        loads[2 * i + 1].wait()
        mixed = dot(left[i], values[i], ((1,), (0,)))
        hold[i] = mixed.astype(BF16).reshape(seq, cols, channels)
    loads[-2].wait()
    loads[-1].wait()
    for c, ref in block_views(me, out_refs):
        wide = gate[:, c].astype(F32) * cotangent[:, c].astype(F32)
        ref[0] = wide.astype(BF16)
        ref[1] = hold[:, c]


def pack_kernel(me_ref, own_ref, other_ref, *out_refs):
    for t, out_ref in enumerate(out_refs):
        out_ref[0] = own_ref[t]
        out_ref[1] = other_ref[t]


def load_columns(blocks, wide):
    rows, cols, channels = blocks[0][1].shape
    size = rows * cols
    for c, ref in blocks:
        block = ref[...].reshape(size, channels).astype(F32)
        start = pl.multiple_of(c * size, size)
        for h in range(channels // 128):
            wide[h, pl.ds(start, size), :] = block[:, h * 128 : (h + 1) * 128]


def column(wide, k, count, cols):
    halves = [wide[h, pl.ds(k, count, stride=cols), :] for h in range(wide.shape[0])]
    return jnp.concatenate(halves, axis=1).astype(BF16)


def store_column(wide, k, count, cols, value):
    for h in range(wide.shape[0]):
        wide[h, pl.ds(k, count, stride=cols), :] = value[:, h * 128 : (h + 1) * 128]


def send_columns(wide, blocks):
    rows, cols, channels = blocks[0][1].shape
    size = rows * cols
    for c, ref in blocks:
        start = pl.multiple_of(c * size, size)
        halves = [wide[h, pl.ds(start, size), :] for h in range(wide.shape[0])]
        block = jnp.concatenate(halves, axis=1).astype(BF16)
        ref[...] = block.reshape(rows, cols, channels)


def column_backward_kernel(order, me_ref, right_ref, *refs):
    chips = len(order)
    in_refs, out_refs = refs[:chips], refs[chips : chips + 2]
    by_column_ref, wide, wide_out = refs[chips + 2 :]
    cols, count, _ = right_ref.shape
    me = me_ref[0]
    load_columns([(c, ref.at[0]) for c, ref in received_views(me, in_refs, order)], wide)
    for k in range(cols):
        grad = column(wide, k, count, cols)
        by_column_ref[k] = grad
        store_column(wide_out, k, count, cols, dot(right_ref[k], grad, ((0,), (0,))))
    send_columns(wide_out, block_views(me, out_refs))


def column_forward_kernel(order, me_ref, right_ref, grad_ref, after_ref, *refs):
    chips = len(order)
    in_refs, out_refs = refs[:chips], refs[chips : chips + 2]
    right_part_ref, wide, wide_out = refs[chips + 2 :]
    cols, count, _ = right_ref.shape
    me = me_ref[0]
    load_columns([(c, ref.at[1]) for c, ref in received_views(me, in_refs, order)], wide)
    for k in range(cols):
        mixed = column(wide, k, count, cols)
        store_column(wide_out, k, count, cols, dot(right_ref[k], mixed, ((1,), (0,))))
        right_part_ref[k] = dot(grad_ref[k], mixed, ((1,), (1,))).astype(BF16)
    send_columns(wide_out, block_views(me, out_refs))


def gather_kernel(me_ref, *refs):
    out_ref = refs[-1]
    for t, ref in enumerate(refs[:-1]):
        for e in range(2):
            out_ref[2 * t + e] = ref[e]


def load_rows(order, me, parts, hold):
    half = parts[0].shape[0]
    for n, t in enumerate(order):
        for e in range(2):
            j = 2 * n + e
            hold[:, me ^ (2 * t + e)] = parts[j // half][j % half]


def row_of(hold, i):
    seq, cols, channels = hold.shape[1:]
    return hold[i].reshape(seq * cols, channels)


def row_backward_kernel(
    order, me_ref, left_ref, values_ref, first_ref, second_ref, signal_ref, term_ref, hold
):
    load_rows(order, me_ref[0], (first_ref, second_ref), hold)
    for i in range(left_ref.shape[0]):
        grad = row_of(hold, i)
        signal_ref[i] = dot(left_ref[i], grad, ((0,), (0,))).astype(BF16)
        term_ref[i] = dot(grad, values_ref[i], ((1,), (1,))).astype(BF16)


def factor_sum_kernel(
    order,
    me_ref,
    term_ref,
    values_ref,
    first_ref,
    second_ref,
    right_ref,
    other_ref,
    left_out_ref,
    right_out_ref,
    hold,
):
    right_out_ref[...] = (right_ref[...].astype(F32) + other_ref[...].astype(F32)).astype(BF16)
    load_rows(order, me_ref[0], (first_ref, second_ref), hold)
    for i in range(term_ref.shape[0]):
        other = dot(row_of(hold, i), values_ref[i], ((1,), (1,))).astype(BF16)
        left_out_ref[i] = (term_ref[i].astype(F32) + other.astype(F32)).astype(BF16)


def output_kernel(order, me_ref, gate_ref, cotangent_ref, *refs):
    chips = len(order)
    out_ref, grad_ref = refs[chips:]
    for c, ref in received_views(me_ref[0], refs[:chips], order):
        second = ref[...].astype(F32)
        out_ref[:, c] = (gate_ref[:, c].astype(F32) * second).astype(BF16)
        grad_ref[:, c] = (cotangent_ref[:, c].astype(F32) * second).astype(BF16)


def direct_shards(signal, gating, upstream, left_factor, right_factor):
    seq = lax.axis_size("seq")
    chips = seq // 2
    rows, block_len = left_factor.shape[:2]
    cols, count = right_factor.shape[:2]
    channels = signal.shape[2]
    me = lax.axis_index("seq").astype(jnp.int32).reshape(1)
    values = signal.reshape(rows, block_len, channels)
    gate = gating.reshape(rows, seq, cols, channels)
    cotangent = upstream.reshape(rows, seq, cols, channels)

    def shape(*dims):
        return jax.ShapeDtypeStruct(dims, BF16)

    in_turns, far_first = orders(chips)

    def ordered(kernel, order=in_turns):
        return functools.partial(kernel, order)

    block = (rows, cols, channels)
    whole = shape(rows, seq, cols, channels)
    by_row = shape(rows, block_len, channels)
    left = shape(*left_factor.shape)
    right = shape(*right_factor.shape)
    wide = pltpu.VMEM((channels // 128, count * cols, 128), F32)
    row_flops = 2 * rows * block_len * block_len * channels
    column_flops = 2 * cols * count * count * channels

    def pack(own, other, earlier=()):
        message = shape(2, *own.shape[1:])
        swapped = permute(after(other, earlier), 1)
        return list(call(pack_kernel, me, [own, swapped], [message] * chips))

    own, other = call(
        send_kernel,
        me,
        [gate, cotangent, left_factor, values],
        [shape(chips, 2, *block)] * 2,
        [pltpu.VMEM(x.shape, BF16) for x in (gate, cotangent, left_factor, values, whole)]
        + [pltpu.SemaphoreType.DMA((3, max(rows, 2)))],
        row_flops,
        unblocked=range(4),
        vmem=60,
    )
    messages = pack(own, other)
    other_values = swap_sequences(after(values, messages[0]))
    columns = listed(exchange(messages), in_turns)
    own, other, grad_column = call(
        ordered(column_backward_kernel),
        me,
        [right_factor, *columns],
        [shape(chips, *block)] * 2 + [shape(cols, count, channels)],
        [wide, wide],
        column_flops,
    )
    back = pack(own, other)
    own, other, right_part = call(
        ordered(column_forward_kernel),
        me,
        [right_factor, grad_column, other_values, *columns],
        [shape(chips, *block)] * 2 + [right],
        [wide, wide],
        2 * column_flops,
        unblocked=[2],
    )
    first = far_first[1]
    first_back = permute(back[first], 2 * first)
    second = pack(own, other, first_back)
    back[far_first[-1]] = after(back[far_first[-1]], second[0])
    other_right = swap_sequences(right_part)
    back = listed(exchange(back, first, first_back), far_first)
    first_second = permute(second[first], 2 * first)
    back[-1] = after(back[-1], (first_second, other_right))
    half_rows = shape(seq // 2, *block)
    hold = pltpu.VMEM(whole.shape, BF16)
    (first_half,) = call(gather_kernel, me, back[: chips // 2], [half_rows])
    (second_half,) = call(gather_kernel, me, back[chips // 2 :], [half_rows])
    other_first = swap_sequences(first_half)
    other_second = swap_sequences(second_half)
    grad_signal, left_term = call(
        ordered(row_backward_kernel, far_first),
        me,
        [left_factor, values, first_half, second_half],
        [by_row, left],
        [hold],
        2 * row_flops,
    )
    second[far_first[-1]] = after(second[far_first[-1]], left_term)
    second = listed(exchange(second, first, first_second), far_first)
    grad_left, grad_right = call(
        ordered(factor_sum_kernel, far_first),
        me,
        [left_term, other_values, other_first, other_second, right_part, other_right],
        [left, right],
        [hold],
        row_flops,
    )
    output, grad_gate = call(
        ordered(output_kernel, far_first), me, [gate, cotangent, *second], [whole, whole]
    )
    return (
        output.reshape(signal.shape),
        grad_gate.reshape(signal.shape),
        grad_signal.reshape(signal.shape),
        grad_left,
        grad_right,
    )


def plain_shards(signal, gating, upstream, left_factor, right_factor):
    seq = lax.axis_size("seq")
    rows, block_len = left_factor.shape[:2]
    cols, block_count = right_factor.shape[:2]
    channels = signal.shape[2]
    values = signal.reshape(rows, block_len, channels)
    gate = gating.reshape(rows, block_len, channels)
    cotangent = upstream.reshape(rows, block_len, channels)

    def einsum(spec, a, b):
        return jnp.einsum(spec, a, b, preferred_element_type=F32).astype(BF16)

    def all_to_all(blocks):
        return lax.all_to_all(blocks, "seq", split_axis=0, concat_axis=0, tiled=True)

    def to_columns(by_row):
        blocks = by_row.reshape(rows, seq, cols, channels).transpose(1, 0, 2, 3)
        return all_to_all(blocks).reshape(block_count, cols, channels)

    def to_rows(by_column):
        blocks = all_to_all(by_column.reshape(seq, rows, cols, channels))
        return blocks.transpose(1, 0, 2, 3).reshape(rows, block_len, channels)

    grad_rows = (cotangent.astype(F32) * gate.astype(F32)).astype(BF16)
    grad_column = to_columns(grad_rows)
    other_values = swap_sequences(values)
    mixed_column = to_columns(einsum("ikj,ijd->ikd", left_factor, values))
    grad_back = to_rows(einsum("kmi,mkd->ikd", right_factor, grad_column))
    second_rows = to_rows(einsum("kmi,ikd->mkd", right_factor, mixed_column))
    right_part = einsum("mkd,ikd->kmi", grad_column, mixed_column)
    other_right = swap_sequences(right_part)
    other_grad_back = swap_sequences(grad_back)
    grad_signal = einsum("ikj,ikd->ijd", left_factor, grad_back)
    left_term = einsum("ikd,ijd->ikj", grad_back, values)
    other_left = einsum("ikd,ijd->ikj", other_grad_back, other_values)
    grad_left = (left_term.astype(F32) + other_left.astype(F32)).astype(BF16)
    grad_right = (right_part.astype(F32) + other_right.astype(F32)).astype(BF16)
    wide = second_rows.astype(F32)
    output = (gate.astype(F32) * wide).astype(BF16)
    grad_gate = (cotangent.astype(F32) * wide).astype(BF16)
    return (
        output.reshape(signal.shape),
        grad_gate.reshape(signal.shape),
        grad_signal.reshape(signal.shape),
        grad_left,
        grad_right,
    )


def shards(signal, gating, upstream, left_factor, right_factor):
    seq = lax.axis_size("seq")
    cols = right_factor.shape[0]
    direct = seq in (8, 16) and cols % 32 == 0
    run = direct_shards if direct else plain_shards
    return run(signal, gating, upstream, left_factor, right_factor)


def solution(mesh):
    by_position = P("dp", "seq", None)
    by_block = P("seq", None, None)
    return jax.shard_map(
        shards,
        mesh=mesh,
        in_specs=(by_position,) * 3 + (by_block,) * 2,
        out_specs=(by_position,) * 3 + (by_block,) * 2,
        check_vma=False,
    )
```

```python
import functools
import math

import jax
import jax.numpy as jnp
from jax import lax
from jax.experimental import pallas as pl
from jax.experimental.pallas import tpu as pltpu
from jax.sharding import PartitionSpec as P

BF16 = jnp.bfloat16
F32 = jnp.float32
MIB = 1024 * 1024


def swap_sequences(array):
    return lax.ppermute(array, "dp", [(0, 1), (1, 0)])


def after(array, earlier):
    return lax.optimization_barrier((array, earlier))[0]


def orders(chips):
    half = chips // 2
    near = list(range(1, half))
    far = list(range(half, chips, 2)) + list(range(half + 1, chips, 2))
    in_turns = [t for pair in zip(far, near) for t in pair]
    return [0] + in_turns + far[half - 1 :], [0] + far[:2] + near + far[2:], [0] + far + near


def permute(array, offset):
    seq = lax.axis_size("seq")
    return lax.ppermute(array, "seq", [(i, i ^ offset) for i in range(seq)])


def exchange(messages, sent=0, received=None):
    result = [permute(message, 2 * t) if t else message for t, message in enumerate(messages)]
    if received is not None:
        result[sent] = received
    return result


def listed(messages, order):
    return [messages[t] for t in order]


def call(kernel, me, inputs, out_shapes, scratch=(), flops=0, unblocked=(), vmem=32):
    whole = pl.BlockSpec(memory_space=pltpu.VMEM)
    moved = sum(x.size * x.dtype.itemsize for x in (*inputs, *out_shapes))
    in_specs = [
        pl.BlockSpec(memory_space=pl.ANY) if n in unblocked else whole for n in range(len(inputs))
    ]
    return pl.pallas_call(
        kernel,
        out_shape=out_shapes,
        in_specs=[pl.BlockSpec(memory_space=pltpu.SMEM)] + in_specs,
        out_specs=[whole] * len(out_shapes),
        scratch_shapes=scratch,
        compiler_params=pltpu.CompilerParams(vmem_limit_bytes=vmem * MIB),
        name=getattr(kernel, "func", kernel).__name__,
        cost_estimate=pl.CostEstimate(flops=flops, bytes_accessed=moved, transcendentals=0),
    )(me, *inputs)


def dot(a, b, contract):
    return lax.dot_general(a, b, (contract, ((), ())), preferred_element_type=F32)


def block_views(me, refs):
    return [(me ^ (2 * t + e), ref.at[t]) for e, ref in enumerate(refs) for t in range(ref.shape[0])]


def received_views(me, refs, order):
    return [(me ^ (2 * t + e), ref.at[e]) for t, ref in zip(order, refs) for e in range(2)]


def send_kernel(me_ref, gate_hbm, cotangent_hbm, left_hbm, values_hbm, *refs):
    out_refs = refs[:2]
    gate, cotangent, left, values, hold, sems = refs[2:]
    rows, seq, cols, channels = hold.shape
    me = me_ref[0]
    loads = []
    for i in range(rows):
        for n, (source, target) in enumerate(((left_hbm, left), (values_hbm, values))):
            loads.append(pltpu.make_async_copy(source.at[i], target.at[i], sems.at[n, i]))
    loads.append(pltpu.make_async_copy(gate_hbm, gate, sems.at[2, 0]))
    loads.append(pltpu.make_async_copy(cotangent_hbm, cotangent, sems.at[2, 1]))
    for load in loads:
        load.start()
    for i in range(rows):
        loads[2 * i].wait()
        loads[2 * i + 1].wait()
        mixed = dot(left[i], values[i], ((1,), (0,)))
        hold[i] = mixed.astype(BF16).reshape(seq, cols, channels)
    loads[-2].wait()
    loads[-1].wait()
    for c, ref in block_views(me, out_refs):
        wide = gate[:, c].astype(F32) * cotangent[:, c].astype(F32)
        ref[0] = wide.astype(BF16)
        ref[1] = hold[:, c]


def pack_kernel(me_ref, own_ref, other_ref, *out_refs):
    for t, out_ref in enumerate(out_refs):
        out_ref[0] = own_ref[t]
        out_ref[1] = other_ref[t]


def load_columns(blocks, wide):
    rows, cols, channels = blocks[0][1].shape
    size = rows * cols
    for c, ref in blocks:
        block = ref[...].reshape(size, channels).astype(F32)
        start = pl.multiple_of(c * size, size)
        for h in range(channels // 128):
            wide[h, pl.ds(start, size), :] = block[:, h * 128 : (h + 1) * 128]


def column(wide, k, count, cols):
    halves = [wide[h, pl.ds(k, count, stride=cols), :] for h in range(wide.shape[0])]
    return jnp.concatenate(halves, axis=1).astype(BF16)


def store_column(wide, k, count, cols, value):
    for h in range(wide.shape[0]):
        wide[h, pl.ds(k, count, stride=cols), :] = value[:, h * 128 : (h + 1) * 128]


def send_columns(wide, blocks):
    rows, cols, channels = blocks[0][1].shape
    size = rows * cols
    for c, ref in blocks:
        start = pl.multiple_of(c * size, size)
        halves = [wide[h, pl.ds(start, size), :] for h in range(wide.shape[0])]
        block = jnp.concatenate(halves, axis=1).astype(BF16)
        ref[...] = block.reshape(rows, cols, channels)


def column_backward_kernel(order, me_ref, right_ref, *refs):
    chips = len(order)
    in_refs, out_refs = refs[:chips], refs[chips : chips + 2]
    by_column_ref, wide, wide_out = refs[chips + 2 :]
    cols, count, _ = right_ref.shape
    me = me_ref[0]
    load_columns([(c, ref.at[0]) for c, ref in received_views(me, in_refs, order)], wide)
    for k in range(cols):
        grad = column(wide, k, count, cols)
        by_column_ref[k] = grad
        store_column(wide_out, k, count, cols, dot(right_ref[k], grad, ((0,), (0,))))
    send_columns(wide_out, block_views(me, out_refs))


def column_forward_kernel(order, me_ref, right_ref, grad_ref, after_ref, *refs):
    chips = len(order)
    in_refs, out_refs = refs[:chips], refs[chips : chips + 2]
    packed_ref, wide, wide_out = refs[chips + 2 :]
    cols, count, _ = right_ref.shape
    channels = packed_ref.shape[1]
    terms = []
    me = me_ref[0]
    load_columns([(c, ref.at[1]) for c, ref in received_views(me, in_refs, order)], wide)
    for k in range(cols):
        mixed = column(wide, k, count, cols)
        store_column(wide_out, k, count, cols, dot(right_ref[k], mixed, ((1,), (0,))))
        terms.append(dot(grad_ref[k], mixed, ((1,), (1,))))
        if len(terms) == channels // count:
            row = k * count // channels * count
            packed_ref[row : row + count] = jnp.concatenate(terms, axis=1).astype(BF16)
            terms = []
    send_columns(wide_out, block_views(me, out_refs))


def gather_kernel(me_ref, *refs):
    out_ref, n = refs[-1], 0
    _, rows, cols, channels = out_ref.shape
    size = rows * cols
    for ref in refs[:-1]:
        if ref.ndim == 2:
            for start in range(0, ref.shape[0], size):
                out_ref[n] = ref[start : start + size].reshape(rows, cols, channels)
                n += 1
            continue
        for e in range(ref.shape[0]):
            out_ref[n] = ref[e]
            n += 1


def load_rows(order, me, parts, hold):
    half = len(order)
    for n, t in enumerate(order):
        for e in range(2):
            j = 2 * n + e
            hold[:, me ^ (2 * t + e)] = parts[j // half][j % half]


def row_of(hold, i):
    seq, cols, channels = hold.shape[1:]
    return hold[i].reshape(seq * cols, channels)


def row_backward_kernel(
    order, me_ref, left_ref, values_ref, first_ref, second_ref, signal_ref, term_ref, hold
):
    load_rows(order, me_ref[0], (first_ref, second_ref), hold)
    for i in range(left_ref.shape[0]):
        grad = row_of(hold, i)
        signal_ref[i] = dot(left_ref[i], grad, ((0,), (0,))).astype(BF16)
        term_ref[i] = dot(grad, values_ref[i], ((1,), (1,))).astype(BF16)


def factor_sum_kernel(
    order,
    me_ref,
    term_ref,
    values_ref,
    first_ref,
    second_ref,
    packed_ref,
    left_out_ref,
    right_out_ref,
    hold,
):
    load_rows(order, me_ref[0], (first_ref, second_ref), hold)
    for i in range(term_ref.shape[0]):
        other = dot(row_of(hold, i), values_ref[i], ((1,), (1,))).astype(BF16)
        left_out_ref[i] = (term_ref[i].astype(F32) + other.astype(F32)).astype(BF16)
    cols, count, _ = right_out_ref.shape
    height, channels = packed_ref.shape
    size = height // (first_ref.shape[0] - len(order))
    share = channels // count
    for n in range(height // count):
        block, row = len(order) + n * count // size, n * count % size
        other = first_ref[block].reshape(size, channels)[row : row + count]
        total = packed_ref[n * count : (n + 1) * count].astype(F32) + other.astype(F32)
        for q in range(share):
            right_out_ref[n * share + q] = total[:, q * count : (q + 1) * count].astype(BF16)


def output_kernel(order, me_ref, gate_ref, cotangent_ref, *refs):
    chips = len(order)
    out_ref, grad_ref = refs[chips:]
    for c, ref in received_views(me_ref[0], refs[:chips], order):
        second = ref[...].astype(F32)
        out_ref[:, c] = (gate_ref[:, c].astype(F32) * second).astype(BF16)
        grad_ref[:, c] = (cotangent_ref[:, c].astype(F32) * second).astype(BF16)


def direct_shards(signal, gating, upstream, left_factor, right_factor):
    seq = lax.axis_size("seq")
    chips = seq // 2
    rows, block_len = left_factor.shape[:2]
    cols, count = right_factor.shape[:2]
    channels = signal.shape[2]
    me = lax.axis_index("seq").astype(jnp.int32).reshape(1)
    values = signal.reshape(rows, block_len, channels)
    gate = gating.reshape(rows, seq, cols, channels)
    cotangent = upstream.reshape(rows, seq, cols, channels)

    def shape(*dims):
        return jax.ShapeDtypeStruct(dims, BF16)

    in_turns, two_far, all_far = orders(chips)

    def ordered(kernel, order):
        return functools.partial(kernel, order)

    block = (rows, cols, channels)
    whole = shape(rows, seq, cols, channels)
    by_row = shape(rows, block_len, channels)
    left = shape(*left_factor.shape)
    right = shape(*right_factor.shape)
    wide = pltpu.VMEM((channels // 128, count * cols, 128), F32)
    row_flops = 2 * rows * block_len * block_len * channels
    column_flops = 2 * cols * count * count * channels

    def pack(own, other, earlier=()):
        message = shape(2, *own.shape[1:])
        swapped = permute(after(other, earlier), 1)
        return list(call(pack_kernel, me, [own, swapped], [message] * chips))

    own, other = call(
        send_kernel,
        me,
        [gate, cotangent, left_factor, values],
        [shape(chips, 2, *block)] * 2,
        [pltpu.VMEM(x.shape, BF16) for x in (gate, cotangent, left_factor, values, whole)]
        + [pltpu.SemaphoreType.DMA((3, max(rows, 2)))],
        row_flops,
        unblocked=range(4),
        vmem=60,
    )
    messages = pack(own, other)
    other_values = swap_sequences(after(values, messages[0]))
    columns = listed(exchange(messages), in_turns)
    own, other, grad_column = call(
        ordered(column_backward_kernel, in_turns),
        me,
        [right_factor, *columns],
        [shape(chips, *block)] * 2 + [shape(cols, count, channels)],
        [wide, wide],
        column_flops,
    )
    back = exchange(pack(own, other))
    packed_right = shape(cols * count * count // channels, channels)
    own, other, right_part = call(
        ordered(column_forward_kernel, in_turns),
        me,
        [right_factor, grad_column, other_values, *columns],
        [shape(chips, *block)] * 2 + [packed_right],
        [wide, wide],
        2 * column_flops,
        unblocked=[2],
    )
    back = listed(back, two_far)
    messages = pack(own, other, back[1 : chips - 2])
    first = all_far[1]
    first_second = permute(messages[first], 2 * first)
    back[-1] = after(back[-1], first_second)
    half_rows = shape(chips, *block)
    extra = packed_right.size // math.prod(block)
    (first_half,) = call(
        gather_kernel, me, [*back[: chips // 2], right_part], [shape(chips + extra, *block)]
    )
    (second_half,) = call(gather_kernel, me, back[chips // 2 :], [half_rows])
    other_first = swap_sequences(first_half)
    other_second = swap_sequences(second_half)
    hold = pltpu.VMEM(whole.shape, BF16)
    grad_signal, left_term = call(
        ordered(row_backward_kernel, two_far),
        me,
        [left_factor, values, first_half, second_half],
        [by_row, left],
        [hold],
        2 * row_flops,
    )
    grad_left, grad_right = call(
        ordered(factor_sum_kernel, two_far),
        me,
        [left_term, other_values, other_first, other_second, right_part],
        [left, right],
        [hold],
        row_flops,
    )
    last = all_far[-1]
    messages[last] = after(messages[last], grad_left)
    second = listed(exchange(messages, first, first_second), all_far)
    output, grad_gate = call(
        ordered(output_kernel, all_far), me, [gate, cotangent, *second], [whole, whole]
    )
    return (
        output.reshape(signal.shape),
        grad_gate.reshape(signal.shape),
        grad_signal.reshape(signal.shape),
        grad_left,
        grad_right,
    )


def plain_shards(signal, gating, upstream, left_factor, right_factor):
    seq = lax.axis_size("seq")
    rows, block_len = left_factor.shape[:2]
    cols, block_count = right_factor.shape[:2]
    channels = signal.shape[2]
    values = signal.reshape(rows, block_len, channels)
    gate = gating.reshape(rows, block_len, channels)
    cotangent = upstream.reshape(rows, block_len, channels)

    def einsum(spec, a, b):
        return jnp.einsum(spec, a, b, preferred_element_type=F32).astype(BF16)

    def all_to_all(blocks):
        return lax.all_to_all(blocks, "seq", split_axis=0, concat_axis=0, tiled=True)

    def to_columns(by_row):
        blocks = by_row.reshape(rows, seq, cols, channels).transpose(1, 0, 2, 3)
        return all_to_all(blocks).reshape(block_count, cols, channels)

    def to_rows(by_column):
        blocks = all_to_all(by_column.reshape(seq, rows, cols, channels))
        return blocks.transpose(1, 0, 2, 3).reshape(rows, block_len, channels)

    grad_rows = (cotangent.astype(F32) * gate.astype(F32)).astype(BF16)
    grad_column = to_columns(grad_rows)
    other_values = swap_sequences(values)
    mixed_column = to_columns(einsum("ikj,ijd->ikd", left_factor, values))
    grad_back = to_rows(einsum("kmi,mkd->ikd", right_factor, grad_column))
    second_rows = to_rows(einsum("kmi,ikd->mkd", right_factor, mixed_column))
    right_part = einsum("mkd,ikd->kmi", grad_column, mixed_column)
    other_right = swap_sequences(right_part)
    other_grad_back = swap_sequences(grad_back)
    grad_signal = einsum("ikj,ikd->ijd", left_factor, grad_back)
    left_term = einsum("ikd,ijd->ikj", grad_back, values)
    other_left = einsum("ikd,ijd->ikj", other_grad_back, other_values)
    grad_left = (left_term.astype(F32) + other_left.astype(F32)).astype(BF16)
    grad_right = (right_part.astype(F32) + other_right.astype(F32)).astype(BF16)
    wide = second_rows.astype(F32)
    output = (gate.astype(F32) * wide).astype(BF16)
    grad_gate = (cotangent.astype(F32) * wide).astype(BF16)
    return (
        output.reshape(signal.shape),
        grad_gate.reshape(signal.shape),
        grad_signal.reshape(signal.shape),
        grad_left,
        grad_right,
    )


def shards(signal, gating, upstream, left_factor, right_factor):
    seq = lax.axis_size("seq")
    cols = right_factor.shape[0]
    direct = seq in (8, 16) and cols % 32 == 0
    run = direct_shards if direct else plain_shards
    return run(signal, gating, upstream, left_factor, right_factor)


def solution(mesh):
    by_position = P("dp", "seq", None)
    by_block = P("seq", None, None)
    return jax.shard_map(
        shards,
        mesh=mesh,
        in_specs=(by_position,) * 3 + (by_block,) * 2,
        out_specs=(by_position,) * 3 + (by_block,) * 2,
        check_vma=False,
    )
```

```python
import functools
import math

import jax
import jax.numpy as jnp
from jax import lax
from jax.experimental import pallas as pl
from jax.experimental.pallas import tpu as pltpu
from jax.sharding import PartitionSpec as P

BF16 = jnp.bfloat16
F32 = jnp.float32
MIB = 1024 * 1024


def swap_sequences(array):
    return lax.ppermute(array, "dp", [(0, 1), (1, 0)])


def after(array, earlier):
    return lax.optimization_barrier((array, earlier))[0]


def orders(chips):
    half = chips // 2
    near = list(range(1, half))
    far = list(range(half, chips, 2)) + list(range(half + 1, chips, 2))
    in_turns = [t for pair in zip(far, near) for t in pair]
    return [0] + in_turns + far[half - 1 :], [0] + far[:2] + near + far[2:], [0] + far + near


def permute(array, offset):
    seq = lax.axis_size("seq")
    return lax.ppermute(array, "seq", [(i, i ^ offset) for i in range(seq)])


def exchange(messages, done=()):
    done = dict(done)
    return [
        done[t] if t in done else permute(message, 2 * t) if t else message
        for t, message in enumerate(messages)
    ]


def listed(messages, order):
    return [messages[t] for t in order]


def call(kernel, me, inputs, out_shapes, scratch=(), flops=0, unblocked=(), vmem=32):
    whole = pl.BlockSpec(memory_space=pltpu.VMEM)
    moved = sum(x.size * x.dtype.itemsize for x in (*inputs, *out_shapes))
    in_specs = [
        pl.BlockSpec(memory_space=pl.ANY) if n in unblocked else whole for n in range(len(inputs))
    ]
    return pl.pallas_call(
        kernel,
        out_shape=out_shapes,
        in_specs=[pl.BlockSpec(memory_space=pltpu.SMEM)] + in_specs,
        out_specs=[whole] * len(out_shapes),
        scratch_shapes=scratch,
        compiler_params=pltpu.CompilerParams(vmem_limit_bytes=vmem * MIB),
        name=getattr(kernel, "func", kernel).__name__,
        cost_estimate=pl.CostEstimate(flops=flops, bytes_accessed=moved, transcendentals=0),
    )(me, *inputs)


def dot(a, b, contract):
    return lax.dot_general(a, b, (contract, ((), ())), preferred_element_type=F32)


def block_views(me, refs):
    return [(me ^ (2 * t + e), ref.at[t]) for e, ref in enumerate(refs) for t in range(ref.shape[0])]


def received_views(me, refs, order):
    return [(me ^ (2 * t + e), ref.at[e]) for t, ref in zip(order, refs) for e in range(2)]


def product_kernel(me_ref, gate_hbm, cotangent_hbm, *refs):
    out_refs, (gate, cotangent, sems) = refs[:2], refs[2:]
    rows = gate.shape[0]
    loads = [
        [
            pltpu.make_async_copy(source.at[i], target.at[i], sems.at[n, i])
            for n, (source, target) in enumerate(((gate_hbm, gate), (cotangent_hbm, cotangent)))
        ]
        for i in range(rows)
    ]
    for pair in loads:
        for load in pair:
            load.start()
    blocks = block_views(me_ref[0], out_refs)
    for i in range(rows):
        for load in loads[i]:
            load.wait()
        for c, ref in blocks:
            ref[i] = (gate[i, c].astype(F32) * cotangent[i, c].astype(F32)).astype(BF16)


def mix_kernel(me_ref, left_ref, values_ref, *refs):
    out_refs, hold = refs[:2], refs[2]
    rows, seq, cols, channels = hold.shape
    for i in range(rows):
        mixed = dot(left_ref[i], values_ref[i], ((1,), (0,)))
        hold[i] = mixed.astype(BF16).reshape(seq, cols, channels)
    for c, ref in block_views(me_ref[0], out_refs):
        ref[...] = hold[:, c]


def pack_kernel(me_ref, own_ref, other_ref, *out_refs):
    for t, out_ref in enumerate(out_refs):
        out_ref[0] = own_ref[t]
        out_ref[1] = other_ref[t]


def pack_pairs_kernel(me_ref, *refs):
    pairs, out_refs = (refs[0:2], refs[2:4]), refs[4:]
    last = len(out_refs) - 2
    for which, pair in enumerate(pairs):
        for e, ref in enumerate(pair):
            for t in range(last):
                out_refs[t][e, which] = ref[t]
            out_refs[last + which][e] = ref[last]


def of_pair(views, which):
    return [(c, ref.at[which] if len(ref.shape) == 4 else ref) for c, ref in views]


def load_columns(blocks, wide):
    rows, cols, channels = blocks[0][1].shape
    size = rows * cols
    for c, ref in blocks:
        block = ref[...].reshape(size, channels).astype(F32)
        start = pl.multiple_of(c * size, size)
        for h in range(channels // 128):
            wide[h, pl.ds(start, size), :] = block[:, h * 128 : (h + 1) * 128]


def column(wide, k, count, cols):
    halves = [wide[h, pl.ds(k, count, stride=cols), :] for h in range(wide.shape[0])]
    return jnp.concatenate(halves, axis=1).astype(BF16)


def store_column(wide, k, count, cols, value):
    for h in range(wide.shape[0]):
        wide[h, pl.ds(k, count, stride=cols), :] = value[:, h * 128 : (h + 1) * 128]


def send_columns(wide, blocks):
    rows, cols, channels = blocks[0][1].shape
    size = rows * cols
    for c, ref in blocks:
        start = pl.multiple_of(c * size, size)
        halves = [wide[h, pl.ds(start, size), :] for h in range(wide.shape[0])]
        block = jnp.concatenate(halves, axis=1).astype(BF16)
        ref[...] = block.reshape(rows, cols, channels)


def column_backward_kernel(order, me_ref, right_ref, *refs):
    chips = len(order)
    in_refs, out_refs = refs[:chips], refs[chips : chips + 2]
    by_column_ref, wide, wide_out = refs[chips + 2 :]
    cols, count, _ = right_ref.shape
    me = me_ref[0]
    load_columns(of_pair(received_views(me, in_refs, order), 0), wide)
    for k in range(cols):
        grad = column(wide, k, count, cols)
        by_column_ref[k] = grad
        store_column(wide_out, k, count, cols, dot(right_ref[k], grad, ((0,), (0,))))
    send_columns(wide_out, block_views(me, out_refs))


def column_forward_kernel(order, me_ref, right_ref, grad_ref, after_ref, *refs):
    chips = len(order)
    in_refs, out_refs = refs[:chips], refs[chips : chips + 2]
    packed_ref, wide, wide_out = refs[chips + 2 :]
    cols, count, _ = right_ref.shape
    channels = packed_ref.shape[1]
    terms = []
    me = me_ref[0]
    load_columns(of_pair(received_views(me, in_refs, order), 1), wide)
    for k in range(cols):
        mixed = column(wide, k, count, cols)
        store_column(wide_out, k, count, cols, dot(right_ref[k], mixed, ((1,), (0,))))
        terms.append(dot(grad_ref[k], mixed, ((1,), (1,))))
        if len(terms) == channels // count:
            row = k * count // channels * count
            packed_ref[row : row + count] = jnp.concatenate(terms, axis=1).astype(BF16)
            terms = []
    send_columns(wide_out, block_views(me, out_refs))


def gather_kernel(me_ref, *refs):
    out_ref, n = refs[-1], 0
    _, rows, cols, channels = out_ref.shape
    size = rows * cols
    for ref in refs[:-1]:
        if ref.ndim == 2:
            for start in range(0, ref.shape[0], size):
                out_ref[n] = ref[start : start + size].reshape(rows, cols, channels)
                n += 1
            continue
        for e in range(ref.shape[0]):
            out_ref[n] = ref[e]
            n += 1


def load_rows(order, me, parts, hold):
    left = 2 * len(order) - parts[1].shape[0]
    for n, t in enumerate(order):
        for e in range(2):
            j = 2 * n + e
            hold[:, me ^ (2 * t + e)] = parts[0][j] if j < left else parts[1][j - left]


def row_of(hold, i):
    seq, cols, channels = hold.shape[1:]
    return hold[i].reshape(seq * cols, channels)


def row_backward_kernel(
    order, me_ref, left_ref, values_ref, first_ref, second_ref, signal_ref, term_ref, hold
):
    load_rows(order, me_ref[0], (first_ref, second_ref), hold)
    for i in range(left_ref.shape[0]):
        grad = row_of(hold, i)
        signal_ref[i] = dot(left_ref[i], grad, ((0,), (0,))).astype(BF16)
        term_ref[i] = dot(grad, values_ref[i], ((1,), (1,))).astype(BF16)


def factor_sum_kernel(
    order,
    me_ref,
    term_ref,
    values_ref,
    first_ref,
    second_ref,
    packed_ref,
    left_out_ref,
    right_out_ref,
    hold,
):
    load_rows(order, me_ref[0], (first_ref, second_ref), hold)
    for i in range(term_ref.shape[0]):
        other = dot(row_of(hold, i), values_ref[i], ((1,), (1,))).astype(BF16)
        left_out_ref[i] = (term_ref[i].astype(F32) + other.astype(F32)).astype(BF16)
    cols, count, _ = right_out_ref.shape
    height, channels = packed_ref.shape
    blocks = 2 * len(order) - second_ref.shape[0]
    size = height // (first_ref.shape[0] - blocks)
    share = channels // count
    for n in range(height // count):
        block, row = blocks + n * count // size, n * count % size
        other = first_ref[block].reshape(size, channels)[row : row + count]
        total = packed_ref[n * count : (n + 1) * count].astype(F32) + other.astype(F32)
        for q in range(share):
            right_out_ref[n * share + q] = total[:, q * count : (q + 1) * count].astype(BF16)


def output_kernel(order, me_ref, gate_ref, cotangent_ref, *refs):
    chips = len(order)
    out_ref, grad_ref = refs[chips:]
    for c, ref in received_views(me_ref[0], refs[:chips], order):
        second = ref[...].astype(F32)
        out_ref[:, c] = (gate_ref[:, c].astype(F32) * second).astype(BF16)
        grad_ref[:, c] = (cotangent_ref[:, c].astype(F32) * second).astype(BF16)


def direct_shards(signal, gating, upstream, left_factor, right_factor):
    seq = lax.axis_size("seq")
    chips = seq // 2
    rows, block_len = left_factor.shape[:2]
    cols, count = right_factor.shape[:2]
    channels = signal.shape[2]
    me = lax.axis_index("seq").astype(jnp.int32).reshape(1)
    values = signal.reshape(rows, block_len, channels)
    gate = gating.reshape(rows, seq, cols, channels)
    cotangent = upstream.reshape(rows, seq, cols, channels)

    def shape(*dims):
        return jax.ShapeDtypeStruct(dims, BF16)

    in_turns, two_far, all_far = orders(chips)

    def ordered(kernel, order):
        return functools.partial(kernel, order)

    block = (rows, cols, channels)
    whole = shape(rows, seq, cols, channels)
    by_row = shape(rows, block_len, channels)
    left = shape(*left_factor.shape)
    right = shape(*right_factor.shape)
    wide = pltpu.VMEM((channels // 128, count * cols, 128), F32)
    row_flops = 2 * rows * block_len * block_len * channels
    column_flops = 2 * cols * count * count * channels

    def pack(own, swapped):
        return list(call(pack_kernel, me, [own, swapped], [shape(2, *own.shape[1:])] * chips))

    hold = pltpu.VMEM(whole.shape, BF16)
    halves = [shape(chips, *block)] * 2
    last = in_turns[-1]
    own, other = call(
        product_kernel,
        me,
        [gate, cotangent],
        halves,
        [hold, hold, pltpu.SemaphoreType.DMA((2, rows))],
        unblocked=range(2),
        vmem=60,
    )
    own_mixed, other_mixed = call(
        mix_kernel, me, [left_factor, after(values, own)], halves, [hold], row_flops
    )
    *messages, mixed_last = call(
        pack_pairs_kernel,
        me,
        [own, permute(other, 1), own_mixed, permute(other_mixed, 1)],
        [shape(2, 2, *block)] * last + [shape(2, *block)] * 2,
    )
    other_values = swap_sequences(after(values, messages[0]))
    columns = listed(exchange(messages), in_turns)
    mixed_last = permute(after(mixed_last, columns[1:]), 2 * last)
    own, other, grad_column = call(
        ordered(column_backward_kernel, in_turns),
        me,
        [right_factor, *columns],
        [shape(chips, *block)] * 2 + [shape(cols, count, channels)],
        [wide, wide],
        column_flops,
    )
    back = exchange(pack(own, permute(after(other, mixed_last), 1)))
    columns[-1] = mixed_last
    packed_right = shape(cols * count * count // channels, channels)
    own, other, right_part = call(
        ordered(column_forward_kernel, in_turns),
        me,
        [right_factor, grad_column, other_values, *columns],
        [shape(chips, *block)] * 2 + [packed_right],
        [wide, wide],
        2 * column_flops,
        unblocked=[2],
    )
    back = listed(back, two_far)
    messages = pack(own, permute(after(other, back[1 : chips - 2]), 1))
    done = [(t, permute(messages[t], 2 * t)) for t in all_far[1:3]]
    back[-1] = after(back[-1], [block for _, block in done])
    extra = packed_right.size // math.prod(block)
    (first_part,) = call(
        gather_kernel, me, [*back[:-2], right_part], [shape(2 * chips - 4 + extra, *block)]
    )
    (second_part,) = call(gather_kernel, me, back[-2:], [shape(4, *block)])
    other_first = swap_sequences(first_part)
    other_second = swap_sequences(second_part)
    grad_signal, left_term = call(
        ordered(row_backward_kernel, two_far),
        me,
        [left_factor, values, first_part, second_part],
        [by_row, left],
        [hold],
        2 * row_flops,
    )
    grad_left, grad_right = call(
        ordered(factor_sum_kernel, two_far),
        me,
        [left_term, other_values, other_first, other_second, right_part],
        [left, right],
        [hold],
        row_flops,
    )
    last = all_far[-1]
    messages[last] = after(messages[last], grad_left)
    second = listed(exchange(messages, done), all_far)
    output, grad_gate = call(
        ordered(output_kernel, all_far), me, [gate, cotangent, *second], [whole, whole]
    )
    return (
        output.reshape(signal.shape),
        grad_gate.reshape(signal.shape),
        grad_signal.reshape(signal.shape),
        grad_left,
        grad_right,
    )


def plain_shards(signal, gating, upstream, left_factor, right_factor):
    seq = lax.axis_size("seq")
    rows, block_len = left_factor.shape[:2]
    cols, block_count = right_factor.shape[:2]
    channels = signal.shape[2]
    values = signal.reshape(rows, block_len, channels)
    gate = gating.reshape(rows, block_len, channels)
    cotangent = upstream.reshape(rows, block_len, channels)

    def einsum(spec, a, b):
        return jnp.einsum(spec, a, b, preferred_element_type=F32).astype(BF16)

    def all_to_all(blocks):
        return lax.all_to_all(blocks, "seq", split_axis=0, concat_axis=0, tiled=True)

    def to_columns(by_row):
        blocks = by_row.reshape(rows, seq, cols, channels).transpose(1, 0, 2, 3)
        return all_to_all(blocks).reshape(block_count, cols, channels)

    def to_rows(by_column):
        blocks = all_to_all(by_column.reshape(seq, rows, cols, channels))
        return blocks.transpose(1, 0, 2, 3).reshape(rows, block_len, channels)

    grad_rows = (cotangent.astype(F32) * gate.astype(F32)).astype(BF16)
    grad_column = to_columns(grad_rows)
    other_values = swap_sequences(values)
    mixed_column = to_columns(einsum("ikj,ijd->ikd", left_factor, values))
    grad_back = to_rows(einsum("kmi,mkd->ikd", right_factor, grad_column))
    second_rows = to_rows(einsum("kmi,ikd->mkd", right_factor, mixed_column))
    right_part = einsum("mkd,ikd->kmi", grad_column, mixed_column)
    other_right = swap_sequences(right_part)
    other_grad_back = swap_sequences(grad_back)
    grad_signal = einsum("ikj,ikd->ijd", left_factor, grad_back)
    left_term = einsum("ikd,ijd->ikj", grad_back, values)
    other_left = einsum("ikd,ijd->ikj", other_grad_back, other_values)
    grad_left = (left_term.astype(F32) + other_left.astype(F32)).astype(BF16)
    grad_right = (right_part.astype(F32) + other_right.astype(F32)).astype(BF16)
    wide = second_rows.astype(F32)
    output = (gate.astype(F32) * wide).astype(BF16)
    grad_gate = (cotangent.astype(F32) * wide).astype(BF16)
    return (
        output.reshape(signal.shape),
        grad_gate.reshape(signal.shape),
        grad_signal.reshape(signal.shape),
        grad_left,
        grad_right,
    )


def shards(signal, gating, upstream, left_factor, right_factor):
    seq = lax.axis_size("seq")
    cols = right_factor.shape[0]
    direct = seq in (8, 16) and cols % 32 == 0
    run = direct_shards if direct else plain_shards
    return run(signal, gating, upstream, left_factor, right_factor)


def solution(mesh):
    by_position = P("dp", "seq", None)
    by_block = P("seq", None, None)
    return jax.shard_map(
        shards,
        mesh=mesh,
        in_specs=(by_position,) * 3 + (by_block,) * 2,
        out_specs=(by_position,) * 3 + (by_block,) * 2,
        check_vma=False,
    )
```

```python
import functools
import math

import jax
import jax.numpy as jnp
from jax import lax
from jax.experimental import pallas as pl
from jax.experimental.pallas import tpu as pltpu
from jax.sharding import PartitionSpec as P

BF16 = jnp.bfloat16
F32 = jnp.float32
MIB = 1024 * 1024


def swap_sequences(array):
    return lax.ppermute(array, "dp", [(0, 1), (1, 0)])


def after(array, earlier):
    return lax.optimization_barrier((array, earlier))[0]


def orders(chips):
    half = chips // 2
    near = list(range(1, half))
    far = list(range(half, chips, 2)) + list(range(half + 1, chips, 2))
    mixed = far[:2] + near[:-1] + far[2:-1] + near[-1:] + far[-1:]
    return [0] + far[:1] + near + far[1:], [0] + mixed, [0] + far + near


def permute(array, offset):
    seq = lax.axis_size("seq")
    return lax.ppermute(array, "seq", [(i, i ^ offset) for i in range(seq)])


def exchange(messages, done=()):
    done = dict(done)
    return [
        done[t] if t in done else permute(message, 2 * t) if t else message
        for t, message in enumerate(messages)
    ]


def listed(messages, order):
    return [messages[t] for t in order]


def call(kernel, me, inputs, out_shapes, scratch=(), flops=0, unblocked=(), vmem=32):
    whole = pl.BlockSpec(memory_space=pltpu.VMEM)
    moved = sum(x.size * x.dtype.itemsize for x in (*inputs, *out_shapes))
    in_specs = [
        pl.BlockSpec(memory_space=pl.ANY) if n in unblocked else whole for n in range(len(inputs))
    ]
    return pl.pallas_call(
        kernel,
        out_shape=out_shapes,
        in_specs=[pl.BlockSpec(memory_space=pltpu.SMEM)] + in_specs,
        out_specs=[whole] * len(out_shapes),
        scratch_shapes=scratch,
        compiler_params=pltpu.CompilerParams(vmem_limit_bytes=vmem * MIB),
        name=getattr(kernel, "func", kernel).__name__,
        cost_estimate=pl.CostEstimate(flops=flops, bytes_accessed=moved, transcendentals=0),
    )(me, *inputs)


def dot(a, b, contract):
    return lax.dot_general(a, b, (contract, ((), ())), preferred_element_type=F32)


def block_views(me, refs):
    return [(me ^ (2 * t + e), ref.at[t]) for e, ref in enumerate(refs) for t in range(ref.shape[0])]


def received_views(me, refs, order):
    return [(me ^ (2 * t + e), ref.at[e]) for t, ref in zip(order, refs) for e in range(2)]


def product_kernel(me_ref, gate_hbm, cotangent_hbm, *refs):
    out_refs, (gate, cotangent, sems) = refs[:2], refs[2:]
    rows = gate.shape[0]
    loads = [
        [
            pltpu.make_async_copy(source.at[i], target.at[i], sems.at[n, i])
            for n, (source, target) in enumerate(((gate_hbm, gate), (cotangent_hbm, cotangent)))
        ]
        for i in range(rows)
    ]
    for pair in loads:
        for load in pair:
            load.start()
    blocks = block_views(me_ref[0], out_refs)
    for i in range(rows):
        for load in loads[i]:
            load.wait()
        for c, ref in blocks:
            ref[i] = (gate[i, c].astype(F32) * cotangent[i, c].astype(F32)).astype(BF16)


def mix_kernel(me_ref, left_ref, values_ref, *refs):
    out_refs, hold = refs[:2], refs[2]
    rows, seq, cols, channels = hold.shape
    for i in range(rows):
        mixed = dot(left_ref[i], values_ref[i], ((1,), (0,)))
        hold[i] = mixed.astype(BF16).reshape(seq, cols, channels)
    for c, ref in block_views(me_ref[0], out_refs):
        ref[...] = hold[:, c]


def pack_kernel(me_ref, own_ref, other_ref, *out_refs):
    for t, out_ref in enumerate(out_refs):
        out_ref[0] = own_ref[t]
        out_ref[1] = other_ref[t]


def pack_pairs_kernel(me_ref, *refs):
    pairs, out_refs = (refs[0:2], refs[2:4]), refs[4:]
    last = len(out_refs) - 2
    for which, pair in enumerate(pairs):
        for e, ref in enumerate(pair):
            for t in range(last):
                out_refs[t][e, which] = ref[t]
            out_refs[last + which][e] = ref[last]


def of_pair(views, which):
    return [(c, ref.at[which] if len(ref.shape) == 4 else ref) for c, ref in views]


def load_columns(blocks, wide):
    rows, cols, channels = blocks[0][1].shape
    size = rows * cols
    for c, ref in blocks:
        block = ref[...].reshape(size, channels).astype(F32)
        start = pl.multiple_of(c * size, size)
        for h in range(channels // 128):
            wide[h, pl.ds(start, size), :] = block[:, h * 128 : (h + 1) * 128]


def column(wide, k, count, cols):
    halves = [wide[h, pl.ds(k, count, stride=cols), :] for h in range(wide.shape[0])]
    return jnp.concatenate(halves, axis=1).astype(BF16)


def store_column(wide, k, count, cols, value):
    for h in range(wide.shape[0]):
        wide[h, pl.ds(k, count, stride=cols), :] = value[:, h * 128 : (h + 1) * 128]


def send_columns(wide, blocks):
    rows, cols, channels = blocks[0][1].shape
    size = rows * cols
    for c, ref in blocks:
        start = pl.multiple_of(c * size, size)
        halves = [wide[h, pl.ds(start, size), :] for h in range(wide.shape[0])]
        block = jnp.concatenate(halves, axis=1).astype(BF16)
        ref[...] = block.reshape(rows, cols, channels)


def column_backward_kernel(order, me_ref, right_ref, *refs):
    chips = len(order)
    in_refs, out_refs = refs[:chips], refs[chips : chips + 2]
    by_column_ref, wide, wide_out = refs[chips + 2 :]
    cols, count, _ = right_ref.shape
    me = me_ref[0]
    load_columns(of_pair(received_views(me, in_refs, order), 0), wide)
    for k in range(cols):
        grad = column(wide, k, count, cols)
        by_column_ref[k] = grad
        store_column(wide_out, k, count, cols, dot(right_ref[k], grad, ((0,), (0,))))
    send_columns(wide_out, block_views(me, out_refs))


def column_forward_kernel(order, me_ref, right_ref, grad_ref, after_ref, *refs):
    chips = len(order)
    in_refs, out_refs = refs[:chips], refs[chips : chips + 2]
    packed_ref, wide, wide_out = refs[chips + 2 :]
    cols, count, _ = right_ref.shape
    channels = packed_ref.shape[1]
    terms = []
    me = me_ref[0]
    load_columns(of_pair(received_views(me, in_refs, order), 1), wide)
    for k in range(cols):
        mixed = column(wide, k, count, cols)
        store_column(wide_out, k, count, cols, dot(right_ref[k], mixed, ((1,), (0,))))
        terms.append(dot(grad_ref[k], mixed, ((1,), (1,))))
        if len(terms) == channels // count:
            row = k * count // channels * count
            packed_ref[row : row + count] = jnp.concatenate(terms, axis=1).astype(BF16)
            terms = []
    send_columns(wide_out, block_views(me, out_refs))


def gather_kernel(me_ref, *refs):
    out_ref, n = refs[-1], 0
    _, rows, cols, channels = out_ref.shape
    size = rows * cols
    for ref in refs[:-1]:
        if ref.ndim == 2:
            for start in range(0, ref.shape[0], size):
                out_ref[n] = ref[start : start + size].reshape(rows, cols, channels)
                n += 1
            continue
        for e in range(ref.shape[0]):
            out_ref[n] = ref[e]
            n += 1


def load_rows(order, me, parts, hold):
    left = 2 * len(order) - parts[1].shape[0]
    for n, t in enumerate(order):
        for e in range(2):
            j = 2 * n + e
            hold[:, me ^ (2 * t + e)] = parts[0][j] if j < left else parts[1][j - left]


def row_of(hold, i):
    seq, cols, channels = hold.shape[1:]
    return hold[i].reshape(seq * cols, channels)


def row_backward_kernel(
    order, me_ref, left_ref, values_ref, first_ref, second_ref, signal_ref, term_ref, hold
):
    load_rows(order, me_ref[0], (first_ref, second_ref), hold)
    for i in range(left_ref.shape[0]):
        grad = row_of(hold, i)
        signal_ref[i] = dot(left_ref[i], grad, ((0,), (0,))).astype(BF16)
        term_ref[i] = dot(grad, values_ref[i], ((1,), (1,))).astype(BF16)


def factor_sum_kernel(
    order,
    me_ref,
    term_ref,
    values_ref,
    first_ref,
    second_ref,
    packed_ref,
    left_out_ref,
    right_out_ref,
    hold,
):
    load_rows(order, me_ref[0], (first_ref, second_ref), hold)
    for i in range(term_ref.shape[0]):
        other = dot(row_of(hold, i), values_ref[i], ((1,), (1,))).astype(BF16)
        left_out_ref[i] = (term_ref[i].astype(F32) + other.astype(F32)).astype(BF16)
    cols, count, _ = right_out_ref.shape
    height, channels = packed_ref.shape
    blocks = 2 * len(order) - second_ref.shape[0]
    size = height // (first_ref.shape[0] - blocks)
    share = channels // count
    for n in range(height // count):
        block, row = blocks + n * count // size, n * count % size
        other = first_ref[block].reshape(size, channels)[row : row + count]
        total = packed_ref[n * count : (n + 1) * count].astype(F32) + other.astype(F32)
        for q in range(share):
            right_out_ref[n * share + q] = total[:, q * count : (q + 1) * count].astype(BF16)


def output_kernel(order, me_ref, gate_ref, cotangent_ref, *refs):
    chips = len(order)
    out_ref, grad_ref = refs[chips:]
    for c, ref in received_views(me_ref[0], refs[:chips], order):
        second = ref[...].astype(F32)
        out_ref[:, c] = (gate_ref[:, c].astype(F32) * second).astype(BF16)
        grad_ref[:, c] = (cotangent_ref[:, c].astype(F32) * second).astype(BF16)


def direct_shards(signal, gating, upstream, left_factor, right_factor):
    seq = lax.axis_size("seq")
    chips = seq // 2
    rows, block_len = left_factor.shape[:2]
    cols, count = right_factor.shape[:2]
    channels = signal.shape[2]
    me = lax.axis_index("seq").astype(jnp.int32).reshape(1)
    values = signal.reshape(rows, block_len, channels)
    gate = gating.reshape(rows, seq, cols, channels)
    cotangent = upstream.reshape(rows, seq, cols, channels)

    def shape(*dims):
        return jax.ShapeDtypeStruct(dims, BF16)

    one_ahead, two_ahead, all_far = orders(chips)

    def ordered(kernel, order):
        return functools.partial(kernel, order)

    block = (rows, cols, channels)
    whole = shape(rows, seq, cols, channels)
    by_row = shape(rows, block_len, channels)
    left = shape(*left_factor.shape)
    right = shape(*right_factor.shape)
    wide = pltpu.VMEM((channels // 128, count * cols, 128), F32)
    row_flops = 2 * rows * block_len * block_len * channels
    column_flops = 2 * cols * count * count * channels

    def pack(own, swapped):
        return list(call(pack_kernel, me, [own, swapped], [shape(2, *own.shape[1:])] * chips))

    hold = pltpu.VMEM(whole.shape, BF16)
    halves = [shape(chips, *block)] * 2
    last = one_ahead[-1]
    own, other = call(
        product_kernel,
        me,
        [gate, cotangent],
        halves,
        [hold, hold, pltpu.SemaphoreType.DMA((2, rows))],
        unblocked=range(2),
        vmem=60,
    )
    own_mixed, other_mixed = call(
        mix_kernel, me, [left_factor, after(values, own)], halves, [hold], row_flops
    )
    *messages, mixed_last = call(
        pack_pairs_kernel,
        me,
        [own, permute(other, 1), own_mixed, permute(other_mixed, 1)],
        [shape(2, 2, *block)] * last + [shape(2, *block)] * 2,
    )
    other_values = swap_sequences(after(values, messages[0]))
    columns = listed(exchange(messages), one_ahead)
    mixed_last = permute(after(mixed_last, columns[1:-2] + columns[-1:]), 2 * last)
    own, other, grad_column = call(
        ordered(column_backward_kernel, one_ahead),
        me,
        [right_factor, *columns],
        [shape(chips, *block)] * 2 + [shape(cols, count, channels)],
        [wide, wide],
        column_flops,
    )
    back = exchange(pack(own, permute(after(other, mixed_last), 1)))
    columns[-1] = mixed_last
    packed_right = shape(cols * count * count // channels, channels)
    own, other, right_part = call(
        ordered(column_forward_kernel, one_ahead),
        me,
        [right_factor, grad_column, other_values, *columns],
        [shape(chips, *block)] * 2 + [packed_right],
        [wide, wide],
        2 * column_flops,
        unblocked=[2],
    )
    back = listed(back, two_ahead)
    ahead = chips // 2 + 1
    messages = pack(own, permute(after(other, back[1:ahead]), 1))
    done = [(t, permute(messages[t], 2 * t)) for t in all_far[1:2]]
    back[-1] = after(back[-1], [block for _, block in done])
    extra = packed_right.size // math.prod(block)
    (first_part,) = call(
        gather_kernel, me, [*back[:ahead], right_part], [shape(2 * ahead + extra, *block)]
    )
    (second_part,) = call(
        gather_kernel, me, back[ahead:], [shape(2 * (chips - ahead), *block)]
    )
    other_first = swap_sequences(first_part)
    other_second = swap_sequences(second_part)
    grad_signal, left_term = call(
        ordered(row_backward_kernel, two_ahead),
        me,
        [left_factor, values, first_part, second_part],
        [by_row, left],
        [hold],
        2 * row_flops,
    )
    grad_left, grad_right = call(
        ordered(factor_sum_kernel, two_ahead),
        me,
        [left_term, other_values, other_first, other_second, right_part],
        [left, right],
        [hold],
        row_flops,
    )
    last = all_far[-1]
    messages[last] = after(messages[last], grad_left)
    second = listed(exchange(messages, done), all_far)
    output, grad_gate = call(
        ordered(output_kernel, all_far), me, [gate, cotangent, *second], [whole, whole]
    )
    return (
        output.reshape(signal.shape),
        grad_gate.reshape(signal.shape),
        grad_signal.reshape(signal.shape),
        grad_left,
        grad_right,
    )


def plain_shards(signal, gating, upstream, left_factor, right_factor):
    seq = lax.axis_size("seq")
    rows, block_len = left_factor.shape[:2]
    cols, block_count = right_factor.shape[:2]
    channels = signal.shape[2]
    values = signal.reshape(rows, block_len, channels)
    gate = gating.reshape(rows, block_len, channels)
    cotangent = upstream.reshape(rows, block_len, channels)

    def einsum(spec, a, b):
        return jnp.einsum(spec, a, b, preferred_element_type=F32).astype(BF16)

    def all_to_all(blocks):
        return lax.all_to_all(blocks, "seq", split_axis=0, concat_axis=0, tiled=True)

    def to_columns(by_row):
        blocks = by_row.reshape(rows, seq, cols, channels).transpose(1, 0, 2, 3)
        return all_to_all(blocks).reshape(block_count, cols, channels)

    def to_rows(by_column):
        blocks = all_to_all(by_column.reshape(seq, rows, cols, channels))
        return blocks.transpose(1, 0, 2, 3).reshape(rows, block_len, channels)

    grad_rows = (cotangent.astype(F32) * gate.astype(F32)).astype(BF16)
    grad_column = to_columns(grad_rows)
    other_values = swap_sequences(values)
    mixed_column = to_columns(einsum("ikj,ijd->ikd", left_factor, values))
    grad_back = to_rows(einsum("kmi,mkd->ikd", right_factor, grad_column))
    second_rows = to_rows(einsum("kmi,ikd->mkd", right_factor, mixed_column))
    right_part = einsum("mkd,ikd->kmi", grad_column, mixed_column)
    other_right = swap_sequences(right_part)
    other_grad_back = swap_sequences(grad_back)
    grad_signal = einsum("ikj,ikd->ijd", left_factor, grad_back)
    left_term = einsum("ikd,ijd->ikj", grad_back, values)
    other_left = einsum("ikd,ijd->ikj", other_grad_back, other_values)
    grad_left = (left_term.astype(F32) + other_left.astype(F32)).astype(BF16)
    grad_right = (right_part.astype(F32) + other_right.astype(F32)).astype(BF16)
    wide = second_rows.astype(F32)
    output = (gate.astype(F32) * wide).astype(BF16)
    grad_gate = (cotangent.astype(F32) * wide).astype(BF16)
    return (
        output.reshape(signal.shape),
        grad_gate.reshape(signal.shape),
        grad_signal.reshape(signal.shape),
        grad_left,
        grad_right,
    )


def shards(signal, gating, upstream, left_factor, right_factor):
    seq = lax.axis_size("seq")
    cols = right_factor.shape[0]
    direct = seq in (8, 16) and cols % 32 == 0
    run = direct_shards if direct else plain_shards
    return run(signal, gating, upstream, left_factor, right_factor)


def solution(mesh):
    by_position = P("dp", "seq", None)
    by_block = P("seq", None, None)
    return jax.shard_map(
        shards,
        mesh=mesh,
        in_specs=(by_position,) * 3 + (by_block,) * 2,
        out_specs=(by_position,) * 3 + (by_block,) * 2,
        check_vma=False,
    )
```

```python
import functools
import math

import jax
import jax.numpy as jnp
from jax import lax
from jax.experimental import pallas as pl
from jax.experimental.pallas import tpu as pltpu
from jax.sharding import PartitionSpec as P

BF16 = jnp.bfloat16
F32 = jnp.float32
MIB = 1024 * 1024


def swap_sequences(array):
    return lax.ppermute(array, "dp", [(0, 1), (1, 0)])


def after(array, earlier):
    return lax.optimization_barrier((array, earlier))[0]


def orders(chips):
    half = chips // 2
    near = list(range(1, half))
    far = list(range(half, chips, 2)) + list(range(half + 1, chips, 2))
    return [0] + far[:1] + near + far[1:], [0] + near + far, [0] + far + near


def permute(array, offset):
    seq = lax.axis_size("seq")
    return lax.ppermute(array, "seq", [(i, i ^ offset) for i in range(seq)])


def exchange(messages, done=()):
    done = dict(done)
    return [
        done[t] if t in done else permute(message, 2 * t) if t else message
        for t, message in enumerate(messages)
    ]


def listed(messages, order):
    return [messages[t] for t in order]


def call(kernel, me, inputs, out_shapes, scratch=(), flops=0, unblocked=(), vmem=32):
    whole = pl.BlockSpec(memory_space=pltpu.VMEM)
    moved = sum(x.size * x.dtype.itemsize for x in (*inputs, *out_shapes))
    in_specs = [
        pl.BlockSpec(memory_space=pl.ANY) if n in unblocked else whole for n in range(len(inputs))
    ]
    return pl.pallas_call(
        kernel,
        out_shape=out_shapes,
        in_specs=[pl.BlockSpec(memory_space=pltpu.SMEM)] + in_specs,
        out_specs=[whole] * len(out_shapes),
        scratch_shapes=scratch,
        compiler_params=pltpu.CompilerParams(vmem_limit_bytes=vmem * MIB),
        name=getattr(kernel, "func", kernel).__name__,
        cost_estimate=pl.CostEstimate(flops=flops, bytes_accessed=moved, transcendentals=0),
    )(me, *inputs)


def dot(a, b, contract):
    return lax.dot_general(a, b, (contract, ((), ())), preferred_element_type=F32)


def block_views(me, refs):
    return [(me ^ (2 * t + e), ref.at[t]) for e, ref in enumerate(refs) for t in range(ref.shape[0])]


def received_views(me, refs, order):
    return [(me ^ (2 * t + e), ref.at[e]) for t, ref in zip(order, refs) for e in range(2)]


def product_kernel(me_ref, gate_hbm, cotangent_hbm, *refs):
    out_refs, (gate, cotangent, sems) = refs[:2], refs[2:]
    rows = gate.shape[0]
    loads = [
        [
            pltpu.make_async_copy(source.at[i], target.at[i], sems.at[n, i])
            for n, (source, target) in enumerate(((gate_hbm, gate), (cotangent_hbm, cotangent)))
        ]
        for i in range(rows)
    ]
    for pair in loads:
        for load in pair:
            load.start()
    blocks = block_views(me_ref[0], out_refs)
    for i in range(rows):
        for load in loads[i]:
            load.wait()
        for c, ref in blocks:
            ref[i] = (gate[i, c].astype(F32) * cotangent[i, c].astype(F32)).astype(BF16)


def mix_kernel(me_ref, left_ref, values_ref, *refs):
    out_refs, hold = refs[:2], refs[2]
    rows, seq, cols, channels = hold.shape
    for i in range(rows):
        mixed = dot(left_ref[i], values_ref[i], ((1,), (0,)))
        hold[i] = mixed.astype(BF16).reshape(seq, cols, channels)
    for c, ref in block_views(me_ref[0], out_refs):
        ref[...] = hold[:, c]


def pack_kernel(me_ref, own_ref, other_ref, *out_refs):
    for t, out_ref in enumerate(out_refs):
        out_ref[0] = own_ref[t]
        out_ref[1] = other_ref[t]


def pack_pairs_kernel(me_ref, *refs):
    pairs, out_refs = (refs[0:2], refs[2:4]), refs[4:]
    last = len(out_refs) - 2
    for which, pair in enumerate(pairs):
        for e, ref in enumerate(pair):
            for t in range(last):
                out_refs[t][e, which] = ref[t]
            out_refs[last + which][e] = ref[last]


def of_pair(views, which):
    return [(c, ref.at[which] if len(ref.shape) == 4 else ref) for c, ref in views]


def load_columns(blocks, wide):
    rows, cols, channels = blocks[0][1].shape
    size = rows * cols
    for c, ref in blocks:
        block = ref[...].reshape(size, channels).astype(F32)
        start = pl.multiple_of(c * size, size)
        for h in range(channels // 128):
            wide[h, pl.ds(start, size), :] = block[:, h * 128 : (h + 1) * 128]


def column(wide, k, count, cols):
    halves = [wide[h, pl.ds(k, count, stride=cols), :] for h in range(wide.shape[0])]
    return jnp.concatenate(halves, axis=1).astype(BF16)


def store_column(wide, k, count, cols, value):
    for h in range(wide.shape[0]):
        wide[h, pl.ds(k, count, stride=cols), :] = value[:, h * 128 : (h + 1) * 128]


def send_columns(wide, blocks):
    rows, cols, channels = blocks[0][1].shape
    size = rows * cols
    for c, ref in blocks:
        start = pl.multiple_of(c * size, size)
        halves = [wide[h, pl.ds(start, size), :] for h in range(wide.shape[0])]
        block = jnp.concatenate(halves, axis=1).astype(BF16)
        ref[...] = block.reshape(rows, cols, channels)


def column_backward_kernel(order, me_ref, right_ref, *refs):
    chips = len(order)
    in_refs, out_refs = refs[:chips], refs[chips : chips + 2]
    by_column_ref, wide, wide_out = refs[chips + 2 :]
    cols, count, _ = right_ref.shape
    me = me_ref[0]
    load_columns(of_pair(received_views(me, in_refs, order), 0), wide)
    for k in range(cols):
        grad = column(wide, k, count, cols)
        by_column_ref[k] = grad
        store_column(wide_out, k, count, cols, dot(right_ref[k], grad, ((0,), (0,))))
    send_columns(wide_out, block_views(me, out_refs))


def column_forward_kernel(order, me_ref, right_ref, grad_ref, *refs):
    chips = len(order)
    in_refs, out_refs = refs[:chips], refs[chips : chips + 2]
    packed_ref, wide, wide_out = refs[chips + 2 :]
    cols, count, _ = right_ref.shape
    channels = packed_ref.shape[1]
    terms = []
    me = me_ref[0]
    load_columns(of_pair(received_views(me, in_refs, order), 1), wide)
    for k in range(cols):
        mixed = column(wide, k, count, cols)
        store_column(wide_out, k, count, cols, dot(right_ref[k], mixed, ((1,), (0,))))
        terms.append(dot(grad_ref[k], mixed, ((1,), (1,))))
        if len(terms) == channels // count:
            row = k * count // channels * count
            packed_ref[row : row + count] = jnp.concatenate(terms, axis=1).astype(BF16)
            terms = []
    send_columns(wide_out, block_views(me, out_refs))


def gather_kernel(me_ref, *refs):
    out_ref, n = refs[-1], 0
    _, rows, cols, channels = out_ref.shape
    size = rows * cols
    for ref in refs[:-1]:
        if ref.ndim == 2:
            for start in range(0, ref.shape[0], size):
                out_ref[n] = ref[start : start + size].reshape(rows, cols, channels)
                n += 1
            continue
        for e in range(ref.shape[0]):
            out_ref[n] = ref[e]
            n += 1


def load_rows(order, me, parts, hold):
    left = 2 * len(order) - parts[1].shape[0]
    for n, t in enumerate(order):
        for e in range(2):
            j = 2 * n + e
            hold[:, me ^ (2 * t + e)] = parts[0][j] if j < left else parts[1][j - left]


def row_of(hold, i):
    seq, cols, channels = hold.shape[1:]
    return hold[i].reshape(seq * cols, channels)


def row_backward_kernel(
    order, me_ref, left_ref, values_ref, first_ref, second_ref, signal_ref, term_ref, hold
):
    load_rows(order, me_ref[0], (first_ref, second_ref), hold)
    for i in range(left_ref.shape[0]):
        grad = row_of(hold, i)
        signal_ref[i] = dot(left_ref[i], grad, ((0,), (0,))).astype(BF16)
        term_ref[i] = dot(grad, values_ref[i], ((1,), (1,))).astype(BF16)


def factor_sum_kernel(
    order,
    me_ref,
    term_ref,
    values_ref,
    first_ref,
    second_ref,
    packed_ref,
    left_out_ref,
    right_out_ref,
    hold,
):
    load_rows(order, me_ref[0], (first_ref, second_ref), hold)
    for i in range(term_ref.shape[0]):
        other = dot(row_of(hold, i), values_ref[i], ((1,), (1,))).astype(BF16)
        left_out_ref[i] = (term_ref[i].astype(F32) + other.astype(F32)).astype(BF16)
    cols, count, _ = right_out_ref.shape
    height, channels = packed_ref.shape
    blocks = 2 * len(order) - second_ref.shape[0]
    size = height // (first_ref.shape[0] - blocks)
    share = channels // count
    for n in range(height // count):
        block, row = blocks + n * count // size, n * count % size
        other = first_ref[block].reshape(size, channels)[row : row + count]
        total = packed_ref[n * count : (n + 1) * count].astype(F32) + other.astype(F32)
        for q in range(share):
            right_out_ref[n * share + q] = total[:, q * count : (q + 1) * count].astype(BF16)


def output_kernel(order, me_ref, gate_ref, cotangent_ref, *refs):
    chips = len(order)
    out_ref, grad_ref = refs[chips:]
    for c, ref in received_views(me_ref[0], refs[:chips], order):
        second = ref[...].astype(F32)
        out_ref[:, c] = (gate_ref[:, c].astype(F32) * second).astype(BF16)
        grad_ref[:, c] = (cotangent_ref[:, c].astype(F32) * second).astype(BF16)


def direct_shards(signal, gating, upstream, left_factor, right_factor):
    seq = lax.axis_size("seq")
    chips = seq // 2
    rows, block_len = left_factor.shape[:2]
    cols, count = right_factor.shape[:2]
    channels = signal.shape[2]
    me = lax.axis_index("seq").astype(jnp.int32).reshape(1)
    values = signal.reshape(rows, block_len, channels)
    gate = gating.reshape(rows, seq, cols, channels)
    cotangent = upstream.reshape(rows, seq, cols, channels)

    def shape(*dims):
        return jax.ShapeDtypeStruct(dims, BF16)

    one_ahead, near_ahead, all_far = orders(chips)

    def ordered(kernel, order):
        return functools.partial(kernel, order)

    block = (rows, cols, channels)
    whole = shape(rows, seq, cols, channels)
    by_row = shape(rows, block_len, channels)
    left = shape(*left_factor.shape)
    right = shape(*right_factor.shape)
    wide = pltpu.VMEM((channels // 128, count * cols, 128), F32)
    row_flops = 2 * rows * block_len * block_len * channels
    column_flops = 2 * cols * count * count * channels

    def pack(own, swapped):
        return list(call(pack_kernel, me, [own, swapped], [shape(2, *own.shape[1:])] * chips))

    hold = pltpu.VMEM(whole.shape, BF16)
    halves = [shape(chips, *block)] * 2
    last = one_ahead[-1]
    own, other = call(
        product_kernel,
        me,
        [gate, cotangent],
        halves,
        [hold, hold, pltpu.SemaphoreType.DMA((2, rows))],
        unblocked=range(2),
        vmem=60,
    )
    own_mixed, other_mixed = call(
        mix_kernel, me, [left_factor, after(values, own)], halves, [hold], row_flops
    )
    *messages, mixed_last = call(
        pack_pairs_kernel,
        me,
        [own, permute(other, 1), own_mixed, permute(other_mixed, 1)],
        [shape(2, 2, *block)] * last + [shape(2, *block)] * 2,
    )
    done = [(t, permute(messages[t], 2 * t)) for t in (one_ahead[2], one_ahead[3])]
    messages[one_ahead[-2]] = after(messages[one_ahead[-2]], done[0][1])
    messages[last] = after(messages[last], done[1][1])
    columns = listed(exchange(messages, done), one_ahead)
    other_values = swap_sequences(after(values, columns[-3]))
    in_before = [*columns[1:-2], columns[-1]]
    mixed_last = permute(after(mixed_last, in_before), 2 * last)
    own, other, grad_column = call(
        ordered(column_backward_kernel, one_ahead),
        me,
        [right_factor, *columns],
        [shape(chips, *block)] * 2 + [shape(cols, count, channels)],
        [wide, wide],
        column_flops,
    )
    back = exchange(pack(own, permute(after(other, mixed_last), 1)))
    columns[-1] = mixed_last
    packed_right = shape(cols * count * count // channels, channels)
    own, other, right_part = call(
        ordered(column_forward_kernel, one_ahead),
        me,
        [right_factor, grad_column, *columns],
        [shape(chips, *block)] * 2 + [packed_right],
        [wide, wide],
        2 * column_flops,
    )
    back = listed(back, near_ahead)
    ahead = chips // 2
    messages = pack(own, permute(after(other, [other_values, *back[1 : ahead + 2]]), 1))
    done = [(t, permute(messages[t], 2 * t)) for t in all_far[1:2]]
    back[-1] = after(back[-1], [block for _, block in done])
    extra = packed_right.size // math.prod(block)
    (first_part,) = call(
        gather_kernel, me, [*back[:ahead], right_part], [shape(2 * ahead + extra, *block)]
    )
    (second_part,) = call(
        gather_kernel, me, back[ahead:], [shape(2 * (chips - ahead), *block)]
    )
    other_first = swap_sequences(first_part)
    other_second = swap_sequences(second_part)
    grad_signal, left_term = call(
        ordered(row_backward_kernel, near_ahead),
        me,
        [left_factor, values, first_part, second_part],
        [by_row, left],
        [hold],
        2 * row_flops,
    )
    grad_left, grad_right = call(
        ordered(factor_sum_kernel, near_ahead),
        me,
        [left_term, other_values, other_first, other_second, right_part],
        [left, right],
        [hold],
        row_flops,
    )
    last = all_far[-1]
    messages[last] = after(messages[last], grad_left)
    second = listed(exchange(messages, done), all_far)
    output, grad_gate = call(
        ordered(output_kernel, all_far), me, [gate, cotangent, *second], [whole, whole]
    )
    return (
        output.reshape(signal.shape),
        grad_gate.reshape(signal.shape),
        grad_signal.reshape(signal.shape),
        grad_left,
        grad_right,
    )


def plain_shards(signal, gating, upstream, left_factor, right_factor):
    seq = lax.axis_size("seq")
    rows, block_len = left_factor.shape[:2]
    cols, block_count = right_factor.shape[:2]
    channels = signal.shape[2]
    values = signal.reshape(rows, block_len, channels)
    gate = gating.reshape(rows, block_len, channels)
    cotangent = upstream.reshape(rows, block_len, channels)

    def einsum(spec, a, b):
        return jnp.einsum(spec, a, b, preferred_element_type=F32).astype(BF16)

    def all_to_all(blocks):
        return lax.all_to_all(blocks, "seq", split_axis=0, concat_axis=0, tiled=True)

    def to_columns(by_row):
        blocks = by_row.reshape(rows, seq, cols, channels).transpose(1, 0, 2, 3)
        return all_to_all(blocks).reshape(block_count, cols, channels)

    def to_rows(by_column):
        blocks = all_to_all(by_column.reshape(seq, rows, cols, channels))
        return blocks.transpose(1, 0, 2, 3).reshape(rows, block_len, channels)

    grad_rows = (cotangent.astype(F32) * gate.astype(F32)).astype(BF16)
    grad_column = to_columns(grad_rows)
    other_values = swap_sequences(values)
    mixed_column = to_columns(einsum("ikj,ijd->ikd", left_factor, values))
    grad_back = to_rows(einsum("kmi,mkd->ikd", right_factor, grad_column))
    second_rows = to_rows(einsum("kmi,ikd->mkd", right_factor, mixed_column))
    right_part = einsum("mkd,ikd->kmi", grad_column, mixed_column)
    other_right = swap_sequences(right_part)
    other_grad_back = swap_sequences(grad_back)
    grad_signal = einsum("ikj,ikd->ijd", left_factor, grad_back)
    left_term = einsum("ikd,ijd->ikj", grad_back, values)
    other_left = einsum("ikd,ijd->ikj", other_grad_back, other_values)
    grad_left = (left_term.astype(F32) + other_left.astype(F32)).astype(BF16)
    grad_right = (right_part.astype(F32) + other_right.astype(F32)).astype(BF16)
    wide = second_rows.astype(F32)
    output = (gate.astype(F32) * wide).astype(BF16)
    grad_gate = (cotangent.astype(F32) * wide).astype(BF16)
    return (
        output.reshape(signal.shape),
        grad_gate.reshape(signal.shape),
        grad_signal.reshape(signal.shape),
        grad_left,
        grad_right,
    )


def shards(signal, gating, upstream, left_factor, right_factor):
    seq = lax.axis_size("seq")
    cols = right_factor.shape[0]
    direct = seq in (8, 16) and cols % 32 == 0
    run = direct_shards if direct else plain_shards
    return run(signal, gating, upstream, left_factor, right_factor)


def solution(mesh):
    by_position = P("dp", "seq", None)
    by_block = P("seq", None, None)
    return jax.shard_map(
        shards,
        mesh=mesh,
        in_specs=(by_position,) * 3 + (by_block,) * 2,
        out_specs=(by_position,) * 3 + (by_block,) * 2,
        check_vma=False,
    )
```

```python
import functools
import math

import jax
import jax.numpy as jnp
from jax import lax
from jax.experimental import pallas as pl
from jax.experimental.pallas import tpu as pltpu
from jax.sharding import PartitionSpec as P

BF16 = jnp.bfloat16
F32 = jnp.float32
MIB = 1024 * 1024


def swap_sequences(array):
    return lax.ppermute(array, "dp", [(0, 1), (1, 0)])


def after(array, earlier):
    return lax.optimization_barrier((array, earlier))[0]


def orders(chips):
    half = chips // 2
    near = list(range(1, half))
    far = list(range(half, chips, 2)) + list(range(half + 1, chips, 2))
    return [0] + far[:1] + near + far[1:], [0] + far + near


def permute(array, offset):
    seq = lax.axis_size("seq")
    return lax.ppermute(array, "seq", [(i, i ^ offset) for i in range(seq)])


def exchange(messages, done=()):
    done = dict(done)
    return [
        done[t] if t in done else permute(message, 2 * t) if t else message
        for t, message in enumerate(messages)
    ]


def listed(messages, order):
    return [messages[t] for t in order]


def call(kernel, me, inputs, out_shapes, scratch=(), flops=0, unblocked=(), vmem=32):
    whole = pl.BlockSpec(memory_space=pltpu.VMEM)
    moved = sum(x.size * x.dtype.itemsize for x in (*inputs, *out_shapes))
    in_specs = [
        pl.BlockSpec(memory_space=pl.ANY) if n in unblocked else whole for n in range(len(inputs))
    ]
    return pl.pallas_call(
        kernel,
        out_shape=out_shapes,
        in_specs=[pl.BlockSpec(memory_space=pltpu.SMEM)] + in_specs,
        out_specs=[whole] * len(out_shapes),
        scratch_shapes=scratch,
        compiler_params=pltpu.CompilerParams(vmem_limit_bytes=vmem * MIB),
        name=getattr(kernel, "func", kernel).__name__,
        cost_estimate=pl.CostEstimate(flops=flops, bytes_accessed=moved, transcendentals=0),
    )(me, *inputs)


def dot(a, b, contract):
    return lax.dot_general(a, b, (contract, ((), ())), preferred_element_type=F32)


def block_views(me, refs):
    return [(me ^ (2 * t + e), ref.at[t]) for e, ref in enumerate(refs) for t in range(ref.shape[0])]


def received_views(me, refs, order):
    return [(me ^ (2 * t + e), ref.at[e]) for t, ref in zip(order, refs) for e in range(2)]


def product_kernel(me_ref, gate_hbm, cotangent_hbm, *refs):
    out_refs, (gate, cotangent, sems) = refs[:2], refs[2:]
    rows = gate.shape[0]
    loads = [
        [
            pltpu.make_async_copy(source.at[i], target.at[i], sems.at[n, i])
            for n, (source, target) in enumerate(((gate_hbm, gate), (cotangent_hbm, cotangent)))
        ]
        for i in range(rows)
    ]
    for pair in loads:
        for load in pair:
            load.start()
    blocks = block_views(me_ref[0], out_refs)
    for i in range(rows):
        for load in loads[i]:
            load.wait()
        for c, ref in blocks:
            ref[i] = (gate[i, c].astype(F32) * cotangent[i, c].astype(F32)).astype(BF16)


def mix_kernel(me_ref, left_ref, values_ref, *refs):
    out_refs, hold = refs[:2], refs[2]
    rows, seq, cols, channels = hold.shape
    for i in range(rows):
        mixed = dot(left_ref[i], values_ref[i], ((1,), (0,)))
        hold[i] = mixed.astype(BF16).reshape(seq, cols, channels)
    for c, ref in block_views(me_ref[0], out_refs):
        ref[...] = hold[:, c]


def pack_kernel(me_ref, own_ref, other_ref, *out_refs):
    for t, out_ref in enumerate(out_refs):
        out_ref[0] = own_ref[t]
        out_ref[1] = other_ref[t]


def pack_pairs_kernel(me_ref, *refs):
    pairs, out_refs = (refs[0:2], refs[2:4]), refs[4:]
    last = len(out_refs) - 2
    for which, pair in enumerate(pairs):
        for e, ref in enumerate(pair):
            for t in range(last):
                out_refs[t][e, which] = ref[t]
            out_refs[last + which][e] = ref[last]


def of_pair(views, which):
    return [(c, ref.at[which] if len(ref.shape) == 4 else ref) for c, ref in views]


def load_columns(blocks, wide):
    rows, cols, channels = blocks[0][1].shape
    size = rows * cols
    for c, ref in blocks:
        block = ref[...].reshape(size, channels).astype(F32)
        start = pl.multiple_of(c * size, size)
        for h in range(channels // 128):
            wide[h, pl.ds(start, size), :] = block[:, h * 128 : (h + 1) * 128]


def column(wide, k, count, cols):
    halves = [wide[h, pl.ds(k, count, stride=cols), :] for h in range(wide.shape[0])]
    return jnp.concatenate(halves, axis=1).astype(BF16)


def store_column(wide, k, count, cols, value):
    for h in range(wide.shape[0]):
        wide[h, pl.ds(k, count, stride=cols), :] = value[:, h * 128 : (h + 1) * 128]


def send_columns(wide, blocks):
    rows, cols, channels = blocks[0][1].shape
    size = rows * cols
    for c, ref in blocks:
        start = pl.multiple_of(c * size, size)
        halves = [wide[h, pl.ds(start, size), :] for h in range(wide.shape[0])]
        block = jnp.concatenate(halves, axis=1).astype(BF16)
        ref[...] = block.reshape(rows, cols, channels)


def column_backward_kernel(order, direct, me_ref, right_ref, *refs):
    chips = len(order)
    in_refs, own_ref, other_ref = refs[:chips], refs[chips], refs[chips + 1]
    direct_refs, (by_column_ref, wide, wide_out) = refs[chips + 2 : -3], refs[-3:]
    cols, count, _ = right_ref.shape
    me = me_ref[0]
    load_columns(of_pair(received_views(me, in_refs, order), 0), wide)
    for k in range(cols):
        grad = column(wide, k, count, cols)
        by_column_ref[k] = grad
        store_column(wide_out, k, count, cols, dot(right_ref[k], grad, ((0,), (0,))))
    views = [(me ^ (2 * t + e), direct_refs[2 * n + e]) for n, t in enumerate(direct) for e in range(2)]
    others = [t for t in range(chips) if t not in direct]
    for e, ref in enumerate((own_ref, other_ref)):
        views += [(me ^ (2 * t + e), ref.at[n]) for n, t in enumerate(others)]
    send_columns(wide_out, views)


def column_forward_kernel(order, me_ref, right_ref, grad_ref, after_ref, *refs):
    chips = len(order)
    in_refs, out_refs = refs[:chips], refs[chips : chips + 2]
    packed_ref, wide, wide_out = refs[chips + 2 :]
    cols, count, _ = right_ref.shape
    channels = packed_ref.shape[1]
    terms = []
    me = me_ref[0]
    load_columns(of_pair(received_views(me, in_refs, order), 1), wide)
    for k in range(cols):
        mixed = column(wide, k, count, cols)
        store_column(wide_out, k, count, cols, dot(right_ref[k], mixed, ((1,), (0,))))
        terms.append(dot(grad_ref[k], mixed, ((1,), (1,))))
        if len(terms) == channels // count:
            row = k * count // channels * count
            packed_ref[row : row + count] = jnp.concatenate(terms, axis=1).astype(BF16)
            terms = []
    send_columns(wide_out, block_views(me, out_refs))


def gather_kernel(me_ref, *refs):
    out_ref, n = refs[-1], 0
    _, rows, cols, channels = out_ref.shape
    size = rows * cols
    for ref in refs[:-1]:
        if ref.ndim == 3:
            out_ref[n] = ref[...]
            n += 1
            continue
        if ref.ndim == 2:
            for start in range(0, ref.shape[0], size):
                out_ref[n] = ref[start : start + size].reshape(rows, cols, channels)
                n += 1
            continue
        for e in range(2):
            out_ref[n] = ref[e]
            n += 1


def load_rows(order, me, parts, hold):
    left = 2 * len(order) - parts[1].shape[0]
    for n, t in enumerate(order):
        for e in range(2):
            j = 2 * n + e
            hold[:, me ^ (2 * t + e)] = parts[0][j] if j < left else parts[1][j - left]


def row_of(hold, i):
    seq, cols, channels = hold.shape[1:]
    return hold[i].reshape(seq * cols, channels)


def row_backward_kernel(
    order, me_ref, left_ref, values_ref, first_ref, second_ref, signal_ref, term_ref, hold
):
    load_rows(order, me_ref[0], (first_ref, second_ref), hold)
    for i in range(left_ref.shape[0]):
        grad = row_of(hold, i)
        signal_ref[i] = dot(left_ref[i], grad, ((0,), (0,))).astype(BF16)
        term_ref[i] = dot(grad, values_ref[i], ((1,), (1,))).astype(BF16)


def factor_sum_kernel(
    order,
    me_ref,
    term_ref,
    values_ref,
    first_ref,
    second_ref,
    packed_ref,
    left_out_ref,
    right_out_ref,
    hold,
):
    load_rows(order, me_ref[0], (first_ref, second_ref), hold)
    for i in range(term_ref.shape[0]):
        other = dot(row_of(hold, i), values_ref[i], ((1,), (1,))).astype(BF16)
        left_out_ref[i] = (term_ref[i].astype(F32) + other.astype(F32)).astype(BF16)
    cols, count, _ = right_out_ref.shape
    height, channels = packed_ref.shape
    blocks = 2 * len(order) - second_ref.shape[0]
    size = height // (first_ref.shape[0] - blocks)
    share = channels // count
    for n in range(height // count):
        block, row = blocks + n * count // size, n * count % size
        other = first_ref[block].reshape(size, channels)[row : row + count]
        total = packed_ref[n * count : (n + 1) * count].astype(F32) + other.astype(F32)
        for q in range(share):
            right_out_ref[n * share + q] = total[:, q * count : (q + 1) * count].astype(BF16)


def output_kernel(order, me_ref, gate_ref, cotangent_ref, *refs):
    chips = len(order)
    out_ref, grad_ref = refs[chips:]
    for c, ref in received_views(me_ref[0], refs[:chips], order):
        second = ref[...].astype(F32)
        out_ref[:, c] = (gate_ref[:, c].astype(F32) * second).astype(BF16)
        grad_ref[:, c] = (cotangent_ref[:, c].astype(F32) * second).astype(BF16)


def direct_shards(signal, gating, upstream, left_factor, right_factor):
    seq = lax.axis_size("seq")
    chips = seq // 2
    rows, block_len = left_factor.shape[:2]
    cols, count = right_factor.shape[:2]
    channels = signal.shape[2]
    me = lax.axis_index("seq").astype(jnp.int32).reshape(1)
    values = signal.reshape(rows, block_len, channels)
    gate = gating.reshape(rows, seq, cols, channels)
    cotangent = upstream.reshape(rows, seq, cols, channels)

    def shape(*dims):
        return jax.ShapeDtypeStruct(dims, BF16)

    one_ahead, all_far = orders(chips)

    def ordered(kernel, order):
        return functools.partial(kernel, order)

    block = (rows, cols, channels)
    whole = shape(rows, seq, cols, channels)
    by_row = shape(rows, block_len, channels)
    left = shape(*left_factor.shape)
    right = shape(*right_factor.shape)
    wide = pltpu.VMEM((channels // 128, count * cols, 128), F32)
    row_flops = 2 * rows * block_len * block_len * channels
    column_flops = 2 * cols * count * count * channels

    def pack(own, swapped):
        return list(call(pack_kernel, me, [own, swapped], [shape(2, *own.shape[1:])] * own.shape[0]))

    hold = pltpu.VMEM(whole.shape, BF16)
    halves = [shape(chips, *block)] * 2
    last = one_ahead[-1]
    own, other = call(
        product_kernel,
        me,
        [gate, cotangent],
        halves,
        [hold, hold, pltpu.SemaphoreType.DMA((2, rows))],
        unblocked=range(2),
        vmem=60,
    )
    own_mixed, other_mixed = call(
        mix_kernel, me, [left_factor, after(values, own)], halves, [hold], row_flops
    )
    *messages, mixed_last = call(
        pack_pairs_kernel,
        me,
        [own, permute(other, 1), own_mixed, permute(other_mixed, 1)],
        [shape(2, 2, *block)] * last + [shape(2, *block)] * 2,
    )
    other_values = swap_sequences(after(values, messages[0]))
    columns = listed(exchange(messages), one_ahead)
    mixed_last = permute(after(mixed_last, columns[1:-2] + columns[-1:]), 2 * last)
    direct = all_far[1:3]
    others = [t for t in range(chips) if t not in direct]
    own, other, *blocks, grad_column = call(
        functools.partial(column_backward_kernel, one_ahead, direct),
        me,
        [right_factor, *columns],
        [shape(len(others), *block)] * 2
        + [shape(*block)] * 2 * len(direct)
        + [shape(cols, count, channels)],
        [wide, wide],
        column_flops,
    )
    blocks = [permute(x, 2 * direct[n // 2] + n % 2) for n, x in enumerate(blocks)]
    own_back, other_back = own, other
    columns[-1] = mixed_last
    packed_right = shape(cols * count * count // channels, channels)
    own, other, right_part = call(
        ordered(column_forward_kernel, one_ahead),
        me,
        [right_factor, grad_column, other_values, *columns],
        [shape(chips, *block)] * 2 + [packed_right],
        [wide, wide],
        2 * column_flops,
        unblocked=[2],
    )
    other_back = after(other_back, [mixed_last, *blocks, right_part])
    back = pack(own_back, permute(other_back, 1))
    back = dict(zip(others, back))
    third = all_far[3]
    back[third] = permute(back[third], 2 * third)
    for t in all_far[4:]:
        message = after(back[t], back[third]) if t in all_far[-1:] else back[t]
        back[t] = permute(message, 2 * t)
    back = [back[t] for t in all_far if t in others]
    messages = pack(own, permute(after(other, blocks), 1))
    done = []
    extra = packed_right.size // math.prod(block)
    sent_first = [back[0], *blocks]
    ahead = 1 + len(direct)
    (first_part,) = call(
        gather_kernel, me, [*sent_first, right_part], [shape(2 * ahead + extra, *block)]
    )
    (second_part,) = call(
        gather_kernel, me, back[1:], [shape(2 * (chips - ahead), *block)]
    )
    other_first = swap_sequences(first_part)
    other_second = swap_sequences(second_part)
    grad_signal, left_term = call(
        ordered(row_backward_kernel, all_far),
        me,
        [left_factor, values, first_part, second_part],
        [by_row, left],
        [hold],
        2 * row_flops,
    )
    grad_left, grad_right = call(
        ordered(factor_sum_kernel, all_far),
        me,
        [left_term, other_values, other_first, other_second, right_part],
        [left, right],
        [hold],
        row_flops,
    )
    last = all_far[-1]
    messages[last] = after(messages[last], left_term)
    second = listed(exchange(messages, done), all_far)
    output, grad_gate = call(
        ordered(output_kernel, all_far), me, [gate, cotangent, *second], [whole, whole]
    )
    return (
        output.reshape(signal.shape),
        grad_gate.reshape(signal.shape),
        grad_signal.reshape(signal.shape),
        grad_left,
        grad_right,
    )


def plain_shards(signal, gating, upstream, left_factor, right_factor):
    seq = lax.axis_size("seq")
    rows, block_len = left_factor.shape[:2]
    cols, block_count = right_factor.shape[:2]
    channels = signal.shape[2]
    values = signal.reshape(rows, block_len, channels)
    gate = gating.reshape(rows, block_len, channels)
    cotangent = upstream.reshape(rows, block_len, channels)

    def einsum(spec, a, b):
        return jnp.einsum(spec, a, b, preferred_element_type=F32).astype(BF16)

    def all_to_all(blocks):
        return lax.all_to_all(blocks, "seq", split_axis=0, concat_axis=0, tiled=True)

    def to_columns(by_row):
        blocks = by_row.reshape(rows, seq, cols, channels).transpose(1, 0, 2, 3)
        return all_to_all(blocks).reshape(block_count, cols, channels)

    def to_rows(by_column):
        blocks = all_to_all(by_column.reshape(seq, rows, cols, channels))
        return blocks.transpose(1, 0, 2, 3).reshape(rows, block_len, channels)

    grad_rows = (cotangent.astype(F32) * gate.astype(F32)).astype(BF16)
    grad_column = to_columns(grad_rows)
    other_values = swap_sequences(values)
    mixed_column = to_columns(einsum("ikj,ijd->ikd", left_factor, values))
    grad_back = to_rows(einsum("kmi,mkd->ikd", right_factor, grad_column))
    second_rows = to_rows(einsum("kmi,ikd->mkd", right_factor, mixed_column))
    right_part = einsum("mkd,ikd->kmi", grad_column, mixed_column)
    other_right = swap_sequences(right_part)
    other_grad_back = swap_sequences(grad_back)
    grad_signal = einsum("ikj,ikd->ijd", left_factor, grad_back)
    left_term = einsum("ikd,ijd->ikj", grad_back, values)
    other_left = einsum("ikd,ijd->ikj", other_grad_back, other_values)
    grad_left = (left_term.astype(F32) + other_left.astype(F32)).astype(BF16)
    grad_right = (right_part.astype(F32) + other_right.astype(F32)).astype(BF16)
    wide = second_rows.astype(F32)
    output = (gate.astype(F32) * wide).astype(BF16)
    grad_gate = (cotangent.astype(F32) * wide).astype(BF16)
    return (
        output.reshape(signal.shape),
        grad_gate.reshape(signal.shape),
        grad_signal.reshape(signal.shape),
        grad_left,
        grad_right,
    )


def shards(signal, gating, upstream, left_factor, right_factor):
    seq = lax.axis_size("seq")
    cols = right_factor.shape[0]
    direct = seq in (8, 16) and cols % 32 == 0
    run = direct_shards if direct else plain_shards
    return run(signal, gating, upstream, left_factor, right_factor)


def solution(mesh):
    by_position = P("dp", "seq", None)
    by_block = P("seq", None, None)
    return jax.shard_map(
        shards,
        mesh=mesh,
        in_specs=(by_position,) * 3 + (by_block,) * 2,
        out_specs=(by_position,) * 3 + (by_block,) * 2,
        check_vma=False,
    )
```

```python
import functools
import math

import jax
import jax.numpy as jnp
from jax import lax
from jax.experimental import pallas as pl
from jax.experimental.pallas import tpu as pltpu
from jax.sharding import PartitionSpec as P

BF16 = jnp.bfloat16
F32 = jnp.float32
MIB = 1024 * 1024


def swap_sequences(array):
    return lax.ppermute(array, "dp", [(0, 1), (1, 0)])


def after(array, earlier):
    return lax.optimization_barrier((array, earlier))[0]


def orders(chips):
    half = chips // 2
    near = list(range(1, half))
    far = list(range(half, chips, 2)) + list(range(half + 1, chips, 2))
    mixed = far[:1] + near[:-1] + far[1:-1] + near[-1:] + far[-1:]
    return [0] + far[:1] + near + far[1:], [0] + mixed, [0] + far + near


def permute(array, offset):
    seq = lax.axis_size("seq")
    return lax.ppermute(array, "seq", [(i, i ^ offset) for i in range(seq)])


def exchange(messages, done=()):
    done = dict(done)
    return [
        done[t] if t in done else permute(message, 2 * t) if t else message
        for t, message in enumerate(messages)
    ]


def listed(messages, order):
    return [messages[t] for t in order]


def call(kernel, me, inputs, out_shapes, scratch=(), flops=0, unblocked=(), vmem=32):
    whole = pl.BlockSpec(memory_space=pltpu.VMEM)
    moved = sum(x.size * x.dtype.itemsize for x in (*inputs, *out_shapes))
    in_specs = [
        pl.BlockSpec(memory_space=pl.ANY) if n in unblocked else whole for n in range(len(inputs))
    ]
    return pl.pallas_call(
        kernel,
        out_shape=out_shapes,
        in_specs=[pl.BlockSpec(memory_space=pltpu.SMEM)] + in_specs,
        out_specs=[whole] * len(out_shapes),
        scratch_shapes=scratch,
        compiler_params=pltpu.CompilerParams(vmem_limit_bytes=vmem * MIB),
        name=getattr(kernel, "func", kernel).__name__,
        cost_estimate=pl.CostEstimate(flops=flops, bytes_accessed=moved, transcendentals=0),
    )(me, *inputs)


def dot(a, b, contract):
    return lax.dot_general(a, b, (contract, ((), ())), preferred_element_type=F32)


def block_views(me, refs):
    return [(me ^ (2 * t + e), ref.at[t]) for e, ref in enumerate(refs) for t in range(ref.shape[0])]


def received_views(me, refs, order):
    return [(me ^ (2 * t + e), ref.at[e]) for t, ref in zip(order, refs) for e in range(2)]


def product_kernel(me_ref, gate_hbm, cotangent_hbm, *refs):
    out_refs, (gate, cotangent, sems) = refs[:2], refs[2:]
    rows = gate.shape[0]
    loads = [
        [
            pltpu.make_async_copy(source.at[i], target.at[i], sems.at[n, i])
            for n, (source, target) in enumerate(((gate_hbm, gate), (cotangent_hbm, cotangent)))
        ]
        for i in range(rows)
    ]
    for pair in loads:
        for load in pair:
            load.start()
    blocks = block_views(me_ref[0], out_refs)
    for i in range(rows):
        for load in loads[i]:
            load.wait()
        for c, ref in blocks:
            ref[i] = (gate[i, c].astype(F32) * cotangent[i, c].astype(F32)).astype(BF16)


def mix_kernel(me_ref, left_ref, values_ref, *refs):
    out_refs, hold = refs[:2], refs[2]
    rows, seq, cols, channels = hold.shape
    for i in range(rows):
        mixed = dot(left_ref[i], values_ref[i], ((1,), (0,)))
        hold[i] = mixed.astype(BF16).reshape(seq, cols, channels)
    for c, ref in block_views(me_ref[0], out_refs):
        ref[...] = hold[:, c]


def pack_kernel(me_ref, own_ref, other_ref, *out_refs):
    for t, out_ref in enumerate(out_refs):
        out_ref[0] = own_ref[t]
        out_ref[1] = other_ref[t]


def pack_pairs_kernel(me_ref, *refs):
    pairs, out_refs = (refs[0:2], refs[2:4]), refs[4:]
    last = len(out_refs) - 2
    for which, pair in enumerate(pairs):
        for e, ref in enumerate(pair):
            for t in range(last):
                out_refs[t][e, which] = ref[t]
            out_refs[last + which][e] = ref[last]


def of_pair(views, which):
    return [(c, ref.at[which] if len(ref.shape) == 4 else ref) for c, ref in views]


def load_columns(blocks, wide):
    rows, cols, channels = blocks[0][1].shape
    size = rows * cols
    for c, ref in blocks:
        block = ref[...].reshape(size, channels).astype(F32)
        start = pl.multiple_of(c * size, size)
        for h in range(channels // 128):
            wide[h, pl.ds(start, size), :] = block[:, h * 128 : (h + 1) * 128]


def column(wide, k, count, cols):
    halves = [wide[h, pl.ds(k, count, stride=cols), :] for h in range(wide.shape[0])]
    return jnp.concatenate(halves, axis=1).astype(BF16)


def store_column(wide, k, count, cols, value):
    for h in range(wide.shape[0]):
        wide[h, pl.ds(k, count, stride=cols), :] = value[:, h * 128 : (h + 1) * 128]


def send_columns(wide, blocks):
    rows, cols, channels = blocks[0][1].shape
    size = rows * cols
    for c, ref in blocks:
        start = pl.multiple_of(c * size, size)
        halves = [wide[h, pl.ds(start, size), :] for h in range(wide.shape[0])]
        block = jnp.concatenate(halves, axis=1).astype(BF16)
        ref[...] = block.reshape(rows, cols, channels)


def column_backward_kernel(order, me_ref, right_ref, *refs):
    chips = len(order)
    in_refs, out_refs = refs[:chips], refs[chips : chips + 2]
    by_column_ref, wide, wide_out = refs[chips + 2 :]
    cols, count, _ = right_ref.shape
    me = me_ref[0]
    load_columns(of_pair(received_views(me, in_refs, order), 0), wide)
    for k in range(cols):
        grad = column(wide, k, count, cols)
        by_column_ref[k] = grad
        store_column(wide_out, k, count, cols, dot(right_ref[k], grad, ((0,), (0,))))
    send_columns(wide_out, block_views(me, out_refs))


def column_forward_kernel(order, me_ref, right_ref, grad_ref, after_ref, *refs):
    chips = len(order)
    in_refs, out_refs = refs[:chips], refs[chips : chips + 2]
    packed_ref, wide, wide_out = refs[chips + 2 :]
    cols, count, _ = right_ref.shape
    channels = packed_ref.shape[1]
    terms = []
    me = me_ref[0]
    load_columns(of_pair(received_views(me, in_refs, order), 1), wide)
    for k in range(cols):
        mixed = column(wide, k, count, cols)
        store_column(wide_out, k, count, cols, dot(right_ref[k], mixed, ((1,), (0,))))
        terms.append(dot(grad_ref[k], mixed, ((1,), (1,))))
        if len(terms) == channels // count:
            row = k * count // channels * count
            packed_ref[row : row + count] = jnp.concatenate(terms, axis=1).astype(BF16)
            terms = []
    send_columns(wide_out, block_views(me, out_refs))


def gather_kernel(me_ref, *refs):
    out_ref, n = refs[-1], 0
    _, rows, cols, channels = out_ref.shape
    size = rows * cols
    for ref in refs[:-1]:
        if ref.ndim == 2:
            for start in range(0, ref.shape[0], size):
                out_ref[n] = ref[start : start + size].reshape(rows, cols, channels)
                n += 1
            continue
        for e in range(ref.shape[0]):
            out_ref[n] = ref[e]
            n += 1


def load_rows(order, me, parts, hold):
    left = 2 * len(order) - parts[1].shape[0]
    for n, t in enumerate(order):
        for e in range(2):
            j = 2 * n + e
            hold[:, me ^ (2 * t + e)] = parts[0][j] if j < left else parts[1][j - left]


def row_of(hold, i):
    seq, cols, channels = hold.shape[1:]
    return hold[i].reshape(seq * cols, channels)


def row_backward_kernel(
    order, me_ref, left_ref, values_ref, first_ref, second_ref, signal_ref, term_ref, hold
):
    load_rows(order, me_ref[0], (first_ref, second_ref), hold)
    for i in range(left_ref.shape[0]):
        grad = row_of(hold, i)
        signal_ref[i] = dot(left_ref[i], grad, ((0,), (0,))).astype(BF16)
        term_ref[i] = dot(grad, values_ref[i], ((1,), (1,))).astype(BF16)


def factor_sum_kernel(
    order,
    me_ref,
    term_ref,
    values_ref,
    first_ref,
    second_ref,
    packed_ref,
    left_out_ref,
    right_out_ref,
    hold,
):
    load_rows(order, me_ref[0], (first_ref, second_ref), hold)
    for i in range(term_ref.shape[0]):
        other = dot(row_of(hold, i), values_ref[i], ((1,), (1,))).astype(BF16)
        left_out_ref[i] = (term_ref[i].astype(F32) + other.astype(F32)).astype(BF16)
    cols, count, _ = right_out_ref.shape
    height, channels = packed_ref.shape
    blocks = 2 * len(order) - second_ref.shape[0]
    size = height // (first_ref.shape[0] - blocks)
    share = channels // count
    for n in range(height // count):
        block, row = blocks + n * count // size, n * count % size
        other = first_ref[block].reshape(size, channels)[row : row + count]
        total = packed_ref[n * count : (n + 1) * count].astype(F32) + other.astype(F32)
        for q in range(share):
            right_out_ref[n * share + q] = total[:, q * count : (q + 1) * count].astype(BF16)


def output_kernel(order, me_ref, gate_ref, cotangent_ref, *refs):
    chips = len(order)
    out_ref, grad_ref = refs[chips:]
    for c, ref in received_views(me_ref[0], refs[:chips], order):
        second = ref[...].astype(F32)
        out_ref[:, c] = (gate_ref[:, c].astype(F32) * second).astype(BF16)
        grad_ref[:, c] = (cotangent_ref[:, c].astype(F32) * second).astype(BF16)


def direct_shards(signal, gating, upstream, left_factor, right_factor):
    seq = lax.axis_size("seq")
    chips = seq // 2
    rows, block_len = left_factor.shape[:2]
    cols, count = right_factor.shape[:2]
    channels = signal.shape[2]
    me = lax.axis_index("seq").astype(jnp.int32).reshape(1)
    values = signal.reshape(rows, block_len, channels)
    gate = gating.reshape(rows, seq, cols, channels)
    cotangent = upstream.reshape(rows, seq, cols, channels)

    def shape(*dims):
        return jax.ShapeDtypeStruct(dims, BF16)

    one_ahead, few_ahead, all_far = orders(chips)

    def ordered(kernel, order):
        return functools.partial(kernel, order)

    block = (rows, cols, channels)
    whole = shape(rows, seq, cols, channels)
    by_row = shape(rows, block_len, channels)
    left = shape(*left_factor.shape)
    right = shape(*right_factor.shape)
    wide = pltpu.VMEM((channels // 128, count * cols, 128), F32)
    row_flops = 2 * rows * block_len * block_len * channels
    column_flops = 2 * cols * count * count * channels

    def pack(own, swapped):
        return list(call(pack_kernel, me, [own, swapped], [shape(2, *own.shape[1:])] * chips))

    hold = pltpu.VMEM(whole.shape, BF16)
    halves = [shape(chips, *block)] * 2
    last = one_ahead[-1]
    own, other = call(
        product_kernel,
        me,
        [gate, cotangent],
        halves,
        [hold, hold, pltpu.SemaphoreType.DMA((2, rows))],
        unblocked=range(2),
        vmem=60,
    )
    own_mixed, other_mixed = call(
        mix_kernel, me, [left_factor, after(values, own)], halves, [hold], row_flops
    )
    *messages, mixed_last = call(
        pack_pairs_kernel,
        me,
        [own, permute(other, 1), own_mixed, permute(other_mixed, 1)],
        [shape(2, 2, *block)] * last + [shape(2, *block)] * 2,
    )
    other_values = swap_sequences(after(values, messages[0]))
    columns = listed(exchange(messages), one_ahead)
    mixed_last = permute(after(mixed_last, columns[1:-2] + columns[-1:]), 2 * last)
    own, other, grad_column = call(
        ordered(column_backward_kernel, one_ahead),
        me,
        [right_factor, *columns],
        [shape(chips, *block)] * 2 + [shape(cols, count, channels)],
        [wide, wide],
        column_flops,
    )
    back = exchange(pack(own, permute(after(other, mixed_last), 1)))
    columns[-1] = mixed_last
    packed_right = shape(cols * count * count // channels, channels)
    own, other, right_part = call(
        ordered(column_forward_kernel, one_ahead),
        me,
        [right_factor, grad_column, other_values, *columns],
        [shape(chips, *block)] * 2 + [packed_right],
        [wide, wide],
        2 * column_flops,
        unblocked=[2],
    )
    back = listed(back, few_ahead)
    ahead = chips // 2
    messages = pack(own, permute(after(other, back[1:ahead]), 1))
    done = [(t, permute(messages[t], 2 * t)) for t in all_far[1:2]]
    back[-1] = after(back[-1], [block for _, block in done])
    extra = packed_right.size // math.prod(block)
    (first_part,) = call(
        gather_kernel, me, [*back[:ahead], right_part], [shape(2 * ahead + extra, *block)]
    )
    (second_part,) = call(
        gather_kernel, me, back[ahead:], [shape(2 * (chips - ahead), *block)]
    )
    other_first = swap_sequences(first_part)
    other_second = swap_sequences(second_part)
    grad_signal, left_term = call(
        ordered(row_backward_kernel, few_ahead),
        me,
        [left_factor, values, first_part, second_part],
        [by_row, left],
        [hold],
        2 * row_flops,
    )
    grad_left, grad_right = call(
        ordered(factor_sum_kernel, few_ahead),
        me,
        [left_term, other_values, other_first, other_second, right_part],
        [left, right],
        [hold],
        row_flops,
    )
    last = all_far[-1]
    messages[last] = after(messages[last], grad_left)
    second = listed(exchange(messages, done), all_far)
    output, grad_gate = call(
        ordered(output_kernel, all_far), me, [gate, cotangent, *second], [whole, whole]
    )
    return (
        output.reshape(signal.shape),
        grad_gate.reshape(signal.shape),
        grad_signal.reshape(signal.shape),
        grad_left,
        grad_right,
    )


def plain_shards(signal, gating, upstream, left_factor, right_factor):
    seq = lax.axis_size("seq")
    rows, block_len = left_factor.shape[:2]
    cols, block_count = right_factor.shape[:2]
    channels = signal.shape[2]
    values = signal.reshape(rows, block_len, channels)
    gate = gating.reshape(rows, block_len, channels)
    cotangent = upstream.reshape(rows, block_len, channels)

    def einsum(spec, a, b):
        return jnp.einsum(spec, a, b, preferred_element_type=F32).astype(BF16)

    def all_to_all(blocks):
        return lax.all_to_all(blocks, "seq", split_axis=0, concat_axis=0, tiled=True)

    def to_columns(by_row):
        blocks = by_row.reshape(rows, seq, cols, channels).transpose(1, 0, 2, 3)
        return all_to_all(blocks).reshape(block_count, cols, channels)

    def to_rows(by_column):
        blocks = all_to_all(by_column.reshape(seq, rows, cols, channels))
        return blocks.transpose(1, 0, 2, 3).reshape(rows, block_len, channels)

    grad_rows = (cotangent.astype(F32) * gate.astype(F32)).astype(BF16)
    grad_column = to_columns(grad_rows)
    other_values = swap_sequences(values)
    mixed_column = to_columns(einsum("ikj,ijd->ikd", left_factor, values))
    grad_back = to_rows(einsum("kmi,mkd->ikd", right_factor, grad_column))
    second_rows = to_rows(einsum("kmi,ikd->mkd", right_factor, mixed_column))
    right_part = einsum("mkd,ikd->kmi", grad_column, mixed_column)
    other_right = swap_sequences(right_part)
    other_grad_back = swap_sequences(grad_back)
    grad_signal = einsum("ikj,ikd->ijd", left_factor, grad_back)
    left_term = einsum("ikd,ijd->ikj", grad_back, values)
    other_left = einsum("ikd,ijd->ikj", other_grad_back, other_values)
    grad_left = (left_term.astype(F32) + other_left.astype(F32)).astype(BF16)
    grad_right = (right_part.astype(F32) + other_right.astype(F32)).astype(BF16)
    wide = second_rows.astype(F32)
    output = (gate.astype(F32) * wide).astype(BF16)
    grad_gate = (cotangent.astype(F32) * wide).astype(BF16)
    return (
        output.reshape(signal.shape),
        grad_gate.reshape(signal.shape),
        grad_signal.reshape(signal.shape),
        grad_left,
        grad_right,
    )


def shards(signal, gating, upstream, left_factor, right_factor):
    seq = lax.axis_size("seq")
    cols = right_factor.shape[0]
    direct = seq in (8, 16) and cols % 32 == 0
    run = direct_shards if direct else plain_shards
    return run(signal, gating, upstream, left_factor, right_factor)


def solution(mesh):
    by_position = P("dp", "seq", None)
    by_block = P("seq", None, None)
    return jax.shard_map(
        shards,
        mesh=mesh,
        in_specs=(by_position,) * 3 + (by_block,) * 2,
        out_specs=(by_position,) * 3 + (by_block,) * 2,
        check_vma=False,
    )
```

```python
import functools
import math

import jax
import jax.numpy as jnp
from jax import lax
from jax.experimental import pallas as pl
from jax.experimental.pallas import tpu as pltpu
from jax.sharding import PartitionSpec as P

BF16 = jnp.bfloat16
F32 = jnp.float32
MIB = 1024 * 1024


def swap_sequences(array):
    return lax.ppermute(array, "dp", [(0, 1), (1, 0)])


def after(array, earlier):
    return lax.optimization_barrier((array, earlier))[0]


def orders(chips):
    half = chips // 2
    near = list(range(1, half))
    far = list(range(half, chips, 2)) + list(range(half + 1, chips, 2))
    mixed = far[:1] + near[:-1] + far[1:-1] + near[-1:] + far[-1:]
    return [0] + far[:1] + near + far[1:], [0] + mixed, [0] + far + near


def permute(array, offset):
    seq = lax.axis_size("seq")
    return lax.ppermute(array, "seq", [(i, i ^ offset) for i in range(seq)])


def exchange(messages, done=()):
    done = dict(done)
    return [
        done[t] if t in done else permute(message, 2 * t) if t else message
        for t, message in enumerate(messages)
    ]


def listed(messages, order):
    return [messages[t] for t in order]


def call(kernel, me, inputs, out_shapes, scratch=(), flops=0, unblocked=(), vmem=32):
    whole = pl.BlockSpec(memory_space=pltpu.VMEM)
    moved = sum(x.size * x.dtype.itemsize for x in (*inputs, *out_shapes))
    in_specs = [
        pl.BlockSpec(memory_space=pl.ANY) if n in unblocked else whole for n in range(len(inputs))
    ]
    return pl.pallas_call(
        kernel,
        out_shape=out_shapes,
        in_specs=[pl.BlockSpec(memory_space=pltpu.SMEM)] + in_specs,
        out_specs=[whole] * len(out_shapes),
        scratch_shapes=scratch,
        compiler_params=pltpu.CompilerParams(vmem_limit_bytes=vmem * MIB),
        name=getattr(kernel, "func", kernel).__name__,
        cost_estimate=pl.CostEstimate(flops=flops, bytes_accessed=moved, transcendentals=0),
    )(me, *inputs)


def dot(a, b, contract):
    return lax.dot_general(a, b, (contract, ((), ())), preferred_element_type=F32)


def block_views(me, refs):
    return [(me ^ (2 * t + e), ref.at[t]) for e, ref in enumerate(refs) for t in range(ref.shape[0])]


def received_views(me, refs, order):
    return [(me ^ (2 * t + e), ref.at[e]) for t, ref in zip(order, refs) for e in range(2)]


def product_kernel(me_ref, gate_hbm, cotangent_hbm, *refs):
    out_refs, (gate, cotangent, sems) = refs[:2], refs[2:]
    rows = gate.shape[0]
    loads = [
        [
            pltpu.make_async_copy(source.at[i], target.at[i], sems.at[n, i])
            for n, (source, target) in enumerate(((gate_hbm, gate), (cotangent_hbm, cotangent)))
        ]
        for i in range(rows)
    ]
    for pair in loads:
        for load in pair:
            load.start()
    blocks = block_views(me_ref[0], out_refs)
    for i in range(rows):
        for load in loads[i]:
            load.wait()
        for c, ref in blocks:
            ref[i] = (gate[i, c].astype(F32) * cotangent[i, c].astype(F32)).astype(BF16)


def mix_kernel(me_ref, left_ref, values_ref, *refs):
    out_refs, hold = refs[:2], refs[2]
    rows, seq, cols, channels = hold.shape
    for i in range(rows):
        mixed = dot(left_ref[i], values_ref[i], ((1,), (0,)))
        hold[i] = mixed.astype(BF16).reshape(seq, cols, channels)
    for c, ref in block_views(me_ref[0], out_refs):
        ref[...] = hold[:, c]


def pack_kernel(me_ref, own_ref, other_ref, *out_refs):
    for t, out_ref in enumerate(out_refs):
        out_ref[0] = own_ref[t]
        out_ref[1] = other_ref[t]


def pack_pairs_kernel(me_ref, *refs):
    pairs, out_refs = (refs[0:2], refs[2:4]), refs[4:]
    last = len(out_refs) - 2
    for which, pair in enumerate(pairs):
        for e, ref in enumerate(pair):
            for t in range(last):
                out_refs[t][e, which] = ref[t]
            out_refs[last + which][e] = ref[last]


def of_pair(views, which):
    return [(c, ref.at[which] if len(ref.shape) == 4 else ref) for c, ref in views]


def load_columns(blocks, wide):
    rows, cols, channels = blocks[0][1].shape
    size = rows * cols
    for c, ref in blocks:
        block = ref[...].reshape(size, channels).astype(F32)
        start = pl.multiple_of(c * size, size)
        for h in range(channels // 128):
            wide[h, pl.ds(start, size), :] = block[:, h * 128 : (h + 1) * 128]


def column(wide, k, count, cols):
    halves = [wide[h, pl.ds(k, count, stride=cols), :] for h in range(wide.shape[0])]
    return jnp.concatenate(halves, axis=1).astype(BF16)


def store_column(wide, k, count, cols, value):
    for h in range(wide.shape[0]):
        wide[h, pl.ds(k, count, stride=cols), :] = value[:, h * 128 : (h + 1) * 128]


def send_columns(wide, blocks):
    rows, cols, channels = blocks[0][1].shape
    size = rows * cols
    for c, ref in blocks:
        start = pl.multiple_of(c * size, size)
        halves = [wide[h, pl.ds(start, size), :] for h in range(wide.shape[0])]
        block = jnp.concatenate(halves, axis=1).astype(BF16)
        ref[...] = block.reshape(rows, cols, channels)


def column_backward_kernel(order, me_ref, right_ref, *refs):
    chips = len(order)
    in_refs, out_refs = refs[:chips], refs[chips : chips + 2]
    by_column_ref, wide, wide_out = refs[chips + 2 :]
    cols, count, _ = right_ref.shape
    me = me_ref[0]
    load_columns(of_pair(received_views(me, in_refs, order), 0), wide)
    for k in range(cols):
        grad = column(wide, k, count, cols)
        by_column_ref[k] = grad
        store_column(wide_out, k, count, cols, dot(right_ref[k], grad, ((0,), (0,))))
    send_columns(wide_out, block_views(me, out_refs))


def column_forward_kernel(order, me_ref, right_ref, grad_ref, after_ref, *refs):
    chips = len(order)
    in_refs, out_refs = refs[:chips], refs[chips : chips + 2]
    packed_ref, wide, wide_out = refs[chips + 2 :]
    cols, count, _ = right_ref.shape
    channels = packed_ref.shape[1]
    terms = []
    me = me_ref[0]
    load_columns(of_pair(received_views(me, in_refs, order), 1), wide)
    for k in range(cols):
        mixed = column(wide, k, count, cols)
        store_column(wide_out, k, count, cols, dot(right_ref[k], mixed, ((1,), (0,))))
        terms.append(dot(grad_ref[k], mixed, ((1,), (1,))))
        if len(terms) == channels // count:
            row = k * count // channels * count
            packed_ref[row : row + count] = jnp.concatenate(terms, axis=1).astype(BF16)
            terms = []
    send_columns(wide_out, block_views(me, out_refs))


def gather_kernel(me_ref, *refs):
    out_ref, n = refs[-1], 0
    _, rows, cols, channels = out_ref.shape
    size = rows * cols
    for ref in refs[:-1]:
        if ref.ndim == 2:
            for start in range(0, ref.shape[0], size):
                out_ref[n] = ref[start : start + size].reshape(rows, cols, channels)
                n += 1
            continue
        for e in range(ref.shape[0]):
            out_ref[n] = ref[e]
            n += 1


def load_rows(order, me, parts, hold):
    left = 2 * len(order) - parts[1].shape[0]
    for n, t in enumerate(order):
        for e in range(2):
            j = 2 * n + e
            hold[:, me ^ (2 * t + e)] = parts[0][j] if j < left else parts[1][j - left]


def row_of(hold, i):
    seq, cols, channels = hold.shape[1:]
    return hold[i].reshape(seq * cols, channels)


def row_backward_kernel(
    order, me_ref, left_ref, values_ref, first_ref, second_ref, signal_ref, term_ref, hold
):
    load_rows(order, me_ref[0], (first_ref, second_ref), hold)
    for i in range(left_ref.shape[0]):
        grad = row_of(hold, i)
        signal_ref[i] = dot(left_ref[i], grad, ((0,), (0,))).astype(BF16)
        term_ref[i] = dot(grad, values_ref[i], ((1,), (1,))).astype(BF16)


def factor_sum_kernel(
    order,
    me_ref,
    term_ref,
    values_ref,
    first_ref,
    second_ref,
    packed_ref,
    left_out_ref,
    right_out_ref,
    hold,
):
    load_rows(order, me_ref[0], (first_ref, second_ref), hold)
    for i in range(term_ref.shape[0]):
        other = dot(row_of(hold, i), values_ref[i], ((1,), (1,))).astype(BF16)
        left_out_ref[i] = (term_ref[i].astype(F32) + other.astype(F32)).astype(BF16)
    cols, count, _ = right_out_ref.shape
    height, channels = packed_ref.shape
    blocks = 2 * len(order) - second_ref.shape[0]
    size = height // (first_ref.shape[0] - blocks)
    share = channels // count
    for n in range(height // count):
        block, row = blocks + n * count // size, n * count % size
        other = first_ref[block].reshape(size, channels)[row : row + count]
        total = packed_ref[n * count : (n + 1) * count].astype(F32) + other.astype(F32)
        for q in range(share):
            right_out_ref[n * share + q] = total[:, q * count : (q + 1) * count].astype(BF16)


def output_kernel(order, me_ref, gate_ref, cotangent_ref, *refs):
    chips = len(order)
    out_ref, grad_ref = refs[chips:]
    for c, ref in received_views(me_ref[0], refs[:chips], order):
        second = ref[...].astype(F32)
        out_ref[:, c] = (gate_ref[:, c].astype(F32) * second).astype(BF16)
        grad_ref[:, c] = (cotangent_ref[:, c].astype(F32) * second).astype(BF16)


def direct_shards(signal, gating, upstream, left_factor, right_factor):
    seq = lax.axis_size("seq")
    chips = seq // 2
    rows, block_len = left_factor.shape[:2]
    cols, count = right_factor.shape[:2]
    channels = signal.shape[2]
    me = lax.axis_index("seq").astype(jnp.int32).reshape(1)
    values = signal.reshape(rows, block_len, channels)
    gate = gating.reshape(rows, seq, cols, channels)
    cotangent = upstream.reshape(rows, seq, cols, channels)

    def shape(*dims):
        return jax.ShapeDtypeStruct(dims, BF16)

    one_ahead, few_ahead, all_far = orders(chips)

    def ordered(kernel, order):
        return functools.partial(kernel, order)

    block = (rows, cols, channels)
    whole = shape(rows, seq, cols, channels)
    by_row = shape(rows, block_len, channels)
    left = shape(*left_factor.shape)
    right = shape(*right_factor.shape)
    wide = pltpu.VMEM((channels // 128, count * cols, 128), F32)
    row_flops = 2 * rows * block_len * block_len * channels
    column_flops = 2 * cols * count * count * channels

    def pack(own, swapped):
        return list(call(pack_kernel, me, [own, swapped], [shape(2, *own.shape[1:])] * chips))

    hold = pltpu.VMEM(whole.shape, BF16)
    halves = [shape(chips, *block)] * 2
    last = one_ahead[-1]
    own, other = call(
        product_kernel,
        me,
        [gate, cotangent],
        halves,
        [hold, hold, pltpu.SemaphoreType.DMA((2, rows))],
        unblocked=range(2),
        vmem=60,
    )
    own_mixed, other_mixed = call(
        mix_kernel, me, [left_factor, after(values, own)], halves, [hold], row_flops
    )
    *messages, mixed_last = call(
        pack_pairs_kernel,
        me,
        [own, permute(other, 1), own_mixed, permute(other_mixed, 1)],
        [shape(2, 2, *block)] * last + [shape(2, *block)] * 2,
    )
    other_values = swap_sequences(after(values, messages[0]))
    columns = listed(exchange(messages), one_ahead)
    mixed_last = permute(after(mixed_last, columns[1:-2] + columns[-1:]), 2 * last)
    own, other, grad_column = call(
        ordered(column_backward_kernel, one_ahead),
        me,
        [right_factor, *columns],
        [shape(chips, *block)] * 2 + [shape(cols, count, channels)],
        [wide, wide],
        column_flops,
    )
    back = exchange(pack(own, permute(after(other, mixed_last), 1)))
    columns[-1] = mixed_last
    packed_right = shape(cols * count * count // channels, channels)
    own, other, right_part = call(
        ordered(column_forward_kernel, one_ahead),
        me,
        [right_factor, grad_column, other_values, *columns],
        [shape(chips, *block)] * 2 + [packed_right],
        [wide, wide],
        2 * column_flops,
        unblocked=[2],
    )
    back = listed(back, few_ahead)
    ahead = chips // 2
    messages = pack(own, permute(after(other, back[1:ahead]), 1))
    done = [(t, permute(messages[t], 2 * t)) for t in all_far[1:3]]
    back[-1] = after(back[-1], [block for _, block in done])
    extra = packed_right.size // math.prod(block)
    (first_part,) = call(
        gather_kernel, me, [*back[:ahead], right_part], [shape(2 * ahead + extra, *block)]
    )
    (second_part,) = call(
        gather_kernel, me, back[ahead:], [shape(2 * (chips - ahead), *block)]
    )
    other_first = swap_sequences(first_part)
    other_second = swap_sequences(second_part)
    grad_signal, left_term = call(
        ordered(row_backward_kernel, few_ahead),
        me,
        [left_factor, values, first_part, second_part],
        [by_row, left],
        [hold],
        2 * row_flops,
    )
    grad_left, grad_right = call(
        ordered(factor_sum_kernel, few_ahead),
        me,
        [left_term, other_values, other_first, other_second, right_part],
        [left, right],
        [hold],
        row_flops,
    )
    last = all_far[-1]
    messages[last] = after(messages[last], grad_left)
    second = listed(exchange(messages, done), all_far)
    output, grad_gate = call(
        ordered(output_kernel, all_far), me, [gate, cotangent, *second], [whole, whole]
    )
    return (
        output.reshape(signal.shape),
        grad_gate.reshape(signal.shape),
        grad_signal.reshape(signal.shape),
        grad_left,
        grad_right,
    )


def plain_shards(signal, gating, upstream, left_factor, right_factor):
    seq = lax.axis_size("seq")
    rows, block_len = left_factor.shape[:2]
    cols, block_count = right_factor.shape[:2]
    channels = signal.shape[2]
    values = signal.reshape(rows, block_len, channels)
    gate = gating.reshape(rows, block_len, channels)
    cotangent = upstream.reshape(rows, block_len, channels)

    def einsum(spec, a, b):
        return jnp.einsum(spec, a, b, preferred_element_type=F32).astype(BF16)

    def all_to_all(blocks):
        return lax.all_to_all(blocks, "seq", split_axis=0, concat_axis=0, tiled=True)

    def to_columns(by_row):
        blocks = by_row.reshape(rows, seq, cols, channels).transpose(1, 0, 2, 3)
        return all_to_all(blocks).reshape(block_count, cols, channels)

    def to_rows(by_column):
        blocks = all_to_all(by_column.reshape(seq, rows, cols, channels))
        return blocks.transpose(1, 0, 2, 3).reshape(rows, block_len, channels)

    grad_rows = (cotangent.astype(F32) * gate.astype(F32)).astype(BF16)
    grad_column = to_columns(grad_rows)
    other_values = swap_sequences(values)
    mixed_column = to_columns(einsum("ikj,ijd->ikd", left_factor, values))
    grad_back = to_rows(einsum("kmi,mkd->ikd", right_factor, grad_column))
    second_rows = to_rows(einsum("kmi,ikd->mkd", right_factor, mixed_column))
    right_part = einsum("mkd,ikd->kmi", grad_column, mixed_column)
    other_right = swap_sequences(right_part)
    other_grad_back = swap_sequences(grad_back)
    grad_signal = einsum("ikj,ikd->ijd", left_factor, grad_back)
    left_term = einsum("ikd,ijd->ikj", grad_back, values)
    other_left = einsum("ikd,ijd->ikj", other_grad_back, other_values)
    grad_left = (left_term.astype(F32) + other_left.astype(F32)).astype(BF16)
    grad_right = (right_part.astype(F32) + other_right.astype(F32)).astype(BF16)
    wide = second_rows.astype(F32)
    output = (gate.astype(F32) * wide).astype(BF16)
    grad_gate = (cotangent.astype(F32) * wide).astype(BF16)
    return (
        output.reshape(signal.shape),
        grad_gate.reshape(signal.shape),
        grad_signal.reshape(signal.shape),
        grad_left,
        grad_right,
    )


def shards(signal, gating, upstream, left_factor, right_factor):
    seq = lax.axis_size("seq")
    cols = right_factor.shape[0]
    direct = seq in (8, 16) and cols % 32 == 0
    run = direct_shards if direct else plain_shards
    return run(signal, gating, upstream, left_factor, right_factor)


def solution(mesh):
    by_position = P("dp", "seq", None)
    by_block = P("seq", None, None)
    return jax.shard_map(
        shards,
        mesh=mesh,
        in_specs=(by_position,) * 3 + (by_block,) * 2,
        out_specs=(by_position,) * 3 + (by_block,) * 2,
        check_vma=False,
    )
```

```python
import functools
import math

import jax
import jax.numpy as jnp
from jax import lax
from jax.experimental import pallas as pl
from jax.experimental.pallas import tpu as pltpu
from jax.sharding import PartitionSpec as P

BF16 = jnp.bfloat16
F32 = jnp.float32
MIB = 1024 * 1024


def swap_sequences(array):
    return lax.ppermute(array, "dp", [(0, 1), (1, 0)])


def after(array, earlier):
    return lax.optimization_barrier((array, earlier))[0]


def orders(chips):
    half = chips // 2
    near = list(range(1, half))
    far = list(range(half, chips, 2)) + list(range(half + 1, chips, 2))
    mixed = far[:1] + near[:-1] + far[1:-1] + near[-1:] + far[-1:]
    return [0] + far[:1] + near + far[1:], [0] + mixed, [0] + far + near


def permute(array, offset):
    seq = lax.axis_size("seq")
    return lax.ppermute(array, "seq", [(i, i ^ offset) for i in range(seq)])


def exchange(messages, done=()):
    done = dict(done)
    return [
        done[t] if t in done else permute(message, 2 * t) if t else message
        for t, message in enumerate(messages)
    ]


def listed(messages, order):
    return [messages[t] for t in order]


def call(kernel, me, inputs, out_shapes, scratch=(), flops=0, unblocked=(), vmem=32, stored=True):
    whole = pl.BlockSpec(memory_space=pltpu.VMEM)
    moved = sum(x.size * x.dtype.itemsize for x in (*inputs, *out_shapes))
    in_specs = [
        pl.BlockSpec(memory_space=pl.ANY) if n in unblocked else whole for n in range(len(inputs))
    ]
    return pl.pallas_call(
        kernel,
        out_shape=out_shapes,
        in_specs=[pl.BlockSpec(memory_space=pltpu.SMEM)] + in_specs,
        out_specs=[whole if stored else pl.BlockSpec(memory_space=pl.ANY)] * len(out_shapes),
        scratch_shapes=scratch,
        compiler_params=pltpu.CompilerParams(vmem_limit_bytes=vmem * MIB),
        name=getattr(kernel, "func", kernel).__name__,
        cost_estimate=pl.CostEstimate(flops=flops, bytes_accessed=moved, transcendentals=0),
    )(me, *inputs)


def dot(a, b, contract):
    return lax.dot_general(a, b, (contract, ((), ())), preferred_element_type=F32)


def block_views(me, refs):
    return [(me ^ (2 * t + e), ref.at[t]) for e, ref in enumerate(refs) for t in range(ref.shape[0])]


def received_views(me, refs, order):
    return [(me ^ (2 * t + e), ref.at[e]) for t, ref in zip(order, refs) for e in range(2)]


def product_kernel(me_ref, gate_hbm, cotangent_hbm, *refs):
    out_refs, (gate, cotangent, sems) = refs[:2], refs[2:]
    rows = gate.shape[0]
    loads = [
        [
            pltpu.make_async_copy(source.at[i], target.at[i], sems.at[n, i])
            for n, (source, target) in enumerate(((gate_hbm, gate), (cotangent_hbm, cotangent)))
        ]
        for i in range(rows)
    ]
    for pair in loads:
        for load in pair:
            load.start()
    blocks = block_views(me_ref[0], out_refs)
    for i in range(rows):
        for load in loads[i]:
            load.wait()
        for c, ref in blocks:
            ref[i] = (gate[i, c].astype(F32) * cotangent[i, c].astype(F32)).astype(BF16)


def mix_kernel(me_ref, left_ref, values_ref, *refs):
    out_refs, hold = refs[:2], refs[2]
    rows, seq, cols, channels = hold.shape
    for i in range(rows):
        mixed = dot(left_ref[i], values_ref[i], ((1,), (0,)))
        hold[i] = mixed.astype(BF16).reshape(seq, cols, channels)
    for c, ref in block_views(me_ref[0], out_refs):
        ref[...] = hold[:, c]


def pack_kernel(me_ref, own_ref, other_ref, *out_refs):
    for t, out_ref in enumerate(out_refs):
        out_ref[0] = own_ref[t]
        out_ref[1] = other_ref[t]


def pack_pairs_kernel(me_ref, *refs):
    pairs, out_refs = (refs[0:2], refs[2:4]), refs[4:]
    last = len(out_refs) - 2
    for which, pair in enumerate(pairs):
        for e, ref in enumerate(pair):
            for t in range(last):
                out_refs[t][e, which] = ref[t]
            out_refs[last + which][e] = ref[last]


def of_pair(views, which):
    return [(c, ref.at[which] if len(ref.shape) == 4 else ref) for c, ref in views]


def load_columns(blocks, wide):
    rows, cols, channels = blocks[0][1].shape
    size = rows * cols
    for c, ref in blocks:
        block = ref[...].reshape(size, channels).astype(F32)
        start = pl.multiple_of(c * size, size)
        for h in range(channels // 128):
            wide[h, pl.ds(start, size), :] = block[:, h * 128 : (h + 1) * 128]


def column(wide, k, count, cols):
    halves = [wide[h, pl.ds(k, count, stride=cols), :] for h in range(wide.shape[0])]
    return jnp.concatenate(halves, axis=1).astype(BF16)


def store_column(wide, k, count, cols, value):
    for h in range(wide.shape[0]):
        wide[h, pl.ds(k, count, stride=cols), :] = value[:, h * 128 : (h + 1) * 128]


def send_columns(wide, blocks):
    rows, cols, channels = blocks[0][1].shape
    size = rows * cols
    for c, ref in blocks:
        start = pl.multiple_of(c * size, size)
        halves = [wide[h, pl.ds(start, size), :] for h in range(wide.shape[0])]
        block = jnp.concatenate(halves, axis=1).astype(BF16)
        ref[...] = block.reshape(rows, cols, channels)


def column_backward_kernel(order, me_ref, right_ref, *refs):
    chips = len(order)
    in_refs, out_refs = refs[:chips], refs[chips : chips + 2]
    by_column_ref, wide, wide_out = refs[chips + 2 :]
    cols, count, _ = right_ref.shape
    me = me_ref[0]
    load_columns(of_pair(received_views(me, in_refs, order), 0), wide)
    for k in range(cols):
        grad = column(wide, k, count, cols)
        by_column_ref[k] = grad
        store_column(wide_out, k, count, cols, dot(right_ref[k], grad, ((0,), (0,))))
    send_columns(wide_out, block_views(me, out_refs))


def column_forward_kernel(order, me_ref, right_ref, grad_ref, after_ref, *refs):
    chips = len(order)
    in_refs, out_refs = refs[:chips], refs[chips : chips + 2]
    packed_ref, wide, wide_out = refs[chips + 2 :]
    cols, count, _ = right_ref.shape
    channels = packed_ref.shape[1]
    terms = []
    me = me_ref[0]
    load_columns(of_pair(received_views(me, in_refs, order), 1), wide)
    for k in range(cols):
        mixed = column(wide, k, count, cols)
        store_column(wide_out, k, count, cols, dot(right_ref[k], mixed, ((1,), (0,))))
        terms.append(dot(grad_ref[k], mixed, ((1,), (1,))))
        if len(terms) == channels // count:
            row = k * count // channels * count
            packed_ref[row : row + count] = jnp.concatenate(terms, axis=1).astype(BF16)
            terms = []
    send_columns(wide_out, block_views(me, out_refs))


def gather_kernel(me_ref, *refs):
    out_ref, n = refs[-1], 0
    _, rows, cols, channels = out_ref.shape
    size = rows * cols
    for ref in refs[:-1]:
        if ref.ndim == 2:
            for start in range(0, ref.shape[0], size):
                out_ref[n] = ref[start : start + size].reshape(rows, cols, channels)
                n += 1
            continue
        for e in range(ref.shape[0]):
            out_ref[n] = ref[e]
            n += 1


def load_rows(order, me, parts, hold):
    left = 2 * len(order) - parts[1].shape[0]
    for n, t in enumerate(order):
        for e in range(2):
            j = 2 * n + e
            hold[:, me ^ (2 * t + e)] = parts[0][j] if j < left else parts[1][j - left]


def row_of(hold, i):
    seq, cols, channels = hold.shape[1:]
    return hold[i].reshape(seq * cols, channels)


def row_backward_kernel(
    order, me_ref, left_ref, values_ref, first_ref, second_ref, signal_ref, term_ref, hold
):
    load_rows(order, me_ref[0], (first_ref, second_ref), hold)
    for i in range(left_ref.shape[0]):
        grad = row_of(hold, i)
        signal_ref[i] = dot(left_ref[i], grad, ((0,), (0,))).astype(BF16)
        term_ref[i] = dot(grad, values_ref[i], ((1,), (1,))).astype(BF16)


def factor_sum_kernel(
    order,
    me_ref,
    term_ref,
    values_ref,
    first_ref,
    second_ref,
    packed_ref,
    left_out_ref,
    right_out_ref,
    hold,
):
    load_rows(order, me_ref[0], (first_ref, second_ref), hold)
    for i in range(term_ref.shape[0]):
        other = dot(row_of(hold, i), values_ref[i], ((1,), (1,))).astype(BF16)
        left_out_ref[i] = (term_ref[i].astype(F32) + other.astype(F32)).astype(BF16)
    cols, count, _ = right_out_ref.shape
    height, channels = packed_ref.shape
    blocks = 2 * len(order) - second_ref.shape[0]
    size = height // (first_ref.shape[0] - blocks)
    share = channels // count
    for n in range(height // count):
        block, row = blocks + n * count // size, n * count % size
        other = first_ref[block].reshape(size, channels)[row : row + count]
        total = packed_ref[n * count : (n + 1) * count].astype(F32) + other.astype(F32)
        for q in range(share):
            right_out_ref[n * share + q] = total[:, q * count : (q + 1) * count].astype(BF16)


def output_kernel(order, me_ref, gate_ref, cotangent_ref, *refs):
    chips = len(order)
    out_hbm, grad_hbm, out, grad, sems = refs[chips:]
    blocks = received_views(me_ref[0], refs[:chips], order)
    stores = []
    for i in range(out.shape[0]):
        for c, ref in blocks:
            second = ref[i].astype(F32)
            out[i, c] = (gate_ref[i, c].astype(F32) * second).astype(BF16)
            grad[i, c] = (cotangent_ref[i, c].astype(F32) * second).astype(BF16)
        for n, (source, target) in enumerate(((out, out_hbm), (grad, grad_hbm))):
            stores.append(pltpu.make_async_copy(source.at[i], target.at[i], sems.at[n, i]))
            stores[-1].start()
    for store in stores:
        store.wait()


def direct_shards(signal, gating, upstream, left_factor, right_factor):
    seq = lax.axis_size("seq")
    chips = seq // 2
    rows, block_len = left_factor.shape[:2]
    cols, count = right_factor.shape[:2]
    channels = signal.shape[2]
    me = lax.axis_index("seq").astype(jnp.int32).reshape(1)
    values = signal.reshape(rows, block_len, channels)
    gate = gating.reshape(rows, seq, cols, channels)
    cotangent = upstream.reshape(rows, seq, cols, channels)

    def shape(*dims):
        return jax.ShapeDtypeStruct(dims, BF16)

    one_ahead, few_ahead, all_far = orders(chips)

    def ordered(kernel, order):
        return functools.partial(kernel, order)

    block = (rows, cols, channels)
    whole = shape(rows, seq, cols, channels)
    by_row = shape(rows, block_len, channels)
    left = shape(*left_factor.shape)
    right = shape(*right_factor.shape)
    wide = pltpu.VMEM((channels // 128, count * cols, 128), F32)
    row_flops = 2 * rows * block_len * block_len * channels
    column_flops = 2 * cols * count * count * channels

    def pack(own, swapped):
        return list(call(pack_kernel, me, [own, swapped], [shape(2, *own.shape[1:])] * chips))

    hold = pltpu.VMEM(whole.shape, BF16)
    halves = [shape(chips, *block)] * 2
    last = one_ahead[-1]
    own, other = call(
        product_kernel,
        me,
        [gate, cotangent],
        halves,
        [hold, hold, pltpu.SemaphoreType.DMA((2, rows))],
        unblocked=range(2),
        vmem=60,
    )
    own_mixed, other_mixed = call(
        mix_kernel, me, [left_factor, after(values, own)], halves, [hold], row_flops
    )
    *messages, mixed_last = call(
        pack_pairs_kernel,
        me,
        [own, permute(other, 1), own_mixed, permute(other_mixed, 1)],
        [shape(2, 2, *block)] * last + [shape(2, *block)] * 2,
    )
    other_values = swap_sequences(after(values, messages[0]))
    columns = listed(exchange(messages), one_ahead)
    mixed_last = permute(after(mixed_last, columns[1:-2] + columns[-1:]), 2 * last)
    own, other, grad_column = call(
        ordered(column_backward_kernel, one_ahead),
        me,
        [right_factor, *columns],
        [shape(chips, *block)] * 2 + [shape(cols, count, channels)],
        [wide, wide],
        column_flops,
    )
    back = exchange(pack(own, permute(after(other, mixed_last), 1)))
    columns[-1] = mixed_last
    packed_right = shape(cols * count * count // channels, channels)
    own, other, right_part = call(
        ordered(column_forward_kernel, one_ahead),
        me,
        [right_factor, grad_column, other_values, *columns],
        [shape(chips, *block)] * 2 + [packed_right],
        [wide, wide],
        2 * column_flops,
        unblocked=[2],
    )
    back = listed(back, few_ahead)
    ahead = chips // 2
    messages = pack(own, permute(after(other, back[1:ahead]), 1))
    done = [(t, permute(messages[t], 2 * t)) for t in all_far[1:2]]
    back[-1] = after(back[-1], [block for _, block in done])
    extra = packed_right.size // math.prod(block)
    (first_part,) = call(
        gather_kernel, me, [*back[:ahead], right_part], [shape(2 * ahead + extra, *block)]
    )
    (second_part,) = call(
        gather_kernel, me, back[ahead:], [shape(2 * (chips - ahead), *block)]
    )
    other_first = swap_sequences(first_part)
    other_second = swap_sequences(second_part)
    grad_signal, left_term = call(
        ordered(row_backward_kernel, few_ahead),
        me,
        [left_factor, values, first_part, second_part],
        [by_row, left],
        [hold],
        2 * row_flops,
    )
    grad_left, grad_right = call(
        ordered(factor_sum_kernel, few_ahead),
        me,
        [left_term, other_values, other_first, other_second, right_part],
        [left, right],
        [hold],
        row_flops,
    )
    last = all_far[-1]
    messages[last] = after(messages[last], grad_left)
    second = listed(exchange(messages, done), all_far)
    output, grad_gate = call(
        ordered(output_kernel, all_far),
        me,
        [gate, cotangent, *second],
        [whole, whole],
        [hold, hold, pltpu.SemaphoreType.DMA((2, rows))],
        stored=False,
    )
    return (
        output.reshape(signal.shape),
        grad_gate.reshape(signal.shape),
        grad_signal.reshape(signal.shape),
        grad_left,
        grad_right,
    )


def plain_shards(signal, gating, upstream, left_factor, right_factor):
    seq = lax.axis_size("seq")
    rows, block_len = left_factor.shape[:2]
    cols, block_count = right_factor.shape[:2]
    channels = signal.shape[2]
    values = signal.reshape(rows, block_len, channels)
    gate = gating.reshape(rows, block_len, channels)
    cotangent = upstream.reshape(rows, block_len, channels)

    def einsum(spec, a, b):
        return jnp.einsum(spec, a, b, preferred_element_type=F32).astype(BF16)

    def all_to_all(blocks):
        return lax.all_to_all(blocks, "seq", split_axis=0, concat_axis=0, tiled=True)

    def to_columns(by_row):
        blocks = by_row.reshape(rows, seq, cols, channels).transpose(1, 0, 2, 3)
        return all_to_all(blocks).reshape(block_count, cols, channels)

    def to_rows(by_column):
        blocks = all_to_all(by_column.reshape(seq, rows, cols, channels))
        return blocks.transpose(1, 0, 2, 3).reshape(rows, block_len, channels)

    grad_rows = (cotangent.astype(F32) * gate.astype(F32)).astype(BF16)
    grad_column = to_columns(grad_rows)
    other_values = swap_sequences(values)
    mixed_column = to_columns(einsum("ikj,ijd->ikd", left_factor, values))
    grad_back = to_rows(einsum("kmi,mkd->ikd", right_factor, grad_column))
    second_rows = to_rows(einsum("kmi,ikd->mkd", right_factor, mixed_column))
    right_part = einsum("mkd,ikd->kmi", grad_column, mixed_column)
    other_right = swap_sequences(right_part)
    other_grad_back = swap_sequences(grad_back)
    grad_signal = einsum("ikj,ikd->ijd", left_factor, grad_back)
    left_term = einsum("ikd,ijd->ikj", grad_back, values)
    other_left = einsum("ikd,ijd->ikj", other_grad_back, other_values)
    grad_left = (left_term.astype(F32) + other_left.astype(F32)).astype(BF16)
    grad_right = (right_part.astype(F32) + other_right.astype(F32)).astype(BF16)
    wide = second_rows.astype(F32)
    output = (gate.astype(F32) * wide).astype(BF16)
    grad_gate = (cotangent.astype(F32) * wide).astype(BF16)
    return (
        output.reshape(signal.shape),
        grad_gate.reshape(signal.shape),
        grad_signal.reshape(signal.shape),
        grad_left,
        grad_right,
    )


def shards(signal, gating, upstream, left_factor, right_factor):
    seq = lax.axis_size("seq")
    cols = right_factor.shape[0]
    direct = seq in (8, 16) and cols % 32 == 0
    run = direct_shards if direct else plain_shards
    return run(signal, gating, upstream, left_factor, right_factor)


def solution(mesh):
    by_position = P("dp", "seq", None)
    by_block = P("seq", None, None)
    return jax.shard_map(
        shards,
        mesh=mesh,
        in_specs=(by_position,) * 3 + (by_block,) * 2,
        out_specs=(by_position,) * 3 + (by_block,) * 2,
        check_vma=False,
    )
```

```python
import functools
import math

import jax
import jax.numpy as jnp
from jax import lax
from jax.experimental import pallas as pl
from jax.experimental.pallas import tpu as pltpu
from jax.sharding import PartitionSpec as P

BF16 = jnp.bfloat16
F32 = jnp.float32
MIB = 1024 * 1024


def swap_sequences(array):
    return lax.ppermute(array, "dp", [(0, 1), (1, 0)])


def after(array, earlier):
    return lax.optimization_barrier((array, earlier))[0]


def orders(chips):
    half = chips // 2
    near = list(range(1, half))
    far = list(range(half, chips, 2)) + list(range(half + 1, chips, 2))
    mixed = far[:1] + near[:-1] + far[1:-1] + near[-1:] + far[-1:]
    return [0] + far[:1] + near + far[1:], [0] + mixed, [0] + far[:2] + far[:1:-1] + near


def permute(array, offset):
    seq = lax.axis_size("seq")
    return lax.ppermute(array, "seq", [(i, i ^ offset) for i in range(seq)])


def exchange(messages, done=()):
    done = dict(done)
    return [
        done[t] if t in done else permute(message, 2 * t) if t else message
        for t, message in enumerate(messages)
    ]


def listed(messages, order):
    return [messages[t] for t in order]


def call(kernel, me, inputs, out_shapes, scratch=(), flops=0, unblocked=(), vmem=32):
    whole = pl.BlockSpec(memory_space=pltpu.VMEM)
    moved = sum(x.size * x.dtype.itemsize for x in (*inputs, *out_shapes))
    in_specs = [
        pl.BlockSpec(memory_space=pl.ANY) if n in unblocked else whole for n in range(len(inputs))
    ]
    return pl.pallas_call(
        kernel,
        out_shape=out_shapes,
        in_specs=[pl.BlockSpec(memory_space=pltpu.SMEM)] + in_specs,
        out_specs=[whole] * len(out_shapes),
        scratch_shapes=scratch,
        compiler_params=pltpu.CompilerParams(vmem_limit_bytes=vmem * MIB),
        name=getattr(kernel, "func", kernel).__name__,
        cost_estimate=pl.CostEstimate(flops=flops, bytes_accessed=moved, transcendentals=0),
    )(me, *inputs)


def dot(a, b, contract):
    return lax.dot_general(a, b, (contract, ((), ())), preferred_element_type=F32)


def block_views(me, refs):
    return [(me ^ (2 * t + e), ref.at[t]) for e, ref in enumerate(refs) for t in range(ref.shape[0])]


def received_views(me, refs, order):
    return [(me ^ (2 * t + e), ref.at[e]) for t, ref in zip(order, refs) for e in range(2)]


def product_kernel(me_ref, gate_hbm, cotangent_hbm, *refs):
    out_refs, (gate, cotangent, sems) = refs[:2], refs[2:]
    rows = gate.shape[0]
    loads = [
        [
            pltpu.make_async_copy(source.at[i], target.at[i], sems.at[n, i])
            for n, (source, target) in enumerate(((gate_hbm, gate), (cotangent_hbm, cotangent)))
        ]
        for i in range(rows)
    ]
    for pair in loads:
        for load in pair:
            load.start()
    blocks = block_views(me_ref[0], out_refs)
    for i in range(rows):
        for load in loads[i]:
            load.wait()
        for c, ref in blocks:
            ref[i] = (gate[i, c].astype(F32) * cotangent[i, c].astype(F32)).astype(BF16)


def mix_kernel(me_ref, left_ref, values_ref, *refs):
    out_refs, hold = refs[:2], refs[2]
    rows, seq, cols, channels = hold.shape
    for i in range(rows):
        mixed = dot(left_ref[i], values_ref[i], ((1,), (0,)))
        hold[i] = mixed.astype(BF16).reshape(seq, cols, channels)
    for c, ref in block_views(me_ref[0], out_refs):
        ref[...] = hold[:, c]


def pack_kernel(me_ref, own_ref, other_ref, *out_refs):
    for t, out_ref in enumerate(out_refs):
        out_ref[0] = own_ref[t]
        out_ref[1] = other_ref[t]


def pack_pairs_kernel(me_ref, *refs):
    pairs, out_refs = (refs[0:2], refs[2:4]), refs[4:]
    last = len(out_refs) - 2
    for which, pair in enumerate(pairs):
        for e, ref in enumerate(pair):
            for t in range(last):
                out_refs[t][e, which] = ref[t]
            out_refs[last + which][e] = ref[last]


def of_pair(views, which):
    return [(c, ref.at[which] if len(ref.shape) == 4 else ref) for c, ref in views]


def load_columns(blocks, wide):
    rows, cols, channels = blocks[0][1].shape
    size = rows * cols
    for c, ref in blocks:
        block = ref[...].reshape(size, channels).astype(F32)
        start = pl.multiple_of(c * size, size)
        for h in range(channels // 128):
            wide[h, pl.ds(start, size), :] = block[:, h * 128 : (h + 1) * 128]


def column(wide, k, count, cols):
    halves = [wide[h, pl.ds(k, count, stride=cols), :] for h in range(wide.shape[0])]
    return jnp.concatenate(halves, axis=1).astype(BF16)


def store_column(wide, k, count, cols, value):
    for h in range(wide.shape[0]):
        wide[h, pl.ds(k, count, stride=cols), :] = value[:, h * 128 : (h + 1) * 128]


def send_columns(wide, blocks):
    rows, cols, channels = blocks[0][1].shape
    size = rows * cols
    for c, ref in blocks:
        start = pl.multiple_of(c * size, size)
        halves = [wide[h, pl.ds(start, size), :] for h in range(wide.shape[0])]
        block = jnp.concatenate(halves, axis=1).astype(BF16)
        ref[...] = block.reshape(rows, cols, channels)


def column_backward_kernel(order, me_ref, right_ref, *refs):
    chips = len(order)
    in_refs, out_refs = refs[:chips], refs[chips : chips + 2]
    by_column_ref, wide, wide_out = refs[chips + 2 :]
    cols, count, _ = right_ref.shape
    me = me_ref[0]
    load_columns(of_pair(received_views(me, in_refs, order), 0), wide)
    for k in range(cols):
        grad = column(wide, k, count, cols)
        by_column_ref[k] = grad
        store_column(wide_out, k, count, cols, dot(right_ref[k], grad, ((0,), (0,))))
    send_columns(wide_out, block_views(me, out_refs))


def column_forward_kernel(order, me_ref, right_ref, grad_ref, after_ref, *refs):
    chips = len(order)
    in_refs, out_refs = refs[:chips], refs[chips : chips + 2]
    packed_ref, wide, wide_out = refs[chips + 2 :]
    cols, count, _ = right_ref.shape
    channels = packed_ref.shape[1]
    terms = []
    me = me_ref[0]
    load_columns(of_pair(received_views(me, in_refs, order), 1), wide)
    for k in range(cols):
        mixed = column(wide, k, count, cols)
        store_column(wide_out, k, count, cols, dot(right_ref[k], mixed, ((1,), (0,))))
        terms.append(dot(grad_ref[k], mixed, ((1,), (1,))))
        if len(terms) == channels // count:
            row = k * count // channels * count
            packed_ref[row : row + count] = jnp.concatenate(terms, axis=1).astype(BF16)
            terms = []
    send_columns(wide_out, block_views(me, out_refs))


def gather_kernel(me_ref, *refs):
    out_ref, n = refs[-1], 0
    _, rows, cols, channels = out_ref.shape
    size = rows * cols
    for ref in refs[:-1]:
        if ref.ndim == 2:
            for start in range(0, ref.shape[0], size):
                out_ref[n] = ref[start : start + size].reshape(rows, cols, channels)
                n += 1
            continue
        for e in range(ref.shape[0]):
            out_ref[n] = ref[e]
            n += 1


def load_rows(order, me, parts, hold):
    left = 2 * len(order) - parts[1].shape[0]
    for n, t in enumerate(order):
        for e in range(2):
            j = 2 * n + e
            hold[:, me ^ (2 * t + e)] = parts[0][j] if j < left else parts[1][j - left]


def row_of(hold, i):
    seq, cols, channels = hold.shape[1:]
    return hold[i].reshape(seq * cols, channels)


def row_backward_kernel(
    order, me_ref, left_ref, values_ref, first_ref, second_ref, signal_ref, term_ref, hold
):
    load_rows(order, me_ref[0], (first_ref, second_ref), hold)
    for i in range(left_ref.shape[0]):
        grad = row_of(hold, i)
        signal_ref[i] = dot(left_ref[i], grad, ((0,), (0,))).astype(BF16)
        term_ref[i] = dot(grad, values_ref[i], ((1,), (1,))).astype(BF16)


def factor_sum_kernel(
    order,
    me_ref,
    term_ref,
    values_ref,
    first_ref,
    second_ref,
    packed_ref,
    left_out_ref,
    right_out_ref,
    hold,
):
    load_rows(order, me_ref[0], (first_ref, second_ref), hold)
    for i in range(term_ref.shape[0]):
        other = dot(row_of(hold, i), values_ref[i], ((1,), (1,))).astype(BF16)
        left_out_ref[i] = (term_ref[i].astype(F32) + other.astype(F32)).astype(BF16)
    cols, count, _ = right_out_ref.shape
    height, channels = packed_ref.shape
    blocks = 2 * len(order) - second_ref.shape[0]
    size = height // (first_ref.shape[0] - blocks)
    share = channels // count
    for n in range(height // count):
        block, row = blocks + n * count // size, n * count % size
        other = first_ref[block].reshape(size, channels)[row : row + count]
        total = packed_ref[n * count : (n + 1) * count].astype(F32) + other.astype(F32)
        for q in range(share):
            right_out_ref[n * share + q] = total[:, q * count : (q + 1) * count].astype(BF16)


def output_kernel(order, me_ref, gate_ref, cotangent_ref, *refs):
    chips = len(order)
    out_ref, grad_ref = refs[chips:]
    for c, ref in received_views(me_ref[0], refs[:chips], order):
        second = ref[...].astype(F32)
        out_ref[:, c] = (gate_ref[:, c].astype(F32) * second).astype(BF16)
        grad_ref[:, c] = (cotangent_ref[:, c].astype(F32) * second).astype(BF16)


def direct_shards(signal, gating, upstream, left_factor, right_factor):
    seq = lax.axis_size("seq")
    chips = seq // 2
    rows, block_len = left_factor.shape[:2]
    cols, count = right_factor.shape[:2]
    channels = signal.shape[2]
    me = lax.axis_index("seq").astype(jnp.int32).reshape(1)
    values = signal.reshape(rows, block_len, channels)
    gate = gating.reshape(rows, seq, cols, channels)
    cotangent = upstream.reshape(rows, seq, cols, channels)

    def shape(*dims):
        return jax.ShapeDtypeStruct(dims, BF16)

    one_ahead, few_ahead, all_far = orders(chips)

    def ordered(kernel, order):
        return functools.partial(kernel, order)

    block = (rows, cols, channels)
    whole = shape(rows, seq, cols, channels)
    by_row = shape(rows, block_len, channels)
    left = shape(*left_factor.shape)
    right = shape(*right_factor.shape)
    wide = pltpu.VMEM((channels // 128, count * cols, 128), F32)
    row_flops = 2 * rows * block_len * block_len * channels
    column_flops = 2 * cols * count * count * channels

    def pack(own, swapped):
        return list(call(pack_kernel, me, [own, swapped], [shape(2, *own.shape[1:])] * chips))

    hold = pltpu.VMEM(whole.shape, BF16)
    halves = [shape(chips, *block)] * 2
    last = one_ahead[-1]
    own, other = call(
        product_kernel,
        me,
        [gate, cotangent],
        halves,
        [hold, hold, pltpu.SemaphoreType.DMA((2, rows))],
        unblocked=range(2),
        vmem=60,
    )
    own_mixed, other_mixed = call(
        mix_kernel, me, [left_factor, after(values, own)], halves, [hold], row_flops
    )
    *messages, mixed_last = call(
        pack_pairs_kernel,
        me,
        [own, permute(other, 1), own_mixed, permute(other_mixed, 1)],
        [shape(2, 2, *block)] * last + [shape(2, *block)] * 2,
    )
    other_values = swap_sequences(after(values, messages[0]))
    columns = listed(exchange(messages), one_ahead)
    mixed_last = permute(after(mixed_last, columns[1:-2] + columns[-1:]), 2 * last)
    own, other, grad_column = call(
        ordered(column_backward_kernel, one_ahead),
        me,
        [right_factor, *columns],
        [shape(chips, *block)] * 2 + [shape(cols, count, channels)],
        [wide, wide],
        column_flops,
    )
    back = exchange(pack(own, permute(after(other, mixed_last), 1)))
    columns[-1] = mixed_last
    packed_right = shape(cols * count * count // channels, channels)
    own, other, right_part = call(
        ordered(column_forward_kernel, one_ahead),
        me,
        [right_factor, grad_column, other_values, *columns],
        [shape(chips, *block)] * 2 + [packed_right],
        [wide, wide],
        2 * column_flops,
        unblocked=[2],
    )
    back = listed(back, few_ahead)
    ahead = chips // 2
    messages = pack(own, permute(after(other, back[1:ahead]), 1))
    done = [(t, permute(messages[t], 2 * t)) for t in all_far[1:2]]
    back[-1] = after(back[-1], [block for _, block in done])
    extra = packed_right.size // math.prod(block)
    (first_part,) = call(
        gather_kernel, me, [*back[:ahead], right_part], [shape(2 * ahead + extra, *block)]
    )
    (second_part,) = call(
        gather_kernel, me, back[ahead:], [shape(2 * (chips - ahead), *block)]
    )
    other_first = swap_sequences(first_part)
    other_second = swap_sequences(second_part)
    grad_signal, left_term = call(
        ordered(row_backward_kernel, few_ahead),
        me,
        [left_factor, values, first_part, second_part],
        [by_row, left],
        [hold],
        2 * row_flops,
    )
    grad_left, grad_right = call(
        ordered(factor_sum_kernel, few_ahead),
        me,
        [left_term, other_values, other_first, other_second, right_part],
        [left, right],
        [hold],
        row_flops,
    )
    last = all_far[-1]
    messages[last] = after(messages[last], grad_left)
    second = listed(exchange(messages, done), all_far)
    output, grad_gate = call(
        ordered(output_kernel, all_far), me, [gate, cotangent, *second], [whole, whole]
    )
    return (
        output.reshape(signal.shape),
        grad_gate.reshape(signal.shape),
        grad_signal.reshape(signal.shape),
        grad_left,
        grad_right,
    )


def plain_shards(signal, gating, upstream, left_factor, right_factor):
    seq = lax.axis_size("seq")
    rows, block_len = left_factor.shape[:2]
    cols, block_count = right_factor.shape[:2]
    channels = signal.shape[2]
    values = signal.reshape(rows, block_len, channels)
    gate = gating.reshape(rows, block_len, channels)
    cotangent = upstream.reshape(rows, block_len, channels)

    def einsum(spec, a, b):
        return jnp.einsum(spec, a, b, preferred_element_type=F32).astype(BF16)

    def all_to_all(blocks):
        return lax.all_to_all(blocks, "seq", split_axis=0, concat_axis=0, tiled=True)

    def to_columns(by_row):
        blocks = by_row.reshape(rows, seq, cols, channels).transpose(1, 0, 2, 3)
        return all_to_all(blocks).reshape(block_count, cols, channels)

    def to_rows(by_column):
        blocks = all_to_all(by_column.reshape(seq, rows, cols, channels))
        return blocks.transpose(1, 0, 2, 3).reshape(rows, block_len, channels)

    grad_rows = (cotangent.astype(F32) * gate.astype(F32)).astype(BF16)
    grad_column = to_columns(grad_rows)
    other_values = swap_sequences(values)
    mixed_column = to_columns(einsum("ikj,ijd->ikd", left_factor, values))
    grad_back = to_rows(einsum("kmi,mkd->ikd", right_factor, grad_column))
    second_rows = to_rows(einsum("kmi,ikd->mkd", right_factor, mixed_column))
    right_part = einsum("mkd,ikd->kmi", grad_column, mixed_column)
    other_right = swap_sequences(right_part)
    other_grad_back = swap_sequences(grad_back)
    grad_signal = einsum("ikj,ikd->ijd", left_factor, grad_back)
    left_term = einsum("ikd,ijd->ikj", grad_back, values)
    other_left = einsum("ikd,ijd->ikj", other_grad_back, other_values)
    grad_left = (left_term.astype(F32) + other_left.astype(F32)).astype(BF16)
    grad_right = (right_part.astype(F32) + other_right.astype(F32)).astype(BF16)
    wide = second_rows.astype(F32)
    output = (gate.astype(F32) * wide).astype(BF16)
    grad_gate = (cotangent.astype(F32) * wide).astype(BF16)
    return (
        output.reshape(signal.shape),
        grad_gate.reshape(signal.shape),
        grad_signal.reshape(signal.shape),
        grad_left,
        grad_right,
    )


def shards(signal, gating, upstream, left_factor, right_factor):
    seq = lax.axis_size("seq")
    cols = right_factor.shape[0]
    direct = seq in (8, 16) and cols % 32 == 0
    run = direct_shards if direct else plain_shards
    return run(signal, gating, upstream, left_factor, right_factor)


def solution(mesh):
    by_position = P("dp", "seq", None)
    by_block = P("seq", None, None)
    return jax.shard_map(
        shards,
        mesh=mesh,
        in_specs=(by_position,) * 3 + (by_block,) * 2,
        out_specs=(by_position,) * 3 + (by_block,) * 2,
        check_vma=False,
    )
```
